32 devices in a mesh: fsdp: 16 (over z, x, core), tp: 2 (over y).
Axes of the slice: x: 2, y: 2, z: 4, core: 2. Of those that a mesh axis runs over, the one named last changes fastest.
Arguments:
- latents_in: float32 [1024, 16, 1024], P('tp', 'fsdp'), may hold values from -6 to 6
- condition: float32 [16, 1024], P('fsdp'), may hold values from -6 to 6
- out_grad: float32 [1024, 16, 1024], P('tp', 'fsdp'), may hold values from -6 to 6
- condition_weight: float32 [1024, 6, 1024], P('fsdp', None, 'tp'), may hold values from -0.1875 to 0.1875
- condition_first: float32 [1024, 6, 1024], P('fsdp', None, 'tp'), may hold values from -80 to 80
- condition_second: float32 [1024, 6, 1024], P('fsdp', None, 'tp'), may hold values from 8.192 to 131.072
- heads_weight: float32 [3, 1024, 1024], P(None, 'fsdp', 'tp'), may hold values from -0.1875 to 0.1875
- heads_first: float32 [3, 1024, 1024], P(None, 'fsdp', 'tp'), may hold values from -80 to 80
- heads_second: float32 [3, 1024, 1024], P(None, 'fsdp', 'tp'), may hold values from 8.192 to 131.072
- merge_weight: float32 [1024, 1024], P('tp', 'fsdp'), may hold values from -1.5 to 1.5
- merge_first: float32 [1024, 1024], P('tp', 'fsdp'), may hold values from -8 to 8
- merge_second: float32 [1024, 1024], P('tp', 'fsdp'), may hold values from 0.08192 to 1.31072
- up_weight: float32 [1024, 4096], P('fsdp', 'tp'), may hold values from -0.1875 to 0.1875
- up_first: float32 [1024, 4096], P('fsdp', 'tp'), may hold values from -20 to 20
- up_second: float32 [1024, 4096], P('fsdp', 'tp'), may hold values from 0.49152 to 8.192
- down_weight: float32 [4096, 1024], P('tp', 'fsdp'), may hold values from -0.09375 to 0.09375
- down_first: float32 [4096, 1024], P('tp', 'fsdp'), may hold values from -32 to 32
- down_second: float32 [4096, 1024], P('tp', 'fsdp'), may hold values from 0.98304 to 16.384
Outputs:
- block_out: float32 [1024, 16, 1024], P('tp', 'fsdp')
- latents_grad: float32 [1024, 16, 1024], P('tp', 'fsdp')
- condition_weight_new: float32 [1024, 6, 1024], P('fsdp', None, 'tp')
- condition_first_new: float32 [1024, 6, 1024], P('fsdp', None, 'tp')
- condition_second_new: float32 [1024, 6, 1024], P('fsdp', None, 'tp')
- heads_weight_new: float32 [3, 1024, 1024], P(None, 'fsdp', 'tp')
- heads_first_new: float32 [3, 1024, 1024], P(None, 'fsdp', 'tp')
- heads_second_new: float32 [3, 1024, 1024], P(None, 'fsdp', 'tp')
- merge_weight_new: float32 [1024, 1024], P('tp', 'fsdp')
- merge_first_new: float32 [1024, 1024], P('tp', 'fsdp')
- merge_second_new: float32 [1024, 1024], P('tp', 'fsdp')
- up_weight_new: float32 [1024, 4096], P('fsdp', 'tp')
- up_first_new: float32 [1024, 4096], P('fsdp', 'tp')
- up_second_new: float32 [1024, 4096], P('fsdp', 'tp')
- down_weight_new: float32 [4096, 1024], P('tp', 'fsdp')
- down_first_new: float32 [4096, 1024], P('tp', 'fsdp')
- down_second_new: float32 [4096, 1024], P('tp', 'fsdp')
The draws below stay inside these ranges and needn't reach their ends.
All inputs are finite; a program needn't handle non-finite values.
Results may differ from the reference program's by a relative error of at most 0.025.
Values may be sent and summed in bfloat16 or wider, within the bound.
No kernel may reach another device: no remote copies, remote signals or barrier semaphores. Data moves between devices by JAX's collectives and lax.ppermute only.
A program may use at most 192 MiB of HBM per device.

```python
import math
import jax
import jax.numpy as jnp
from jax import lax

D = 1024
HEADS = 16
HEAD = 64
FF = 4096
SEQ = 1024
STEP = 5
LAT = 16


def strengthened(entries, own_key, source, target, blocks, factor):
    def block_of(position):
        return (jnp.arange(entries.shape[position]) // (entries.shape[position] // blocks)).reshape((-1,) + (1,) * (entries.ndim - 1 - position))

    one_side = jax.random.permutation(own_key, blocks)[block_of(target)]
    far = (block_of(target) + blocks // 2) % blocks
    return jnp.where((block_of(source) == one_side) | (block_of(source) == far), factor * entries, entries)


def steps_of(key, extent, split, low, top_value):
    loudness = 1.0
    for dim, shards_of in split:
        draws = jax.random.uniform(jax.random.fold_in(jax.random.fold_in(key, 6), dim), (shards_of,), jnp.float32, low / len(split), top_value / len(split))
        loudness = loudness * jnp.repeat(jnp.exp(draws), extent[dim] // shards_of).reshape((-1,) + (1,) * (len(extent) - 1 - dim))
    return loudness


def noise(key, dims, scale, reach, split=(), dtype=jnp.bfloat16):
    level = steps_of(key, dims, split, -0.22, 0.18) if split else 1.0
    values = jax.random.normal(key, dims, jnp.float32) * scale * level
    return jnp.minimum(jnp.maximum(values, -reach), reach).astype(dtype)


def heavy_noise(rng, dims, scale, limit, pieces, heavy, kind=jnp.bfloat16):
    result = scale * jax.random.normal(rng, dims, jnp.float32)
    if pieces:
        result = result * steps_of(rng, dims, pieces, -0.22, 0.18)
    return jnp.clip(strengthened(result, jax.random.fold_in(rng, 3), *heavy), -limit, limit).astype(kind)


def setup_inputs(seed: int = 0) -> dict:
    arg_keys = jax.random.split(jax.random.key(seed), 19)
    return {
        "latents_in": noise(arg_keys[0], (SEQ, LAT, D), 1.0, 6.0, ((0, 2), (1, 16)), jnp.float32),
        "condition": noise(arg_keys[1], (LAT, D), 1.0, 6.0, ((0, 16),), jnp.float32),
        "out_grad": heavy_noise(arg_keys[2], (SEQ, LAT, D), 1.0, 6.0, ((0, 2), (1, 16)), (1, 2, 16, 2.0), jnp.float32),
        "condition_weight": noise(arg_keys[3], (D, 6, D), D ** -0.5, 0.1875, ((0, 16), (2, 2)), jnp.float32),
        "condition_first": noise(arg_keys[4], (D, 6, D), (0.111 * (SEQ * LAT) ** 0.5), 80.0, ((0, 16), (2, 2)), jnp.float32),
        "condition_second": jnp.clip(jnp.exp(math.log(131.072) - 2.7725887 * jax.random.uniform(arg_keys[5], (D, 6, D), jnp.float32) ** steps_of(arg_keys[5], (D, 6, D), ((0, 16), (2, 2)), -0.2, 0.2)), 8.192, 131.072),
        "heads_weight": noise(arg_keys[6], (3, D, D), D ** -0.5, 0.1875, ((1, 16), (2, 2)), jnp.float32),
        "heads_first": noise(arg_keys[7], (3, D, D), (0.111 * (SEQ * LAT) ** 0.5), 80.0, ((1, 16), (2, 2)), jnp.float32),
        "heads_second": jnp.clip(jnp.exp(math.log(131.072) - 2.7725887 * jax.random.uniform(arg_keys[8], (3, D, D), jnp.float32) ** steps_of(arg_keys[8], (3, D, D), ((1, 16), (2, 2)), -0.2, 0.2)), 8.192, 131.072),
        "merge_weight": noise(arg_keys[9], (D, D), (D * 16 // SEQ) ** -0.5, 1.5, ((0, 2), (1, 16)), jnp.float32),
        "merge_first": noise(arg_keys[10], (D, D), (0.0111 * (SEQ * LAT) ** 0.5), 8.0, ((0, 2), (1, 16)), jnp.float32),
        "merge_second": jnp.clip(jnp.exp(math.log(1.31072) - 2.7725887 * jax.random.uniform(arg_keys[11], (D, D), jnp.float32) ** steps_of(arg_keys[11], (D, D), ((0, 2), (1, 16)), -0.2, 0.2)), 0.08192, 1.31072),
        "up_weight": noise(arg_keys[12], (D, FF), D ** -0.5, 0.1875, ((0, 16), (1, 2)), jnp.float32),
        "up_first": noise(arg_keys[13], (D, FF), (0.028 * (SEQ * LAT) ** 0.5), 20.0, ((0, 16), (1, 2)), jnp.float32),
        "up_second": jnp.clip(jnp.exp(math.log(8.192) - 2.8134108 * jax.random.uniform(arg_keys[14], (D, FF), jnp.float32) ** steps_of(arg_keys[14], (D, FF), ((0, 16), (1, 2)), -0.2, 0.2)), 0.49152, 8.192),
        "down_weight": noise(arg_keys[15], (FF, D), FF ** -0.5, 0.09375, ((0, 2), (1, 16)), jnp.float32),
        "down_first": noise(arg_keys[16], (FF, D), (0.039 * (SEQ * LAT) ** 0.5), 32.0, ((0, 2), (1, 16)), jnp.float32),
        "down_second": jnp.clip(jnp.exp(math.log(16.384) - 2.8134108 * jax.random.uniform(arg_keys[17], (FF, D), jnp.float32) ** steps_of(arg_keys[17], (FF, D), ((0, 2), (1, 16)), -0.2, 0.2)), 0.98304, 16.384),
    }


@jax.custom_vjp
def low(v):
    return lax.optimization_barrier(v.astype(jnp.bfloat16)).astype(jnp.float32)

@jax.custom_vjp
def low_back(v):
    return v

def low_keep(v):
    return (low(v), None)

def low_pass(kept, grad):
    return (grad,)

def back_keep(v):
    return (v, None)

def back_low(kept, grad):
    return (low(grad),)
low.defvjp(low_keep, low_pass)
low_back.defvjp(back_keep, back_low)
highest = lax.Precision.HIGHEST

def modulate(values, shift_term, scale_term):
    middle = lax.optimization_barrier(jnp.mean(values, axis=-1, keepdims=True))
    centred = values - middle
    spread = lax.optimization_barrier(jnp.mean(centred * centred, axis=-1, keepdims=True))
    return centred * lax.rsqrt(spread + 1e-06) * (1.0 + scale_term) + shift_term

def gelu_tanh(values):
    return jax.nn.gelu(values, approximate=True)

def block(latent, cond_vec, cond_mat, heads_mat, merge_mat, up_mat, down_mat):
    activated = low(jax.nn.silu(cond_vec))
    modulation = jnp.einsum('d,dkc->kc', activated, low(cond_mat), precision=highest)
    normed_one = low(modulate(latent, modulation[0], modulation[1]))
    triple = jnp.einsum('sd,tdc->tsc', normed_one, low(heads_mat), precision=highest)
    triple = low_back(low(triple)).reshape(3, SEQ, HEADS, HEAD)
    scores = jnp.einsum('qhe,khe->hqk', triple[0], triple[1], precision=highest) * HEAD ** (-0.5)
    scores = low_back(scores)
    raised = jnp.exp(scores - lax.optimization_barrier(jnp.max(scores, axis=-1, keepdims=True)))
    probs = raised / lax.optimization_barrier(jnp.sum(raised, axis=-1, keepdims=True))
    attended = jnp.einsum('hqk,khe->qhe', low(probs), triple[2], precision=highest)
    attended = low_back(low(attended)).reshape(SEQ, D)
    attn_branch = low_back(jnp.dot(attended, low(merge_mat), precision=highest))
    after_attn = latent + modulation[2] * attn_branch
    normed_two = low(modulate(after_attn, modulation[3], modulation[4]))
    hidden_pre = low_back(jnp.dot(normed_two, low(up_mat), precision=highest))
    hidden = low(gelu_tanh(hidden_pre))
    mlp_branch = low_back(jnp.dot(hidden, low(down_mat), precision=highest))
    return after_attn + modulation[5] * mlp_branch

def adam_step(weight, first, second, grad_sum, rate):
    first_new = 0.9 * first + 0.1 * grad_sum
    second_new = 0.999 * second + 0.001 * grad_sum * grad_sum
    first_hat = first_new / (1.0 - 0.9 ** STEP)
    second_hat = second_new / (1.0 - 0.999 ** STEP)
    weight_new = weight - rate * (first_hat / (jnp.sqrt(second_hat) + 1e-08) + 0.01 * weight)
    return (weight_new, first_new, second_new)

def reference(latents_in, condition, out_grad, condition_weight, condition_first, condition_second, heads_weight, heads_first, heads_second, merge_weight, merge_first, merge_second, up_weight, up_first, up_second, down_weight, down_first, down_second):
    weights = (condition_weight, heads_weight, merge_weight, up_weight, down_weight)

    def per_latent(totals, parts):
        latent, cond_vec, grad_rows = parts

        def local_block(lat, cond_mat, heads_mat, merge_mat, up_mat, down_mat):
            return block(lat, cond_vec, cond_mat, heads_mat, merge_mat, up_mat, down_mat)
        outputs, backward = jax.vjp(local_block, latent, weights[0], weights[1], weights[2], weights[3], weights[4])
        grads = backward(grad_rows)
        new_totals = tuple((total + grad_part for total, grad_part in zip(totals, grads[1:])))
        return (new_totals, (outputs, grads[0]))
    start = tuple((jnp.zeros(weight.shape, jnp.float32) for weight in weights))
    sums, (outputs, input_grads) = lax.scan(per_latent, start, (jnp.moveaxis(latents_in, 1, 0), condition, jnp.moveaxis(out_grad, 1, 0)))
    block_out = jnp.moveaxis(outputs, 0, 1)
    latents_grad = jnp.moveaxis(input_grads, 0, 1)
    cond_new = adam_step(condition_weight, condition_first, condition_second, sums[0], 0.02)
    heads_new = adam_step(heads_weight, heads_first, heads_second, sums[1], 0.02)
    merge_new = adam_step(merge_weight, merge_first, merge_second, sums[2], 0.15)
    up_new = adam_step(up_weight, up_first, up_second, sums[3], 0.02)
    down_new = adam_step(down_weight, down_first, down_second, sums[4], 0.01)
    return (block_out, latents_grad, cond_new[0], cond_new[1], cond_new[2], heads_new[0], heads_new[1], heads_new[2], merge_new[0], merge_new[1], merge_new[2], up_new[0], up_new[1], up_new[2], down_new[0], down_new[1], down_new[2])
```

```python
import functools

import jax
import jax.numpy as jnp
from jax import lax
from jax.experimental import pallas as pl
from jax.experimental.pallas import tpu as pltpu
from jax.sharding import PartitionSpec as P

HEAD = 64
PAIR = 2 * HEAD
STEP = 5
LOW = jnp.bfloat16
FULL = jnp.float32
NT = (((1,), (1,)), ((), ()))
TN = (((0,), (0,)), ((), ()))


def params(limit=56):
    return pltpu.CompilerParams(vmem_limit_bytes=limit * 1024 * 1024)


def cost(flops, moved, raised=0):
    return pl.CostEstimate(flops=int(flops), bytes_accessed=int(moved), transcendentals=int(raised))


def resident(shape):
    return pl.BlockSpec(shape, lambda *step: (0,) * len(shape))


def fit(width, most):
    return next(tile for tile in (most, 512, 256, PAIR) if tile <= most and width % tile == 0)


def product(left, right, out_type, start=0, width=None):
    rows, depth = left.shape
    width = width or right.shape[1]
    tile = fit(width, 512)
    first = start // tile

    def body(left_ref, right_ref, out_ref):
        out_ref[...] = jnp.dot(
            left_ref[...], right_ref[...], preferred_element_type=FULL
        ).astype(out_type)

    return pl.pallas_call(
        body,
        grid=(width // tile,),
        in_specs=[
            resident((rows, depth)),
            pl.BlockSpec((depth, tile), lambda j: (0, first + j)),
        ],
        out_specs=pl.BlockSpec((rows, tile), lambda j: (0, j)),
        out_shape=jax.ShapeDtypeStruct((rows, width), out_type),
        compiler_params=params(),
        cost_estimate=cost(2 * rows * depth * width, 2 * (rows * depth + depth * width) + 4 * rows * width),
        name="product",
    )(left, right)


def product_back(lefts, right, out_type):
    rows = lefts[0].shape[0]
    width, depth = right.shape
    tile = min(256, width)

    def body(*refs):
        total = None
        start = 0
        for left_ref in refs[:-2]:
            extent = left_ref.shape[1]
            term = lax.dot_general(
                left_ref[...], refs[-2][:, start : start + extent], NT, preferred_element_type=FULL
            )
            total = term if total is None else total + term
            start += extent
        refs[-1][...] = total.astype(out_type)

    return pl.pallas_call(
        body,
        grid=(width // tile,),
        in_specs=[resident(left.shape) for left in lefts]
        + [pl.BlockSpec((tile, depth), lambda j: (j, 0))],
        out_specs=pl.BlockSpec((rows, tile), lambda j: (0, j)),
        out_shape=jax.ShapeDtypeStruct((rows, width), out_type),
        compiler_params=params(),
        cost_estimate=cost(2 * rows * depth * width, 2 * (rows * depth + width * depth) + 4 * rows * width),
        name="product_back",
    )(*lefts, right)


def token_sum(jobs, count, ordered=True):
    depth = jobs[0][0][0].shape[1]
    widths = [rights[0].shape[1] for _, rights in jobs]
    width = sum(widths)
    tokens = max(sum(left.shape[0] for left in lefts) for lefts, _ in jobs)
    tile = min(fit(extent, 512) for extent in widths)
    deep, across, cores = digits(count)
    group = depth // count
    pieces = len(jobs[0][0])
    starts = [sum(widths[:index]) // tile for index in range(len(jobs) + 1)]

    def flip(left_refs, turned):
        me = lax.axis_index("fsdp")
        my_z, my_x, my_c = me // (across * cores), (me // cores) % across, me % cores
        start = 0
        for left_ref in left_refs:
            flipped = left_ref[...].T
            extent = left_ref.shape[0]
            if not ordered:
                turned[:, start : start + extent] = flipped
            for source in range(count if ordered else 0):
                z, x, c = source // (across * cores), (source // cores) % across, source % cores
                place = (
                    ((c - my_c + cores) % cores) * across + (x - my_x + across) % across
                ) * deep + (z - my_z + deep) % deep
                turned[pl.ds(pl.multiple_of(place * group, group), group), start : start + extent] = (
                    flipped[source * group : (source + 1) * group]
                )
            start += extent

    def body(*refs):
        out_refs, turned = refs[2 * pieces * len(jobs) : -1], refs[-1]
        step = pl.program_id(0)
        for index in range(len(jobs)):
            mine = refs[2 * pieces * index : 2 * pieces * (index + 1)]

            @pl.when(step == starts[index])
            def _():
                flip(mine[:pieces], turned)

            @pl.when((step >= starts[index]) & (step < starts[index + 1]))
            def _():
                total = None
                start = 0
                for right_ref in mine[pieces:]:
                    extent = right_ref.shape[0]
                    term = jnp.dot(
                        turned[:, start : start + extent], right_ref[...], preferred_element_type=FULL
                    )
                    total = term if total is None else total + term
                    start += extent
                total = total.astype(LOW)
                start = 0
                for out_ref in out_refs:
                    out_ref[...] = total[start : start + out_ref.shape[0]]
                    start += out_ref.shape[0]

    def place_of(index):
        last = widths[index] // tile - 1
        return lambda j: (0, jnp.clip(j - starts[index], 0, last))

    half = depth // cores
    heights = (half, depth - half) if ordered else (depth,)
    in_specs = []
    operands = []
    for index, (lefts, rights) in enumerate(jobs):
        in_specs += [resident(left.shape) for left in lefts]
        in_specs += [pl.BlockSpec((right.shape[0], tile), place_of(index)) for right in rights]
        operands += [*lefts, *rights]
    return pl.pallas_call(
        body,
        grid=(width // tile,),
        in_specs=in_specs,
        out_specs=[pl.BlockSpec((height, tile), lambda j: (0, j)) for height in heights],
        out_shape=[jax.ShapeDtypeStruct((height, width), LOW) for height in heights],
        scratch_shapes=[pltpu.VMEM((depth, tokens), LOW)],
        compiler_params=params(),
        cost_estimate=cost(
            2 * depth * tokens * width, 2 * (len(jobs) * depth * tokens + tokens * width + depth * width)
        ),
        name="token_sum",
    )(*operands)


def head_lanes():
    lane = lax.broadcasted_iota(jnp.int32, (1, PAIR), 1)
    first = (lane < HEAD).astype(FULL)
    return lane, ((first, HEAD), (1.0 - first, 0))


def in_lanes(lane, free, column):
    total = 0.0
    for index in range(3):
        piece = column.astype(LOW).astype(FULL)
        total = total + jnp.where(lane == free + index, piece, 0.0)
        column = column - piece
    return total


def ones_in_lanes(lane, free, values):
    return jnp.where((lane >= free) & (lane < free + 3), 1.0, values.astype(FULL)).astype(LOW)


def attend_forward(triple, width):
    tokens = triple.shape[0]
    pairs = width // PAIR
    block = min(512, tokens)
    scaling = HEAD ** (-0.5)

    def body(query_ref, keys_ref, values_ref, out_ref, level_ref):
        lane, heads = head_lanes()
        keys = keys_ref[...]
        values = values_ref[...].astype(FULL)
        query = query_ref[...].astype(FULL)
        total = level = 0.0
        for mask, free in heads:
            scores = lax.dot_general(
                (query * (mask * scaling)).astype(LOW), keys, NT, preferred_element_type=FULL
            )
            peak = jnp.max(scores, axis=-1, keepdims=True)
            raised = jnp.exp(scores - peak).astype(LOW)
            counted = jnp.where(lane == free, 1.0, values * mask).astype(LOW)
            mixed = jnp.dot(raised, counted, preferred_element_type=FULL)
            sums = mixed[:, free : free + 1]
            total = total + mixed * mask / sums
            level = level + mask * (peak + jnp.log(sums))
        out_ref[...] = total.astype(LOW)
        level_ref[...] = level

    return pl.pallas_call(
        body,
        grid=(pairs, tokens // block),
        in_specs=[
            pl.BlockSpec((block, PAIR), lambda h, i: (i, h)),
            pl.BlockSpec((tokens, PAIR), lambda h, i: (0, pairs + h)),
            pl.BlockSpec((tokens, PAIR), lambda h, i: (0, 2 * pairs + h)),
        ],
        out_specs=[pl.BlockSpec((block, PAIR), lambda h, i: (i, h))] * 2,
        out_shape=[
            jax.ShapeDtypeStruct((tokens, width), LOW),
            jax.ShapeDtypeStruct((tokens, width), FULL),
        ],
        compiler_params=params(),
        cost_estimate=cost(16 * tokens * tokens * width, 12 * tokens * width, tokens * tokens * width // HEAD),
        name="attend_forward",
    )(triple, triple, triple)


def attend_backward(triple, attended, level, grads, width):
    tokens = triple.shape[0]
    pairs = width // PAIR
    block = min(512, tokens)
    steps = tokens // block
    scaling = HEAD ** (-0.5)

    def body(query_ref, keys_ref, values_ref, out_low_ref, level_ref, grad_ref, out_ref, key_sum, value_sum):
        pair = pl.program_id(0)
        step = pl.program_id(1)
        lane, heads = head_lanes()
        keys = keys_ref[...]
        values = values_ref[...]
        query = query_ref[...].astype(FULL)
        grad = grad_ref[...].astype(FULL)
        inner = grad * out_low_ref[...].astype(FULL)
        query_grad = key_grad = value_grad = None
        for index, (mask, free) in enumerate(heads):
            own = HEAD * index
            query_part = query * (mask * scaling)
            grad_part = grad * mask
            probs = jnp.exp(
                lax.dot_general(
                    ones_in_lanes(lane, free, keys),
                    (query_part - in_lanes(lane, free, level_ref[:, own : own + 1])).astype(LOW),
                    NT,
                    preferred_element_type=FULL,
                )
            )
            prob_grad = lax.dot_general(
                ones_in_lanes(lane, free, values),
                (
                    grad_part - in_lanes(lane, free, jnp.sum(inner * mask, axis=-1, keepdims=True))
                ).astype(LOW),
                NT,
                preferred_element_type=FULL,
            )
            score_grad = (probs * prob_grad).astype(LOW)
            value_part = jnp.dot(probs.astype(LOW), grad_part.astype(LOW), preferred_element_type=FULL)
            key_part = jnp.dot(score_grad, query_part.astype(LOW), preferred_element_type=FULL)
            asked_part = lax.dot_general(
                score_grad, keys * (mask * scaling).astype(LOW), TN, preferred_element_type=FULL
            )
            if query_grad is None:
                query_grad, key_grad, value_grad = asked_part, key_part, value_part
            else:
                query_grad, key_grad, value_grad = (
                    query_grad + asked_part,
                    key_grad + key_part,
                    value_grad + value_part,
                )

        @pl.when(step == 0)
        def _():
            key_sum[...] = key_grad
            value_sum[...] = value_grad

        @pl.when(step > 0)
        def _():
            key_sum[...] += key_grad
            value_sum[...] += value_grad

        rows = pl.ds(pl.multiple_of(step * block, block), block)
        out_ref[rows, pl.ds(pl.multiple_of(pair * PAIR, PAIR), PAIR)] = query_grad.astype(LOW)

        @pl.when(step == steps - 1)
        def _():
            out_ref[:, pl.ds(pl.multiple_of(width + pair * PAIR, PAIR), PAIR)] = key_sum[...].astype(LOW)
            out_ref[:, pl.ds(pl.multiple_of(2 * width + pair * PAIR, PAIR), PAIR)] = value_sum[
                ...
            ].astype(LOW)

    rows_of_pair = pl.BlockSpec((block, PAIR), lambda h, i: (i, h))
    return pl.pallas_call(
        body,
        grid=(pairs, steps),
        in_specs=[
            rows_of_pair,
            pl.BlockSpec((tokens, PAIR), lambda h, i: (0, pairs + h)),
            pl.BlockSpec((tokens, PAIR), lambda h, i: (0, 2 * pairs + h)),
            rows_of_pair,
            rows_of_pair,
            rows_of_pair,
        ],
        out_specs=resident((tokens, 3 * width)),
        out_shape=jax.ShapeDtypeStruct((tokens, 3 * width), LOW),
        scratch_shapes=[pltpu.VMEM((tokens, PAIR), FULL), pltpu.VMEM((tokens, PAIR), FULL)],
        compiler_params=params(),
        cost_estimate=cost(40 * tokens * tokens * width, 20 * tokens * width, tokens * tokens * width // HEAD),
        name="attend_backward",
    )(triple, triple, triple, attended, level, grads)


def feed_both(normed, branch_grad, weights, out_type):
    tokens, depth = normed.shape
    units = weights.shape[1] // 2
    tile = min(512, units)
    steps = units // tile

    def body(normed_ref, grad_ref, up_ref, down_ref, out_ref, back_ref, hidden_ref, pre_ref, out_sum, back_sum):
        step = pl.program_id(0)
        up = up_ref[...]
        down = down_ref[...]
        pre = jnp.dot(normed_ref[...], up, preferred_element_type=FULL)
        hidden_grad = jnp.dot(grad_ref[...], down, preferred_element_type=FULL)
        square = pre * pre
        bent = jnp.tanh(0.7978845608028654 * (pre + 0.044715 * (square * pre)))
        half = 0.5 * (1.0 + bent)
        hidden = (pre * half).astype(LOW)
        slope = half + 0.5 * pre * (1.0 - bent * bent) * (
            0.7978845608028654 * (1.0 + 0.134145 * square)
        )
        pre_grad = (hidden_grad * slope).astype(LOW)
        hidden_ref[...] = hidden
        pre_ref[...] = pre_grad
        out_part = lax.dot_general(hidden, down, NT, preferred_element_type=FULL)
        back_part = lax.dot_general(pre_grad, up, NT, preferred_element_type=FULL)

        @pl.when(step == 0)
        def _():
            out_sum[...] = out_part
            back_sum[...] = back_part

        @pl.when(step > 0)
        def _():
            out_sum[...] += out_part
            back_sum[...] += back_part

        @pl.when(step == steps - 1)
        def _():
            out_ref[...] = out_sum[...].astype(out_type)
            back_ref[...] = back_sum[...].astype(out_type)

    return pl.pallas_call(
        body,
        grid=(steps,),
        in_specs=[
            resident((tokens, depth)),
            resident((tokens, depth)),
            pl.BlockSpec((depth, tile), lambda j: (0, j)),
            pl.BlockSpec((depth, tile), lambda j: (0, steps + j)),
        ],
        out_specs=[
            resident((tokens, depth)),
            resident((tokens, depth)),
            pl.BlockSpec((tokens, tile), lambda j: (0, j)),
            pl.BlockSpec((tokens, tile), lambda j: (0, j)),
        ],
        out_shape=[
            jax.ShapeDtypeStruct((tokens, depth), out_type),
            jax.ShapeDtypeStruct((tokens, depth), out_type),
            jax.ShapeDtypeStruct((tokens, units), LOW),
            jax.ShapeDtypeStruct((tokens, units), LOW),
        ],
        scratch_shapes=[pltpu.VMEM((tokens, depth), FULL), pltpu.VMEM((tokens, depth), FULL)],
        compiler_params=params(),
        cost_estimate=cost(8 * tokens * depth * units, 4 * depth * units + 12 * tokens * depth + 4 * tokens * units, tokens * units),
        name="feed_both",
    )(normed, branch_grad, weights, weights)


def standardize(values):
    middle = jnp.mean(values, axis=-1, keepdims=True)
    centred = values - middle
    spread = jnp.mean(centred * centred, axis=-1, keepdims=True)
    rate = lax.rsqrt(spread + 1e-06)
    return centred * rate, rate


def standardize_back(grad, unit, rate, scale_term):
    pulled = grad * (1.0 + scale_term)
    resid = rate * (
        pulled
        - jnp.mean(pulled, axis=-1, keepdims=True)
        - unit * jnp.mean(pulled * unit, axis=-1, keepdims=True)
    )
    return resid, jnp.sum(grad, axis=0), jnp.sum(grad * unit, axis=0)


def adam_step(weight, first, second, grad_sum, rate):
    first_new = 0.9 * first + 0.1 * grad_sum
    second_new = 0.999 * second + 0.001 * grad_sum * grad_sum
    first_hat = first_new / (1.0 - 0.9**STEP)
    second_hat = second_new / (1.0 - 0.999**STEP)
    weight_new = weight - rate * (first_hat / (jnp.sqrt(second_hat) + 1e-08) + 0.01 * weight)
    return (weight_new, first_new, second_new)


def shift_tp(values, steps, count):
    steps = steps % count
    if steps == 0:
        return values
    return lax.ppermute(values, "tp", [(i, (i + steps) % count) for i in range(count)])


def digits(count):
    if count % 8 == 0:
        return 4, count // 8, 2
    return count // 2, 1, 2


def shift_fsdp(values, digit, steps, count):
    sizes = digits(count)
    scale = (sizes[1] * sizes[2], sizes[2], 1)[digit]
    size = sizes[digit]
    pairs = []
    for source in range(count):
        own = (source // scale) % size
        pairs.append((source, source + ((own + steps) % size - own) * scale))
    return lax.ppermute(values, "fsdp", pairs)


def arrange(pieces, count, group):
    deep, across, cores = digits(count)
    width = pieces[0].shape[1]
    tile = fit(width, 512)

    def body(*refs):
        out_ref = refs[-1]
        me = lax.axis_index("fsdp")
        my_z, my_x, my_c = me // (across * cores), (me // cores) % across, me % cores
        for core in range(cores):
            for x in range(across):
                source = refs[core * across + x]
                for z in range(deep):
                    place = (
                        ((my_z - z + deep) % deep) * across + (my_x - x + across) % across
                    ) * cores + (my_c - core + cores) % cores
                    out_ref[pl.ds(pl.multiple_of(place * group, group), group), :] = source[
                        z * group : (z + 1) * group, :
                    ]

    return pl.pallas_call(
        body,
        grid=(width // tile,),
        in_specs=[pl.BlockSpec((piece.shape[0], tile), lambda j: (0, j)) for piece in pieces],
        out_specs=pl.BlockSpec((count * group, tile), lambda j: (0, j)),
        out_shape=jax.ShapeDtypeStruct((count * group, width), LOW),
        compiler_params=params(),
        cost_estimate=cost(0, 4 * count * group * width),
        name="arrange",
    )(*pieces)


def gather_z(shard, count):
    deep = digits(count)[0]
    return [shard] + [shift_fsdp(shard, 0, k, count) for k in range(1, deep)]


def gather_x(line, count):
    across = digits(count)[1]
    line = jnp.concatenate(line, axis=0)
    return [line] + [shift_fsdp(line, 1, k, count) for k in range(1, across)]


def gather_core(plane, count):
    cores = digits(count)[2]
    return plane + [shift_fsdp(piece, 2, k, count) for k in range(1, cores) for piece in plane]


def scatter_core(pair, count):
    kept, sent = pair
    return kept, shift_fsdp(sent, 2, 1, count)


def scatter_x(pair, count):
    kept, came = pair
    across = digits(count)[1]
    rows = kept.shape[0] // across

    def both(x):
        part = slice(x * rows, (x + 1) * rows)
        return kept[part].astype(FULL) + came[part].astype(FULL)

    return kept[:rows], came[:rows], [
        shift_fsdp(both(k).astype(LOW), 1, k, count) for k in range(1, across)
    ]


def scatter_z(state, count):
    kept, came, parts = state
    deep = digits(count)[0]
    group = kept.shape[0] // deep

    def both(z):
        rows = slice(z * group, (z + 1) * group)
        return sum(
            (part[rows].astype(FULL) for part in [came] + parts), start=kept[rows].astype(FULL)
        )

    return both(0), [shift_fsdp(both(k).astype(LOW), 0, k, count) for k in range(1, deep)]


def scatter_end(state):
    own, parts = state
    return sum((part.astype(FULL) for part in parts), start=own)


def gather_rows(shard):
    return lax.all_gather(shard, "fsdp", axis=0, tiled=True)


def scatter_rows(whole):
    return lax.psum_scatter(whole, "fsdp", scatter_dimension=0, tiled=True).astype(FULL)


def together(*values):
    return lax.optimization_barrier(values)


def modulation_shares(grads, tp_count, fsdp_count, part):
    count = grads.shape[0]
    by_owner = grads.reshape(count, tp_count, part)
    place = lax.axis_index("tp")
    total = sum(
        shift_tp(
            lax.dynamic_index_in_dim(by_owner, (place + k) % tp_count, axis=1, keepdims=False),
            k,
            tp_count,
        )
        for k in range(tp_count)
    )
    every = lax.all_to_all(
        jnp.broadcast_to(total.reshape(1, count * part), (fsdp_count, count * part)),
        "fsdp",
        split_axis=0,
        concat_axis=0,
        tiled=True,
    )
    return every


def local(
    fsdp_count,
    tp_count,
    latents_in,
    condition,
    out_grad,
    condition_weight,
    condition_first,
    condition_second,
    heads_weight,
    heads_first,
    heads_second,
    merge_weight,
    merge_first,
    merge_second,
    up_weight,
    up_first,
    up_second,
    down_weight,
    down_first,
    down_second,
):
    own, _, depth = latents_in.shape
    latents = latents_in.reshape(own, depth)
    cotangent = out_grad.reshape(own, depth)
    shard_rows = condition_weight.shape[0]
    part = condition_weight.shape[2]
    width = heads_weight.shape[2]
    units = up_weight.shape[1]
    ring = range(tp_count)
    others = range(1, tp_count)

    def blocks_of_tokens(values):
        return [shift_tp(values, -k, tp_count) for k in ring]

    pairs = width // PAIR
    spans = [(0, pairs // 2), (pairs // 2, pairs)] if pairs > 1 else [(0, pairs)]
    spans = [(start * PAIR, end * PAIR) for start, end in spans]

    activated = jax.nn.silu(condition).astype(LOW)
    activated_rows = lax.all_to_all(
        activated.reshape(fsdp_count, shard_rows), "fsdp", split_axis=0, concat_axis=0, tiled=True
    )

    heads_low = jnp.moveaxis(heads_weight.astype(LOW), 0, 1)
    heads_whole = gather_rows(
        jnp.concatenate(
            [heads_low[:, :, start:end].reshape(shard_rows, -1) for start, end in spans], axis=1
        )
    )
    unit_one, rate_one = standardize(latents)
    unit_blocks = blocks_of_tokens(unit_one.astype(LOW))
    shares = jnp.dot(
        activated_rows,
        condition_weight.astype(LOW).reshape(shard_rows, 6 * part),
        preferred_element_type=FULL,
    )
    shares = lax.all_to_all(shares, "fsdp", split_axis=0, concat_axis=0, tiled=True)
    merge_shard = merge_weight.astype(LOW).T
    merge_shard = jnp.concatenate([shift_tp(merge_shard, k, tp_count) for k in ring], axis=1)
    merge_line = gather_z(merge_shard, fsdp_count)
    feed_shard = jnp.concatenate([up_weight.astype(LOW), down_weight.astype(LOW).T], axis=1)
    shares, unit_blocks = together(shares, unit_blocks)
    modulation_part = jnp.sum(shares, axis=0).reshape(6, part)
    modulation = lax.all_gather(modulation_part, "tp", axis=1, tiled=True)
    shift_one, scale_one, gate_one, shift_two, scale_two, gate_two = (
        modulation[k : k + 1] for k in range(6)
    )

    branch_grad = (gate_two * cotangent).astype(LOW)
    branch_grad_blocks = blocks_of_tokens(branch_grad)

    normed_one = jnp.concatenate(
        [
            ((unit_one if k == 0 else unit_blocks[k].astype(FULL)) * (1.0 + scale_one) + shift_one).astype(LOW)
            for k in ring
        ],
        axis=0,
    )
    heads_whole, feed_shard, normed_one, merge_line = together(
        heads_whole, feed_shard, normed_one, merge_line
    )
    feed_whole = gather_rows(feed_shard)
    triples = [
        product(normed_one, heads_whole, LOW, 3 * start, 3 * (end - start)) for start, end in spans
    ]
    triples[0], merge_line = together(triples[0], merge_line)
    merge_plane = gather_x(merge_line, fsdp_count)
    attended = []
    mixes = []
    for index, (start, end) in enumerate(spans):
        mixed, level = attend_forward(triples[index], end - start)
        if index == 0:
            mixed, merge_plane, branch_grad_blocks = together(mixed, merge_plane, branch_grad_blocks)
            merge_whole = arrange(gather_core(merge_plane, fsdp_count), fsdp_count, shard_rows)
        mixes.append((mixed, level))
        attended.append([shift_tp(mixed[k * own : (k + 1) * own], k, tp_count) for k in ring])
    attended_own = jnp.concatenate([part[k] for k in ring for part in attended], axis=1)
    attn_branch = product_back([attended_own], merge_whole, FULL)
    after_attn = latents + gate_one * attn_branch
    unit_two, rate_two = standardize(after_attn)
    normed_two = (unit_two * (1.0 + scale_two) + shift_two).astype(LOW)
    normed_two_blocks = blocks_of_tokens(normed_two)

    fed = [feed_both(normed_two_blocks[0], branch_grad_blocks[0], feed_whole, FULL)]
    if tp_count > 1:
        fed, normed_two_blocks = together(fed, normed_two_blocks)
    fed += [feed_both(normed_two_blocks[k], branch_grad_blocks[k], feed_whole, LOW) for k in others]
    back_parts = [shift_tp(fed[k][1], k, tp_count) for k in others]
    (feed_grad,) = token_sum(
        [
            (normed_two_blocks, [fed[k][3] for k in ring]),
            (branch_grad_blocks, [fed[k][2] for k in ring]),
        ],
        fsdp_count,
        ordered=False,
    )
    branch_parts = [fed[k][0] for k in others]
    back_parts, branch_parts, feed_grad = together(back_parts, branch_parts, feed_grad)
    feed_sum = scatter_rows(feed_grad)
    branch_parts = [shift_tp(values, k, tp_count) for k, values in zip(others, branch_parts)]
    normed_two_grad = fed[0][1]
    for part_grad in back_parts:
        normed_two_grad = normed_two_grad + part_grad.astype(FULL)
    resid_two, shift_two_grad, scale_two_grad = standardize_back(
        normed_two_grad, unit_two, rate_two, scale_two
    )
    after_grad = cotangent + resid_two
    attn_grad = (gate_one * after_grad).astype(LOW)
    gate_one_grad = jnp.sum(after_grad * attn_branch, axis=0)
    attended_grad_own = product(attn_grad, merge_whole, LOW)
    attended_grads = [
        jnp.concatenate(
            [
                shift_tp(attended_grad_own[:, k * width + start : k * width + end], -k, tp_count)
                for k in ring
            ],
            axis=0,
        )
        for start, end in spans
    ]

    triple_grads = [
        attend_backward(triples[0], *mixes[0], attended_grads[0], spans[0][1] - spans[0][0])
    ]
    triple_grads, branch_parts = together(triple_grads, branch_parts)
    mlp_branch = fed[0][0]
    for part_branch in branch_parts:
        mlp_branch = mlp_branch + part_branch.astype(FULL)
    block_out = after_attn + gate_two * mlp_branch
    gate_two_grad = jnp.sum(cotangent * mlp_branch, axis=0)
    early_grads = jnp.stack([gate_one_grad, shift_two_grad, scale_two_grad, gate_two_grad], axis=0)

    pair = token_sum([([attn_grad], [attended_own]), ([normed_one], triple_grads)], fsdp_count)
    state = scatter_core(pair, fsdp_count)
    if len(spans) > 1:
        attended_grads, state, early_grads, block_out = together(
            attended_grads, state, early_grads, block_out
        )
    state = scatter_x(state, fsdp_count)
    for index in range(1, len(spans)):
        start, end = spans[index]
        triple_grads.append(
            attend_backward(triples[index], *mixes[index], attended_grads[index], end - start)
        )
    triple_grads, state = together(triple_grads, state)
    parts = [
        product_back([grad[k * own : (k + 1) * own] for grad in triple_grads], heads_whole, LOW)
        for k in others
    ]
    one_parts = [shift_tp(values, k, tp_count) for k, values in zip(others, parts)]
    triple_grads, parts = together(triple_grads, parts)
    last = None
    if len(spans) > 1:
        pair = token_sum([([normed_one], triple_grads[1:])], fsdp_count)
        triple_grads, pair = together(triple_grads, pair)
        last = scatter_core(pair, fsdp_count)
    normed_one_grad = product_back([grad[:own] for grad in triple_grads], heads_whole, FULL)
    up_new = adam_step(up_weight, up_first, up_second, feed_sum[:, :units], 0.02)
    down_new = adam_step(down_weight, down_first, down_second, feed_sum[:, units:].T, 0.01)
    one_parts, normed_one_grad, state, last, up_new, down_new = together(
        one_parts, normed_one_grad, state, last, up_new, down_new
    )
    if last:
        last = scatter_x(last, fsdp_count)
    for part_grad in one_parts:
        normed_one_grad = normed_one_grad + part_grad.astype(FULL)
    resid_one, shift_one_grad, scale_one_grad = standardize_back(
        normed_one_grad, unit_one, rate_one, scale_one
    )
    shift_one_grad, scale_one_grad, last = together(shift_one_grad, scale_one_grad, last)
    first_sum = scatter_end(scatter_z(state, fsdp_count))
    merge_sum_all, heads_sums = first_sum[:, : tp_count * width], [first_sum[:, tp_count * width :]]
    if last:
        heads_sums.append(scatter_end(scatter_z(last, fsdp_count)))
    heads_sums = [total.reshape(shard_rows, 3, -1) for total in heads_sums]
    latents_grad = after_grad + resid_one
    modulation_all = modulation_shares(
        jnp.concatenate([jnp.stack([shift_one_grad, scale_one_grad], axis=0), early_grads], axis=0),
        tp_count,
        fsdp_count,
        part,
    )
    condition_sum = lax.dot_general(
        activated_rows.astype(FULL),
        modulation_all,
        TN,
        precision=lax.Precision.HIGHEST,
        preferred_element_type=FULL,
    ).reshape(shard_rows, 6, part)
    merge_sum = merge_sum_all[:, :width]
    for k in others:
        merge_sum = merge_sum + shift_tp(
            merge_sum_all[:, k * width : (k + 1) * width], -k, tp_count
        )
    heads_sum = jnp.moveaxis(jnp.concatenate(heads_sums, axis=2), 1, 0)
    cond_new = adam_step(condition_weight, condition_first, condition_second, condition_sum, 0.02)
    heads_new = adam_step(heads_weight, heads_first, heads_second, heads_sum, 0.02)
    merge_new = adam_step(merge_weight, merge_first, merge_second, merge_sum.T, 0.15)
    return (
        block_out.reshape(own, 1, depth),
        latents_grad.reshape(own, 1, depth),
        *cond_new,
        *heads_new,
        *merge_new,
        *up_new,
        *down_new,
    )


def solution(mesh):
    stream = P("tp", "fsdp", None)
    cond = P("fsdp", None, "tp")
    heads = P(None, "fsdp", "tp")
    wide = P("tp", "fsdp")
    tall = P("fsdp", "tp")
    in_specs = (stream, P("fsdp", None), stream) + (cond,) * 3 + (heads,) * 3 + (wide,) * 3 + (tall,) * 3 + (wide,) * 3
    out_specs = (stream, stream) + (cond,) * 3 + (heads,) * 3 + (wide,) * 3 + (tall,) * 3 + (wide,) * 3
    return jax.shard_map(
        functools.partial(local, mesh.shape["fsdp"], mesh.shape["tp"]),
        mesh=mesh,
        in_specs=in_specs,
        out_specs=out_specs,
        check_vma=False,
    )
```

```python
import functools

import jax
import jax.numpy as jnp
from jax import lax
from jax.experimental import pallas as pl
from jax.experimental.pallas import tpu as pltpu
from jax.sharding import PartitionSpec as P

HEAD = 64
PAIR = 2 * HEAD
STEP = 5
LOW = jnp.bfloat16
FULL = jnp.float32
NT = (((1,), (1,)), ((), ()))
TN = (((0,), (0,)), ((), ()))


def params(limit=56):
    return pltpu.CompilerParams(vmem_limit_bytes=limit * 1024 * 1024)


def cost(flops, moved, raised=0):
    return pl.CostEstimate(flops=int(flops), bytes_accessed=int(moved), transcendentals=int(raised))


def resident(shape):
    return pl.BlockSpec(shape, lambda *step: (0,) * len(shape))


def fit(width, most):
    return next(tile for tile in (most, 512, 256, PAIR) if tile <= most and width % tile == 0)


def product(left, right, out_type, start=0, width=None):
    rows, depth = left.shape
    width = width or right.shape[1]
    tile = fit(width, 512)
    first = start // tile

    def body(left_ref, right_ref, out_ref):
        out_ref[...] = jnp.dot(
            left_ref[...], right_ref[...], preferred_element_type=FULL
        ).astype(out_type)

    return pl.pallas_call(
        body,
        grid=(width // tile,),
        in_specs=[
            resident((rows, depth)),
            pl.BlockSpec((depth, tile), lambda j: (0, first + j)),
        ],
        out_specs=pl.BlockSpec((rows, tile), lambda j: (0, j)),
        out_shape=jax.ShapeDtypeStruct((rows, width), out_type),
        compiler_params=params(),
        cost_estimate=cost(2 * rows * depth * width, 2 * (rows * depth + depth * width) + 4 * rows * width),
        name="product",
    )(left, right)


def product_back(lefts, right, out_type, rows, part):
    width, depth = right.shape
    tile = min(256, width)

    def body(*refs):
        total = None
        start = 0
        for left_ref in refs[:-2]:
            extent = left_ref.shape[1]
            term = lax.dot_general(
                left_ref[...], refs[-2][:, start : start + extent], NT, preferred_element_type=FULL
            )
            total = term if total is None else total + term
            start += extent
        refs[-1][...] = total.astype(out_type)

    return pl.pallas_call(
        body,
        grid=(width // tile,),
        in_specs=[pl.BlockSpec((rows, left.shape[1]), lambda j: (part, 0)) for left in lefts]
        + [pl.BlockSpec((tile, depth), lambda j: (j, 0))],
        out_specs=pl.BlockSpec((rows, tile), lambda j: (0, j)),
        out_shape=jax.ShapeDtypeStruct((rows, width), out_type),
        compiler_params=params(),
        cost_estimate=cost(2 * rows * depth * width, 2 * (rows * depth + width * depth) + 4 * rows * width),
        name="product_back",
    )(*lefts, right)


def token_sum(jobs, count, ordered=True):
    depth = jobs[0][0][0].shape[1]
    widths = [rights[0].shape[1] for _, rights in jobs]
    width = sum(widths)
    tokens = max(sum(left.shape[0] for left in lefts) for lefts, _ in jobs)
    tile = min(fit(extent, 512) for extent in widths)
    deep, across, cores = digits(count)
    group = depth // count
    pieces = len(jobs[0][0])
    starts = [sum(widths[:index]) // tile for index in range(len(jobs) + 1)]

    def flip(left_refs, turned):
        me = lax.axis_index("fsdp")
        my_z, my_x, my_c = me // (across * cores), (me // cores) % across, me % cores
        start = 0
        for left_ref in left_refs:
            flipped = left_ref[...].T
            extent = left_ref.shape[0]
            if not ordered:
                turned[:, start : start + extent] = flipped
            for source in range(count if ordered else 0):
                z, x, c = source // (across * cores), (source // cores) % across, source % cores
                place = (
                    ((c - my_c + cores) % cores) * across + (x - my_x + across) % across
                ) * deep + (z - my_z + deep) % deep
                turned[pl.ds(pl.multiple_of(place * group, group), group), start : start + extent] = (
                    flipped[source * group : (source + 1) * group]
                )
            start += extent

    def body(*refs):
        out_refs, turned = refs[2 * pieces * len(jobs) : -1], refs[-1]
        step = pl.program_id(0)
        for index in range(len(jobs)):
            mine = refs[2 * pieces * index : 2 * pieces * (index + 1)]

            @pl.when(step == starts[index])
            def _():
                flip(mine[:pieces], turned)

            @pl.when((step >= starts[index]) & (step < starts[index + 1]))
            def _():
                total = None
                start = 0
                for right_ref in mine[pieces:]:
                    extent = right_ref.shape[0]
                    term = jnp.dot(
                        turned[:, start : start + extent], right_ref[...], preferred_element_type=FULL
                    )
                    total = term if total is None else total + term
                    start += extent
                total = total.astype(LOW)
                start = 0
                for out_ref in out_refs:
                    out_ref[...] = total[start : start + out_ref.shape[0]]
                    start += out_ref.shape[0]

    def place_of(index):
        last = widths[index] // tile - 1
        return lambda j: (0, jnp.clip(j - starts[index], 0, last))

    half = depth // cores
    heights = (half, depth - half) if ordered else (depth,)
    in_specs = []
    operands = []
    for index, (lefts, rights) in enumerate(jobs):
        in_specs += [resident(left.shape) for left in lefts]
        in_specs += [pl.BlockSpec((right.shape[0], tile), place_of(index)) for right in rights]
        operands += [*lefts, *rights]
    return pl.pallas_call(
        body,
        grid=(width // tile,),
        in_specs=in_specs,
        out_specs=[pl.BlockSpec((height, tile), lambda j: (0, j)) for height in heights],
        out_shape=[jax.ShapeDtypeStruct((height, width), LOW) for height in heights],
        scratch_shapes=[pltpu.VMEM((depth, tokens), LOW)],
        compiler_params=params(),
        cost_estimate=cost(
            2 * depth * tokens * width, 2 * (len(jobs) * depth * tokens + tokens * width + depth * width)
        ),
        name="token_sum",
    )(*operands)


def head_lanes():
    lane = lax.broadcasted_iota(jnp.int32, (1, PAIR), 1)
    first = (lane < HEAD).astype(FULL)
    return lane, ((first, HEAD), (1.0 - first, 0))


def in_lanes(lane, free, column):
    total = 0.0
    for index in range(3):
        piece = column.astype(LOW).astype(FULL)
        total = total + jnp.where(lane == free + index, piece, 0.0)
        column = column - piece
    return total


def ones_in_lanes(lane, free, values):
    return jnp.where((lane >= free) & (lane < free + 3), 1.0, values.astype(FULL)).astype(LOW)


def attend_forward(triple, width):
    tokens = triple.shape[0]
    pairs = width // PAIR
    block = min(512, tokens)
    scaling = HEAD ** (-0.5)

    def body(query_ref, keys_ref, values_ref, out_ref, level_ref):
        lane, heads = head_lanes()
        keys = keys_ref[...]
        values = values_ref[...].astype(FULL)
        query = query_ref[...].astype(FULL)
        total = level = 0.0
        for mask, free in heads:
            scores = lax.dot_general(
                (query * (mask * scaling)).astype(LOW), keys, NT, preferred_element_type=FULL
            )
            peak = jnp.max(scores, axis=-1, keepdims=True)
            raised = jnp.exp(scores - peak).astype(LOW)
            counted = jnp.where(lane == free, 1.0, values * mask).astype(LOW)
            mixed = jnp.dot(raised, counted, preferred_element_type=FULL)
            sums = mixed[:, free : free + 1]
            total = total + mixed * mask / sums
            level = level + mask * (peak + jnp.log(sums))
        out_ref[...] = total.astype(LOW)
        level_ref[...] = level

    return pl.pallas_call(
        body,
        grid=(pairs, tokens // block),
        in_specs=[
            pl.BlockSpec((block, PAIR), lambda h, i: (i, h)),
            pl.BlockSpec((tokens, PAIR), lambda h, i: (0, pairs + h)),
            pl.BlockSpec((tokens, PAIR), lambda h, i: (0, 2 * pairs + h)),
        ],
        out_specs=[pl.BlockSpec((block, PAIR), lambda h, i: (i, h))] * 2,
        out_shape=[
            jax.ShapeDtypeStruct((tokens, width), LOW),
            jax.ShapeDtypeStruct((tokens, width), FULL),
        ],
        compiler_params=params(),
        cost_estimate=cost(16 * tokens * tokens * width, 12 * tokens * width, tokens * tokens * width // HEAD),
        name="attend_forward",
    )(triple, triple, triple)


def attend_backward(triple, attended, level, grads, width):
    tokens = triple.shape[0]
    pairs = width // PAIR
    block = min(512, tokens)
    steps = tokens // block
    scaling = HEAD ** (-0.5)

    def body(query_ref, keys_ref, values_ref, out_low_ref, level_ref, grad_ref, out_ref, key_sum, value_sum):
        pair = pl.program_id(0)
        step = pl.program_id(1)
        lane, heads = head_lanes()
        keys = keys_ref[...]
        values = values_ref[...]
        query = query_ref[...].astype(FULL)
        grad = grad_ref[...].astype(FULL)
        inner = grad * out_low_ref[...].astype(FULL)
        query_grad = key_grad = value_grad = None
        for index, (mask, free) in enumerate(heads):
            own = HEAD * index
            query_part = query * (mask * scaling)
            grad_part = grad * mask
            probs = jnp.exp(
                lax.dot_general(
                    ones_in_lanes(lane, free, keys),
                    (query_part - in_lanes(lane, free, level_ref[:, own : own + 1])).astype(LOW),
                    NT,
                    preferred_element_type=FULL,
                )
            )
            prob_grad = lax.dot_general(
                ones_in_lanes(lane, free, values),
                (
                    grad_part - in_lanes(lane, free, jnp.sum(inner * mask, axis=-1, keepdims=True))
                ).astype(LOW),
                NT,
                preferred_element_type=FULL,
            )
            score_grad = (probs * prob_grad).astype(LOW)
            value_part = jnp.dot(probs.astype(LOW), grad_part.astype(LOW), preferred_element_type=FULL)
            key_part = jnp.dot(score_grad, query_part.astype(LOW), preferred_element_type=FULL)
            asked_part = lax.dot_general(
                score_grad, keys * (mask * scaling).astype(LOW), TN, preferred_element_type=FULL
            )
            if query_grad is None:
                query_grad, key_grad, value_grad = asked_part, key_part, value_part
            else:
                query_grad, key_grad, value_grad = (
                    query_grad + asked_part,
                    key_grad + key_part,
                    value_grad + value_part,
                )

        @pl.when(step == 0)
        def _():
            key_sum[...] = key_grad
            value_sum[...] = value_grad

        @pl.when(step > 0)
        def _():
            key_sum[...] += key_grad
            value_sum[...] += value_grad

        rows = pl.ds(pl.multiple_of(step * block, block), block)
        out_ref[rows, pl.ds(pl.multiple_of(pair * PAIR, PAIR), PAIR)] = query_grad.astype(LOW)

        @pl.when(step == steps - 1)
        def _():
            out_ref[:, pl.ds(pl.multiple_of(width + pair * PAIR, PAIR), PAIR)] = key_sum[...].astype(LOW)
            out_ref[:, pl.ds(pl.multiple_of(2 * width + pair * PAIR, PAIR), PAIR)] = value_sum[
                ...
            ].astype(LOW)

    rows_of_pair = pl.BlockSpec((block, PAIR), lambda h, i: (i, h))
    return pl.pallas_call(
        body,
        grid=(pairs, steps),
        in_specs=[
            rows_of_pair,
            pl.BlockSpec((tokens, PAIR), lambda h, i: (0, pairs + h)),
            pl.BlockSpec((tokens, PAIR), lambda h, i: (0, 2 * pairs + h)),
            rows_of_pair,
            rows_of_pair,
            rows_of_pair,
        ],
        out_specs=resident((tokens, 3 * width)),
        out_shape=jax.ShapeDtypeStruct((tokens, 3 * width), LOW),
        scratch_shapes=[pltpu.VMEM((tokens, PAIR), FULL), pltpu.VMEM((tokens, PAIR), FULL)],
        compiler_params=params(),
        cost_estimate=cost(40 * tokens * tokens * width, 20 * tokens * width, tokens * tokens * width // HEAD),
        name="attend_backward",
    )(triple, triple, triple, attended, level, grads)


def feed_both(normed, branch_grad, weights, out_type):
    tokens, depth = normed.shape
    units = weights.shape[1] // 2
    tile = min(512, units)
    steps = units // tile

    def body(normed_ref, grad_ref, up_ref, down_ref, out_ref, back_ref, hidden_ref, pre_ref, out_sum, back_sum):
        step = pl.program_id(0)
        up = up_ref[...]
        down = down_ref[...]
        pre = jnp.dot(normed_ref[...], up, preferred_element_type=FULL)
        hidden_grad = jnp.dot(grad_ref[...], down, preferred_element_type=FULL)
        square = pre * pre
        bent = jnp.tanh(0.7978845608028654 * (pre + 0.044715 * (square * pre)))
        half = 0.5 * (1.0 + bent)
        hidden = (pre * half).astype(LOW)
        slope = half + 0.5 * pre * (1.0 - bent * bent) * (
            0.7978845608028654 * (1.0 + 0.134145 * square)
        )
        pre_grad = (hidden_grad * slope).astype(LOW)
        hidden_ref[...] = hidden
        pre_ref[...] = pre_grad
        out_part = lax.dot_general(hidden, down, NT, preferred_element_type=FULL)
        back_part = lax.dot_general(pre_grad, up, NT, preferred_element_type=FULL)

        @pl.when(step == 0)
        def _():
            out_sum[...] = out_part
            back_sum[...] = back_part

        @pl.when(step > 0)
        def _():
            out_sum[...] += out_part
            back_sum[...] += back_part

        @pl.when(step == steps - 1)
        def _():
            out_ref[...] = out_sum[...].astype(out_type)
            back_ref[...] = back_sum[...].astype(out_type)

    return pl.pallas_call(
        body,
        grid=(steps,),
        in_specs=[
            resident((tokens, depth)),
            resident((tokens, depth)),
            pl.BlockSpec((depth, tile), lambda j: (0, j)),
            pl.BlockSpec((depth, tile), lambda j: (0, steps + j)),
        ],
        out_specs=[
            resident((tokens, depth)),
            resident((tokens, depth)),
            pl.BlockSpec((tokens, tile), lambda j: (0, j)),
            pl.BlockSpec((tokens, tile), lambda j: (0, j)),
        ],
        out_shape=[
            jax.ShapeDtypeStruct((tokens, depth), out_type),
            jax.ShapeDtypeStruct((tokens, depth), out_type),
            jax.ShapeDtypeStruct((tokens, units), LOW),
            jax.ShapeDtypeStruct((tokens, units), LOW),
        ],
        scratch_shapes=[pltpu.VMEM((tokens, depth), FULL), pltpu.VMEM((tokens, depth), FULL)],
        compiler_params=params(),
        cost_estimate=cost(8 * tokens * depth * units, 4 * depth * units + 12 * tokens * depth + 4 * tokens * units, tokens * units),
        name="feed_both",
    )(normed, branch_grad, weights, weights)


def standardize(values):
    middle = jnp.mean(values, axis=-1, keepdims=True)
    centred = values - middle
    spread = jnp.mean(centred * centred, axis=-1, keepdims=True)
    rate = lax.rsqrt(spread + 1e-06)
    return centred * rate, rate


def standardize_back(grad, values, scale_term):
    unit, rate = standardize(values)
    pulled = grad * (1.0 + scale_term)
    resid = rate * (
        pulled
        - jnp.mean(pulled, axis=-1, keepdims=True)
        - unit * jnp.mean(pulled * unit, axis=-1, keepdims=True)
    )
    return resid, jnp.sum(grad, axis=0, keepdims=True), jnp.sum(grad * unit, axis=0, keepdims=True)


def store_sums(sums_ref, rows):
    @pl.when(pl.program_id(0) == 0)
    def _():
        sums_ref[...] = jnp.zeros_like(sums_ref)

    for index, row in enumerate(rows):
        sums_ref[index : index + 1, :] += row


def store_lines(out_ref, values):
    for index in range(out_ref.shape[1]):
        out_ref[:, index, :] = values[:, index * PAIR : (index + 1) * PAIR]


def by_tokens(body, arrays, wholes, outs, sums, flops, name):
    tokens = arrays[0].shape[0]
    block = min(256, tokens)

    def cut(shape):
        return pl.BlockSpec((block,) + shape[1:], lambda j: (j,) + (0,) * (len(shape) - 1))

    out_specs = [cut(shape) for shape, _ in outs]
    out_shape = [jax.ShapeDtypeStruct(shape, kind) for shape, kind in outs]
    if sums:
        out_specs.append(resident((8, sums)))
        out_shape.append(jax.ShapeDtypeStruct((8, sums), FULL))
    moved = sum(value.size * value.dtype.itemsize for value in list(arrays) + list(wholes) + out_shape)
    return pl.pallas_call(
        body,
        grid=(tokens // block,),
        in_specs=[cut(value.shape) for value in arrays] + [resident(value.shape) for value in wholes],
        out_specs=out_specs,
        out_shape=out_shape,
        compiler_params=params(),
        cost_estimate=cost(flops, moved),
        name=name,
    )(*arrays, *wholes)


def merge_and_normalize(attended, latents, merge, gate, shift, scale):
    tokens, depth = latents.shape

    def body(attended_ref, latents_ref, merge_ref, gate_ref, shift_ref, scale_ref, branch_ref, after_ref, normed_ref):
        branch = lax.dot_general(attended_ref[...], merge_ref[...], NT, preferred_element_type=FULL)
        after = latents_ref[...] + gate_ref[...] * branch
        branch_ref[...] = branch
        after_ref[...] = after
        normed_ref[...] = (
            standardize(after)[0] * (1.0 + scale_ref[...]) + shift_ref[...]
        ).astype(LOW)

    shape = (tokens, depth)
    return by_tokens(
        body,
        [attended, latents],
        [merge, gate, shift, scale],
        [(shape, FULL), (shape, FULL), (shape, LOW)],
        0,
        2 * tokens * depth * merge.shape[1],
        "merge_and_normalize",
    )


def second_back(grad, parts, after, branch, cotangent, merge, gate, scale, spans):
    tokens, depth = after.shape
    count = len(parts)

    def body(*refs):
        total = refs[0][...]
        for part_ref in refs[1 : 1 + count]:
            total = total + part_ref[...].astype(FULL)
        after_ref, branch_ref, cotangent_ref, merge_ref, gate_ref, scale_ref = refs[1 + count : 7 + count]
        grad_ref, low_ref = refs[7 + count : 9 + count]
        piece_refs, sums_ref = refs[9 + count : -1], refs[-1]
        resid, shift_grad, scale_grad = standardize_back(total, after_ref[...], scale_ref[...])
        after_grad = cotangent_ref[...] + resid
        low = (gate_ref[...] * after_grad).astype(LOW)
        grad_ref[...] = after_grad
        low_ref[...] = low
        back = jnp.dot(low, merge_ref[...], preferred_element_type=FULL).astype(LOW)
        for piece_ref, (start, end) in zip(piece_refs, spans):
            piece_ref[...] = back[:, start:end]
        store_sums(
            sums_ref,
            [jnp.sum(after_grad * branch_ref[...], axis=0, keepdims=True), shift_grad, scale_grad],
        )

    outs = [((tokens, depth), FULL), ((tokens, depth), LOW)]
    outs += [((tokens, end - start), LOW) for start, end in spans]
    results = by_tokens(
        body,
        [grad, *parts, after, branch, cotangent],
        [merge, gate, scale],
        outs,
        depth,
        2 * tokens * depth * merge.shape[1],
        "second_back",
    )
    return results[0], results[1], results[2:-1], results[-1]


def first_back(grad, parts, latents, after_grad, scale):
    tokens, depth = latents.shape
    count = len(parts)

    def body(*refs):
        total = refs[0][...]
        for part_ref in refs[1 : 1 + count]:
            total = total + part_ref[...].astype(FULL)
        latents_ref, after_ref, scale_ref, out_ref, sums_ref = refs[1 + count :]
        resid, shift_grad, scale_grad = standardize_back(total, latents_ref[...], scale_ref[...])
        store_lines(out_ref, after_ref[...] + resid)
        store_sums(sums_ref, [shift_grad, scale_grad])

    return by_tokens(
        body,
        [grad, *parts, latents, after_grad],
        [scale],
        [((tokens, depth // PAIR, PAIR), FULL)],
        depth,
        20 * tokens * depth,
        "first_back",
    )


def last_forward(branch, parts, after, cotangent, gate):
    tokens, depth = after.shape
    count = len(parts)

    def body(*refs):
        total = refs[0][...]
        for part_ref in refs[1 : 1 + count]:
            total = total + part_ref[...].astype(FULL)
        after_ref, cotangent_ref, gate_ref, out_ref, sums_ref = refs[1 + count :]
        store_lines(out_ref, after_ref[...] + gate_ref[...] * total)
        store_sums(sums_ref, [jnp.sum(cotangent_ref[...] * total, axis=0, keepdims=True)])

    return by_tokens(
        body,
        [branch, *parts, after, cotangent],
        [gate],
        [((tokens, depth // PAIR, PAIR), FULL)],
        depth,
        6 * tokens * depth,
        "last_forward",
    )


def adam_step(weight, first, second, grad_sum, rate):
    first_new = 0.9 * first + 0.1 * grad_sum
    second_new = 0.999 * second + 0.001 * grad_sum * grad_sum
    first_hat = first_new / (1.0 - 0.9**STEP)
    second_hat = second_new / (1.0 - 0.999**STEP)
    weight_new = weight - rate * (first_hat / (jnp.sqrt(second_hat) + 1e-08) + 0.01 * weight)
    return (weight_new, first_new, second_new)


def shift_tp(values, steps, count):
    steps = steps % count
    if steps == 0:
        return values
    return lax.ppermute(values, "tp", [(i, (i + steps) % count) for i in range(count)])


def digits(count):
    if count % 8 == 0:
        return 4, count // 8, 2
    return count // 2, 1, 2


def shift_fsdp(values, digit, steps, count):
    sizes = digits(count)
    scale = (sizes[1] * sizes[2], sizes[2], 1)[digit]
    size = sizes[digit]
    pairs = []
    for source in range(count):
        own = (source // scale) % size
        pairs.append((source, source + ((own + steps) % size - own) * scale))
    return lax.ppermute(values, "fsdp", pairs)


def arrange(pieces, count, group):
    deep, across, cores = digits(count)
    width = pieces[0].shape[1]
    tile = fit(width, 512)

    def body(*refs):
        out_ref = refs[-1]
        me = lax.axis_index("fsdp")
        my_z, my_x, my_c = me // (across * cores), (me // cores) % across, me % cores
        for core in range(cores):
            for x in range(across):
                source = refs[core * across + x]
                for z in range(deep):
                    place = (
                        ((my_z - z + deep) % deep) * across + (my_x - x + across) % across
                    ) * cores + (my_c - core + cores) % cores
                    out_ref[pl.ds(pl.multiple_of(place * group, group), group), :] = source[
                        z * group : (z + 1) * group, :
                    ]

    return pl.pallas_call(
        body,
        grid=(width // tile,),
        in_specs=[pl.BlockSpec((piece.shape[0], tile), lambda j: (0, j)) for piece in pieces],
        out_specs=pl.BlockSpec((count * group, tile), lambda j: (0, j)),
        out_shape=jax.ShapeDtypeStruct((count * group, width), LOW),
        compiler_params=params(),
        cost_estimate=cost(0, 4 * count * group * width),
        name="arrange",
    )(*pieces)


def gather_z(shard, count):
    deep = digits(count)[0]
    return [shard] + [shift_fsdp(shard, 0, k, count) for k in range(1, deep)]


def gather_x(line, count):
    across = digits(count)[1]
    line = jnp.concatenate(line, axis=0)
    return [line] + [shift_fsdp(line, 1, k, count) for k in range(1, across)]


def gather_core(plane, count):
    cores = digits(count)[2]
    return plane + [shift_fsdp(piece, 2, k, count) for k in range(1, cores) for piece in plane]


def scatter_core(pair, count):
    kept, sent = pair
    return kept, shift_fsdp(sent, 2, 1, count)


def scatter_x(pair, count):
    kept, came = pair
    across = digits(count)[1]
    rows = kept.shape[0] // across

    def both(x):
        part = slice(x * rows, (x + 1) * rows)
        return kept[part].astype(FULL) + came[part].astype(FULL)

    return kept[:rows], came[:rows], [
        shift_fsdp(both(k).astype(LOW), 1, k, count) for k in range(1, across)
    ]


def scatter_z(state, count):
    kept, came, parts = state
    deep = digits(count)[0]
    group = kept.shape[0] // deep

    def both(z):
        rows = slice(z * group, (z + 1) * group)
        return sum(
            (part[rows].astype(FULL) for part in [came] + parts), start=kept[rows].astype(FULL)
        )

    return both(0), [shift_fsdp(both(k).astype(LOW), 0, k, count) for k in range(1, deep)]


def scatter_end(state):
    own, parts = state
    return sum((part.astype(FULL) for part in parts), start=own)


def gather_rows(shard):
    return lax.all_gather(shard, "fsdp", axis=0, tiled=True)


def scatter_rows(whole):
    return lax.psum_scatter(whole, "fsdp", scatter_dimension=0, tiled=True)


def together(*values):
    return lax.optimization_barrier(values)


def modulation_shares(grads, tp_count, fsdp_count, part):
    count = grads.shape[0]
    place = lax.axis_index("tp")
    total = sum(
        shift_tp(
            lax.dynamic_slice_in_dim(grads, (place + k) % tp_count * part, part, axis=1), k, tp_count
        )
        for k in range(tp_count)
    )
    every = lax.all_to_all(
        jnp.broadcast_to(total.reshape(1, count * part), (fsdp_count, count * part)),
        "fsdp",
        split_axis=0,
        concat_axis=0,
        tiled=True,
    )
    return every


def local(
    fsdp_count,
    tp_count,
    latents_in,
    condition,
    out_grad,
    condition_weight,
    condition_first,
    condition_second,
    heads_weight,
    heads_first,
    heads_second,
    merge_weight,
    merge_first,
    merge_second,
    up_weight,
    up_first,
    up_second,
    down_weight,
    down_first,
    down_second,
):
    own, _, depth = latents_in.shape
    shard_rows = condition_weight.shape[0]
    part = condition_weight.shape[2]
    width = heads_weight.shape[2]
    units = up_weight.shape[1]
    ring = range(tp_count)
    others = range(1, tp_count)

    def blocks_of_tokens(values):
        return [shift_tp(values, -k, tp_count) for k in ring]

    pairs = width // PAIR
    spans = [(0, pairs // 2), (pairs // 2, pairs)] if pairs > 1 else [(0, pairs)]
    spans = [(start * PAIR, end * PAIR) for start, end in spans]

    heads_low = jnp.moveaxis(heads_weight.astype(LOW), 0, 1)
    heads_shard = jnp.concatenate(
        [heads_low[:, :, start:end].reshape(shard_rows, -1) for start, end in spans], axis=1
    )
    activated = jax.nn.silu(condition).astype(LOW)
    activated, heads_shard = together(activated, heads_shard)
    heads_whole = gather_rows(heads_shard)
    activated_rows = lax.all_to_all(
        activated.reshape(fsdp_count, shard_rows), "fsdp", split_axis=0, concat_axis=0, tiled=True
    )
    latents, _ = together(latents_in.reshape(own, depth), heads_shard)
    (cotangent,) = together(out_grad.reshape(own, depth))

    unit_one, _ = standardize(latents)
    unit_blocks = blocks_of_tokens(unit_one.astype(LOW))
    shares = jnp.dot(
        activated_rows,
        condition_weight.astype(LOW).reshape(shard_rows, 6 * part),
        preferred_element_type=FULL,
    )
    shares = lax.all_to_all(shares, "fsdp", split_axis=0, concat_axis=0, tiled=True)
    merge_shard = merge_weight.astype(LOW).T
    merge_shard = jnp.concatenate([shift_tp(merge_shard, k, tp_count) for k in ring], axis=1)
    merge_line = gather_z(merge_shard, fsdp_count)
    feed_shard = jnp.concatenate([up_weight.astype(LOW), down_weight.astype(LOW).T], axis=1)
    shares, unit_blocks, cotangent = together(shares, unit_blocks, cotangent)
    modulation_part = jnp.sum(shares, axis=0).reshape(6, part)
    modulation = lax.all_gather(modulation_part, "tp", axis=1, tiled=True)
    shift_one, scale_one, gate_one, shift_two, scale_two, gate_two = (
        modulation[k : k + 1] for k in range(6)
    )

    branch_grad = (gate_two * cotangent).astype(LOW)
    branch_grad_blocks = blocks_of_tokens(branch_grad)

    normed_one = jnp.concatenate(
        [
            ((unit_one if k == 0 else unit_blocks[k].astype(FULL)) * (1.0 + scale_one) + shift_one).astype(LOW)
            for k in ring
        ],
        axis=0,
    )
    heads_whole, feed_shard, normed_one, merge_line = together(
        heads_whole, feed_shard, normed_one, merge_line
    )
    feed_whole = gather_rows(feed_shard)
    triples = [
        product(normed_one, heads_whole, LOW, 3 * start, 3 * (end - start)) for start, end in spans
    ]
    triples[0], merge_line = together(triples[0], merge_line)
    merge_plane = gather_x(merge_line, fsdp_count)
    attended = []
    mixes = []
    for index, (start, end) in enumerate(spans):
        mixed, level = attend_forward(triples[index], end - start)
        if index == 0:
            mixed, merge_plane, branch_grad_blocks = together(mixed, merge_plane, branch_grad_blocks)
            merge_whole = arrange(gather_core(merge_plane, fsdp_count), fsdp_count, shard_rows)
        mixes.append((mixed, level))
        attended.append([shift_tp(mixed[k * own : (k + 1) * own], k, tp_count) for k in ring])
    attended_own = jnp.concatenate([part[k] for k in ring for part in attended], axis=1)
    attn_branch, after_attn, normed_two = merge_and_normalize(
        attended_own, latents, merge_whole, gate_one, shift_two, scale_two
    )
    normed_two_blocks = blocks_of_tokens(normed_two)

    fed = [feed_both(normed_two_blocks[0], branch_grad_blocks[0], feed_whole, FULL)]
    if tp_count > 1:
        fed, normed_two_blocks = together(fed, normed_two_blocks)
    fed += [feed_both(normed_two_blocks[k], branch_grad_blocks[k], feed_whole, LOW) for k in others]
    back_parts = [shift_tp(fed[k][1], k, tp_count) for k in others]
    (feed_grad,) = token_sum(
        [
            (normed_two_blocks, [fed[k][3] for k in ring]),
            (branch_grad_blocks, [fed[k][2] for k in ring]),
        ],
        fsdp_count,
        ordered=False,
    )
    branch_parts = [fed[k][0] for k in others]
    back_parts, branch_parts, feed_grad = together(back_parts, branch_parts, feed_grad)
    feed_sum = scatter_rows(feed_grad)
    branch_parts = [shift_tp(values, k, tp_count) for k, values in zip(others, branch_parts)]
    cuts = [(k * width + start, k * width + end) for k in ring for start, end in spans]
    after_grad, attn_grad, pieces, second_sums = second_back(
        fed[0][1], back_parts, after_attn, attn_branch, cotangent, merge_whole, gate_one, scale_two, cuts
    )
    attended_grads = [
        jnp.concatenate(
            [shift_tp(pieces[k * len(spans) + index], -k, tp_count) for k in ring], axis=0
        )
        for index in range(len(spans))
    ]
    triple_grads = [
        attend_backward(triples[0], *mixes[0], attended_grads[0], spans[0][1] - spans[0][0])
    ]
    triple_grads, branch_parts = together(triple_grads, branch_parts)
    pair = token_sum([([attn_grad], [attended_own]), ([normed_one], triple_grads)], fsdp_count)
    if len(spans) > 1:
        attended_grads, pair = together(attended_grads, pair)
    state = scatter_core(pair, fsdp_count)
    for index in range(1, len(spans)):
        start, end = spans[index]
        triple_grads.append(
            attend_backward(triples[index], *mixes[index], attended_grads[index], end - start)
        )
    triple_grads, state = together(triple_grads, state)
    parts = [product_back(triple_grads, heads_whole, LOW, own, k) for k in others]
    one_parts = [shift_tp(values, k, tp_count) for k, values in zip(others, parts)]
    state = scatter_x(state, fsdp_count)
    triple_grads, parts = together(triple_grads, parts)
    last = None
    if len(spans) > 1:
        pair = token_sum([([normed_one], triple_grads[1:])], fsdp_count)
        triple_grads, pair = together(triple_grads, pair)
        last = scatter_core(pair, fsdp_count)
    normed_one_grad = product_back(triple_grads, heads_whole, FULL, own, 0)
    block_out, last_sums = last_forward(fed[0][0], branch_parts, after_attn, cotangent, gate_two)
    up_new = adam_step(up_weight, up_first, up_second, feed_sum[:, :units].astype(FULL), 0.02)
    down_new = adam_step(down_weight, down_first, down_second, feed_sum[:, units:].T.astype(FULL), 0.01)
    one_parts, normed_one_grad, block_out, state, last, up_new, down_new = together(
        one_parts, normed_one_grad, block_out, state, last, up_new, down_new
    )
    if last:
        last = scatter_x(last, fsdp_count)
    latents_grad, first_sums = first_back(normed_one_grad, one_parts, latents, after_grad, scale_one)
    first_sums, last = together(first_sums, last)
    state = scatter_z(state, fsdp_count)
    if last:
        last = scatter_z(last, fsdp_count)
    modulation_all = modulation_shares(
        jnp.concatenate([first_sums[:2], second_sums[:3], last_sums[:1]], axis=0),
        tp_count,
        fsdp_count,
        part,
    )
    modulation_all, state, last = together(modulation_all, state, last)
    first_sum = scatter_end(state)
    merge_sum_all, heads_sums = first_sum[:, : tp_count * width], [first_sum[:, tp_count * width :]]
    if last:
        heads_sums.append(scatter_end(last))
    heads_sums = [total.reshape(shard_rows, 3, -1) for total in heads_sums]
    condition_sum = lax.dot_general(
        activated_rows.astype(FULL),
        modulation_all,
        TN,
        precision=lax.Precision.HIGHEST,
        preferred_element_type=FULL,
    ).reshape(shard_rows, 6, part)
    merge_sum = merge_sum_all[:, :width]
    for k in others:
        merge_sum = merge_sum + shift_tp(
            merge_sum_all[:, k * width : (k + 1) * width], -k, tp_count
        )
    heads_sum = jnp.moveaxis(jnp.concatenate(heads_sums, axis=2), 1, 0)
    cond_new = adam_step(condition_weight, condition_first, condition_second, condition_sum, 0.02)
    heads_new = adam_step(heads_weight, heads_first, heads_second, heads_sum, 0.02)
    merge_new = adam_step(merge_weight, merge_first, merge_second, merge_sum.T, 0.15)
    return (
        block_out.reshape(own, 1, depth),
        latents_grad.reshape(own, 1, depth),
        *cond_new,
        *heads_new,
        *merge_new,
        *up_new,
        *down_new,
    )


def solution(mesh):
    stream = P("tp", "fsdp", None)
    cond = P("fsdp", None, "tp")
    heads = P(None, "fsdp", "tp")
    wide = P("tp", "fsdp")
    tall = P("fsdp", "tp")
    in_specs = (stream, P("fsdp", None), stream) + (cond,) * 3 + (heads,) * 3 + (wide,) * 3 + (tall,) * 3 + (wide,) * 3
    out_specs = (stream, stream) + (cond,) * 3 + (heads,) * 3 + (wide,) * 3 + (tall,) * 3 + (wide,) * 3
    return jax.shard_map(
        functools.partial(local, mesh.shape["fsdp"], mesh.shape["tp"]),
        mesh=mesh,
        in_specs=in_specs,
        out_specs=out_specs,
        check_vma=False,
    )
```

```python
import functools

import jax
import jax.numpy as jnp
from jax import lax
from jax.experimental import pallas as pl
from jax.experimental.pallas import tpu as pltpu
from jax.sharding import PartitionSpec as P

HEAD = 64
PAIR = 2 * HEAD
STEP = 5
LOW = jnp.bfloat16
FULL = jnp.float32
NT = (((1,), (1,)), ((), ()))
TN = (((0,), (0,)), ((), ()))


def params(limit=56):
    return pltpu.CompilerParams(vmem_limit_bytes=limit * 1024 * 1024)


def cost(flops, moved, raised=0):
    return pl.CostEstimate(flops=int(flops), bytes_accessed=int(moved), transcendentals=int(raised))


def resident(shape):
    return pl.BlockSpec(shape, lambda *step: (0,) * len(shape))


def fit(width, most):
    return next(tile for tile in (most, 512, 256, PAIR) if tile <= most and width % tile == 0)


def product(left, right, out_type):
    rows, depth = left.shape
    width = right.shape[1]
    tile = fit(width, 512)

    def body(left_ref, right_ref, out_ref):
        out_ref[...] = jnp.dot(
            left_ref[...], right_ref[...], preferred_element_type=FULL
        ).astype(out_type)

    return pl.pallas_call(
        body,
        grid=(width // tile,),
        in_specs=[
            resident((rows, depth)),
            pl.BlockSpec((depth, tile), lambda j: (0, j)),
        ],
        out_specs=pl.BlockSpec((rows, tile), lambda j: (0, j)),
        out_shape=jax.ShapeDtypeStruct((rows, width), out_type),
        compiler_params=params(),
        cost_estimate=cost(2 * rows * depth * width, 2 * (rows * depth + depth * width) + 4 * rows * width),
        name="product",
    )(left, right)


def product_back(lefts, right, out_type, rows, part):
    width, depth = right.shape
    tile = min(256, width)

    def body(*refs):
        total = None
        start = 0
        for left_ref in refs[:-2]:
            extent = left_ref.shape[1]
            term = lax.dot_general(
                left_ref[...], refs[-2][:, start : start + extent], NT, preferred_element_type=FULL
            )
            total = term if total is None else total + term
            start += extent
        refs[-1][...] = total.astype(out_type)

    return pl.pallas_call(
        body,
        grid=(width // tile,),
        in_specs=[pl.BlockSpec((rows, left.shape[1]), lambda j: (part, 0)) for left in lefts]
        + [pl.BlockSpec((tile, depth), lambda j: (j, 0))],
        out_specs=pl.BlockSpec((rows, tile), lambda j: (0, j)),
        out_shape=jax.ShapeDtypeStruct((rows, width), out_type),
        compiler_params=params(),
        cost_estimate=cost(2 * rows * depth * width, 2 * (rows * depth + width * depth) + 4 * rows * width),
        name="product_back",
    )(*lefts, right)


def token_sum(jobs, count, ordered=True):
    depth = jobs[0][0][0].shape[1]
    widths = [rights[0].shape[1] for _, rights in jobs]
    width = sum(widths)
    tokens = max(sum(left.shape[0] for left in lefts) for lefts, _ in jobs)
    tile = min(fit(extent, 512) for extent in widths)
    deep, across, cores = digits(count)
    group = depth // count
    pieces = len(jobs[0][0])
    starts = [sum(widths[:index]) // tile for index in range(len(jobs) + 1)]

    def flip(left_refs, turned):
        me = lax.axis_index("fsdp")
        my_z, my_x, my_c = me // (across * cores), (me // cores) % across, me % cores
        start = 0
        for left_ref in left_refs:
            flipped = left_ref[...].T
            extent = left_ref.shape[0]
            if not ordered:
                turned[:, start : start + extent] = flipped
            for source in range(count if ordered else 0):
                z, x, c = source // (across * cores), (source // cores) % across, source % cores
                place = (
                    ((c - my_c + cores) % cores) * across + (x - my_x + across) % across
                ) * deep + (z - my_z + deep) % deep
                turned[pl.ds(pl.multiple_of(place * group, group), group), start : start + extent] = (
                    flipped[source * group : (source + 1) * group]
                )
            start += extent

    def body(*refs):
        out_refs, turned = refs[2 * pieces * len(jobs) : -1], refs[-1]
        step = pl.program_id(0)
        for index in range(len(jobs)):
            mine = refs[2 * pieces * index : 2 * pieces * (index + 1)]

            @pl.when(step == starts[index])
            def _():
                flip(mine[:pieces], turned)

            @pl.when((step >= starts[index]) & (step < starts[index + 1]))
            def _():
                total = None
                start = 0
                for right_ref in mine[pieces:]:
                    extent = right_ref.shape[0]
                    term = jnp.dot(
                        turned[:, start : start + extent], right_ref[...], preferred_element_type=FULL
                    )
                    total = term if total is None else total + term
                    start += extent
                total = total.astype(LOW)
                start = 0
                for out_ref in out_refs:
                    out_ref[...] = total[start : start + out_ref.shape[0]]
                    start += out_ref.shape[0]

    def place_of(index):
        last = widths[index] // tile - 1
        return lambda j: (0, jnp.clip(j - starts[index], 0, last))

    half = depth // cores
    heights = (half, depth - half) if ordered else (depth,)
    in_specs = []
    operands = []
    for index, (lefts, rights) in enumerate(jobs):
        in_specs += [resident(left.shape) for left in lefts]
        in_specs += [pl.BlockSpec((right.shape[0], tile), place_of(index)) for right in rights]
        operands += [*lefts, *rights]
    return pl.pallas_call(
        body,
        grid=(width // tile,),
        in_specs=in_specs,
        out_specs=[pl.BlockSpec((height, tile), lambda j: (0, j)) for height in heights],
        out_shape=[jax.ShapeDtypeStruct((height, width), LOW) for height in heights],
        scratch_shapes=[pltpu.VMEM((depth, tokens), LOW)],
        compiler_params=params(),
        cost_estimate=cost(
            2 * depth * tokens * width, 2 * (len(jobs) * depth * tokens + tokens * width + depth * width)
        ),
        name="token_sum",
    )(*operands)


def head_lanes():
    lane = lax.broadcasted_iota(jnp.int32, (1, PAIR), 1)
    first = (lane < HEAD).astype(FULL)
    return lane, ((first, HEAD), (1.0 - first, 0))


def in_lanes(lane, free, column):
    total = 0.0
    for index in range(3):
        piece = column.astype(LOW).astype(FULL)
        total = total + jnp.where(lane == free + index, piece, 0.0)
        column = column - piece
    return total


def ones_in_lanes(lane, free, values):
    return jnp.where((lane >= free) & (lane < free + 3), 1.0, values.astype(FULL)).astype(LOW)


def attend_forward(triple, start, width):
    tokens = triple.shape[0]
    pairs = width // PAIR
    first = start // PAIR
    block = min(512, tokens)
    scaling = HEAD ** (-0.5)

    def body(query_ref, keys_ref, values_ref, out_ref, level_ref):
        lane, heads = head_lanes()
        keys = keys_ref[...]
        values = values_ref[...].astype(FULL)
        query = query_ref[...].astype(FULL)
        total = level = 0.0
        for mask, free in heads:
            scores = lax.dot_general(
                (query * (mask * scaling)).astype(LOW), keys, NT, preferred_element_type=FULL
            )
            peak = jnp.max(scores, axis=-1, keepdims=True)
            raised = jnp.exp(scores - peak).astype(LOW)
            counted = jnp.where(lane == free, 1.0, values * mask).astype(LOW)
            mixed = jnp.dot(raised, counted, preferred_element_type=FULL)
            sums = mixed[:, free : free + 1]
            total = total + mixed * mask / sums
            level = level + mask * (peak + jnp.log(sums))
        out_ref[...] = total.astype(LOW)
        level_ref[...] = level

    return pl.pallas_call(
        body,
        grid=(pairs, tokens // block),
        in_specs=[
            pl.BlockSpec((block, PAIR), lambda h, i: (i, first + h)),
            pl.BlockSpec((tokens, PAIR), lambda h, i: (0, first + pairs + h)),
            pl.BlockSpec((tokens, PAIR), lambda h, i: (0, first + 2 * pairs + h)),
        ],
        out_specs=[pl.BlockSpec((block, PAIR), lambda h, i: (i, h))] * 2,
        out_shape=[
            jax.ShapeDtypeStruct((tokens, width), LOW),
            jax.ShapeDtypeStruct((tokens, width), FULL),
        ],
        compiler_params=params(),
        cost_estimate=cost(16 * tokens * tokens * width, 12 * tokens * width, tokens * tokens * width // HEAD),
        name="attend_forward",
    )(triple, triple, triple)


def attend_backward(triple, start, attended, level, grads, width):
    tokens = triple.shape[0]
    pairs = width // PAIR
    first = start // PAIR
    block = min(512, tokens)
    steps = tokens // block
    scaling = HEAD ** (-0.5)

    def body(query_ref, keys_ref, values_ref, out_low_ref, level_ref, grad_ref, out_ref, key_sum, value_sum):
        pair = pl.program_id(0)
        step = pl.program_id(1)
        lane, heads = head_lanes()
        keys = keys_ref[...]
        values = values_ref[...]
        query = query_ref[...].astype(FULL)
        grad = grad_ref[...].astype(FULL)
        inner = grad * out_low_ref[...].astype(FULL)
        query_grad = key_grad = value_grad = None
        for index, (mask, free) in enumerate(heads):
            own = HEAD * index
            query_part = query * (mask * scaling)
            grad_part = grad * mask
            probs = jnp.exp(
                lax.dot_general(
                    ones_in_lanes(lane, free, keys),
                    (query_part - in_lanes(lane, free, level_ref[:, own : own + 1])).astype(LOW),
                    NT,
                    preferred_element_type=FULL,
                )
            )
            prob_grad = lax.dot_general(
                ones_in_lanes(lane, free, values),
                (
                    grad_part - in_lanes(lane, free, jnp.sum(inner * mask, axis=-1, keepdims=True))
                ).astype(LOW),
                NT,
                preferred_element_type=FULL,
            )
            score_grad = (probs * prob_grad).astype(LOW)
            value_part = jnp.dot(probs.astype(LOW), grad_part.astype(LOW), preferred_element_type=FULL)
            key_part = jnp.dot(score_grad, query_part.astype(LOW), preferred_element_type=FULL)
            asked_part = lax.dot_general(
                score_grad, keys * (mask * scaling).astype(LOW), TN, preferred_element_type=FULL
            )
            if query_grad is None:
                query_grad, key_grad, value_grad = asked_part, key_part, value_part
            else:
                query_grad, key_grad, value_grad = (
                    query_grad + asked_part,
                    key_grad + key_part,
                    value_grad + value_part,
                )

        @pl.when(step == 0)
        def _():
            key_sum[...] = key_grad
            value_sum[...] = value_grad

        @pl.when(step > 0)
        def _():
            key_sum[...] += key_grad
            value_sum[...] += value_grad

        rows = pl.ds(pl.multiple_of(step * block, block), block)
        out_ref[rows, pl.ds(pl.multiple_of(pair * PAIR, PAIR), PAIR)] = query_grad.astype(LOW)

        @pl.when(step == steps - 1)
        def _():
            out_ref[:, pl.ds(pl.multiple_of(width + pair * PAIR, PAIR), PAIR)] = key_sum[...].astype(LOW)
            out_ref[:, pl.ds(pl.multiple_of(2 * width + pair * PAIR, PAIR), PAIR)] = value_sum[
                ...
            ].astype(LOW)

    rows_of_pair = pl.BlockSpec((block, PAIR), lambda h, i: (i, h))
    return pl.pallas_call(
        body,
        grid=(pairs, steps),
        in_specs=[
            pl.BlockSpec((block, PAIR), lambda h, i: (i, first + h)),
            pl.BlockSpec((tokens, PAIR), lambda h, i: (0, first + pairs + h)),
            pl.BlockSpec((tokens, PAIR), lambda h, i: (0, first + 2 * pairs + h)),
            rows_of_pair,
            rows_of_pair,
            rows_of_pair,
        ],
        out_specs=resident((tokens, 3 * width)),
        out_shape=jax.ShapeDtypeStruct((tokens, 3 * width), LOW),
        scratch_shapes=[pltpu.VMEM((tokens, PAIR), FULL), pltpu.VMEM((tokens, PAIR), FULL)],
        compiler_params=params(),
        cost_estimate=cost(40 * tokens * tokens * width, 20 * tokens * width, tokens * tokens * width // HEAD),
        name="attend_backward",
    )(triple, triple, triple, attended, level, grads)


def feed_both(normed, branch_grad, weights, out_type):
    tokens, depth = normed.shape
    units = weights.shape[1] // 2
    tile = min(512, units)
    steps = units // tile

    def body(normed_ref, grad_ref, up_ref, down_ref, out_ref, back_ref, hidden_ref, pre_ref, out_sum, back_sum):
        step = pl.program_id(0)
        up = up_ref[...]
        down = down_ref[...]
        pre = jnp.dot(normed_ref[...], up, preferred_element_type=FULL)
        hidden_grad = jnp.dot(grad_ref[...], down, preferred_element_type=FULL)
        square = pre * pre
        bent = jnp.tanh(0.7978845608028654 * (pre + 0.044715 * (square * pre)))
        half = 0.5 * (1.0 + bent)
        hidden = (pre * half).astype(LOW)
        slope = half + 0.5 * pre * (1.0 - bent * bent) * (
            0.7978845608028654 * (1.0 + 0.134145 * square)
        )
        pre_grad = (hidden_grad * slope).astype(LOW)
        hidden_ref[...] = hidden
        pre_ref[...] = pre_grad
        out_part = lax.dot_general(hidden, down, NT, preferred_element_type=FULL)
        back_part = lax.dot_general(pre_grad, up, NT, preferred_element_type=FULL)

        @pl.when(step == 0)
        def _():
            out_sum[...] = out_part
            back_sum[...] = back_part

        @pl.when(step > 0)
        def _():
            out_sum[...] += out_part
            back_sum[...] += back_part

        @pl.when(step == steps - 1)
        def _():
            out_ref[...] = out_sum[...].astype(out_type)
            back_ref[...] = back_sum[...].astype(out_type)

    return pl.pallas_call(
        body,
        grid=(steps,),
        in_specs=[
            resident((tokens, depth)),
            resident((tokens, depth)),
            pl.BlockSpec((depth, tile), lambda j: (0, j)),
            pl.BlockSpec((depth, tile), lambda j: (0, steps + j)),
        ],
        out_specs=[
            resident((tokens, depth)),
            resident((tokens, depth)),
            pl.BlockSpec((tokens, tile), lambda j: (0, j)),
            pl.BlockSpec((tokens, tile), lambda j: (0, j)),
        ],
        out_shape=[
            jax.ShapeDtypeStruct((tokens, depth), out_type),
            jax.ShapeDtypeStruct((tokens, depth), out_type),
            jax.ShapeDtypeStruct((tokens, units), LOW),
            jax.ShapeDtypeStruct((tokens, units), LOW),
        ],
        scratch_shapes=[pltpu.VMEM((tokens, depth), FULL), pltpu.VMEM((tokens, depth), FULL)],
        compiler_params=params(),
        cost_estimate=cost(8 * tokens * depth * units, 4 * depth * units + 12 * tokens * depth + 4 * tokens * units, tokens * units),
        name="feed_both",
    )(normed, branch_grad, weights, weights)


def standardize(values):
    middle = jnp.mean(values, axis=-1, keepdims=True)
    centred = values - middle
    spread = jnp.mean(centred * centred, axis=-1, keepdims=True)
    rate = lax.rsqrt(spread + 1e-06)
    return centred * rate, rate


def standardize_back(grad, values, scale_term):
    unit, rate = standardize(values)
    pulled = grad * (1.0 + scale_term)
    resid = rate * (
        pulled
        - jnp.mean(pulled, axis=-1, keepdims=True)
        - unit * jnp.mean(pulled * unit, axis=-1, keepdims=True)
    )
    return resid, jnp.sum(grad, axis=0, keepdims=True), jnp.sum(grad * unit, axis=0, keepdims=True)


def store_sums(sums_ref, rows):
    @pl.when(pl.program_id(0) == 0)
    def _():
        sums_ref[...] = jnp.zeros_like(sums_ref)

    for index, row in enumerate(rows):
        sums_ref[index : index + 1, :] += row


def store_lines(out_ref, values):
    for index in range(out_ref.shape[1]):
        out_ref[:, index, :] = values[:, index * PAIR : (index + 1) * PAIR]


def by_tokens(body, arrays, wholes, outs, sums, flops, name):
    tokens = arrays[0].shape[0]
    block = min(256, tokens)

    def cut(shape):
        return pl.BlockSpec((block,) + shape[1:], lambda j: (j,) + (0,) * (len(shape) - 1))

    out_specs = [cut(shape) for shape, _ in outs]
    out_shape = [jax.ShapeDtypeStruct(shape, kind) for shape, kind in outs]
    if sums:
        out_specs.append(resident((8, sums)))
        out_shape.append(jax.ShapeDtypeStruct((8, sums), FULL))
    moved = sum(value.size * value.dtype.itemsize for value in list(arrays) + list(wholes) + out_shape)
    return pl.pallas_call(
        body,
        grid=(tokens // block,),
        in_specs=[cut(value.shape) for value in arrays] + [resident(value.shape) for value in wholes],
        out_specs=out_specs,
        out_shape=out_shape,
        compiler_params=params(),
        cost_estimate=cost(flops, moved),
        name=name,
    )(*arrays, *wholes)


def merge_and_normalize(attended, latents, merge, gate, shift, scale):
    tokens, depth = latents.shape

    def body(attended_ref, latents_ref, merge_ref, gate_ref, shift_ref, scale_ref, branch_ref, after_ref, normed_ref):
        branch = lax.dot_general(attended_ref[...], merge_ref[...], NT, preferred_element_type=FULL)
        after = latents_ref[...] + gate_ref[...] * branch
        branch_ref[...] = branch
        after_ref[...] = after
        normed_ref[...] = (
            standardize(after)[0] * (1.0 + scale_ref[...]) + shift_ref[...]
        ).astype(LOW)

    shape = (tokens, depth)
    return by_tokens(
        body,
        [attended, latents],
        [merge, gate, shift, scale],
        [(shape, FULL), (shape, FULL), (shape, LOW)],
        0,
        2 * tokens * depth * merge.shape[1],
        "merge_and_normalize",
    )


def second_back(grad, parts, after, branch, cotangent, merge, gate, scale, spans):
    tokens, depth = after.shape
    count = len(parts)

    def body(*refs):
        total = refs[0][...]
        for part_ref in refs[1 : 1 + count]:
            total = total + part_ref[...].astype(FULL)
        after_ref, branch_ref, cotangent_ref, merge_ref, gate_ref, scale_ref = refs[1 + count : 7 + count]
        grad_ref, low_ref = refs[7 + count : 9 + count]
        piece_refs, sums_ref = refs[9 + count : -1], refs[-1]
        resid, shift_grad, scale_grad = standardize_back(total, after_ref[...], scale_ref[...])
        after_grad = cotangent_ref[...] + resid
        low = (gate_ref[...] * after_grad).astype(LOW)
        grad_ref[...] = after_grad
        low_ref[...] = low
        back = jnp.dot(low, merge_ref[...], preferred_element_type=FULL).astype(LOW)
        for piece_ref, (start, end) in zip(piece_refs, spans):
            piece_ref[...] = back[:, start:end]
        store_sums(
            sums_ref,
            [jnp.sum(after_grad * branch_ref[...], axis=0, keepdims=True), shift_grad, scale_grad],
        )

    outs = [((tokens, depth), FULL), ((tokens, depth), LOW)]
    outs += [((tokens, end - start), LOW) for start, end in spans]
    results = by_tokens(
        body,
        [grad, *parts, after, branch, cotangent],
        [merge, gate, scale],
        outs,
        depth,
        2 * tokens * depth * merge.shape[1],
        "second_back",
    )
    return results[0], results[1], results[2:-1], results[-1]


def first_back(grad, parts, latents, after_grad, scale):
    tokens, depth = latents.shape
    count = len(parts)

    def body(*refs):
        total = refs[0][...]
        for part_ref in refs[1 : 1 + count]:
            total = total + part_ref[...].astype(FULL)
        latents_ref, after_ref, scale_ref, out_ref, sums_ref = refs[1 + count :]
        resid, shift_grad, scale_grad = standardize_back(total, latents_ref[...], scale_ref[...])
        store_lines(out_ref, after_ref[...] + resid)
        store_sums(sums_ref, [shift_grad, scale_grad])

    return by_tokens(
        body,
        [grad, *parts, latents, after_grad],
        [scale],
        [((tokens, depth // PAIR, PAIR), FULL)],
        depth,
        20 * tokens * depth,
        "first_back",
    )


def last_forward(branch, parts, after, cotangent, gate):
    tokens, depth = after.shape
    count = len(parts)

    def body(*refs):
        total = refs[0][...]
        for part_ref in refs[1 : 1 + count]:
            total = total + part_ref[...].astype(FULL)
        after_ref, cotangent_ref, gate_ref, out_ref, sums_ref = refs[1 + count :]
        store_lines(out_ref, after_ref[...] + gate_ref[...] * total)
        store_sums(sums_ref, [jnp.sum(cotangent_ref[...] * total, axis=0, keepdims=True)])

    return by_tokens(
        body,
        [branch, *parts, after, cotangent],
        [gate],
        [((tokens, depth // PAIR, PAIR), FULL)],
        depth,
        6 * tokens * depth,
        "last_forward",
    )


def adam_step(weight, first, second, grad_sum, rate):
    first_new = 0.9 * first + 0.1 * grad_sum
    second_new = 0.999 * second + 0.001 * grad_sum * grad_sum
    first_hat = first_new / (1.0 - 0.9**STEP)
    second_hat = second_new / (1.0 - 0.999**STEP)
    weight_new = weight - rate * (first_hat / (jnp.sqrt(second_hat) + 1e-08) + 0.01 * weight)
    return (weight_new, first_new, second_new)


def shift_tp(values, steps, count):
    steps = steps % count
    if steps == 0:
        return values
    return lax.ppermute(values, "tp", [(i, (i + steps) % count) for i in range(count)])


def digits(count):
    if count % 8 == 0:
        return 4, count // 8, 2
    return count // 2, 1, 2


def shift_fsdp(values, digit, steps, count):
    sizes = digits(count)
    scale = (sizes[1] * sizes[2], sizes[2], 1)[digit]
    size = sizes[digit]
    pairs = []
    for source in range(count):
        own = (source // scale) % size
        pairs.append((source, source + ((own + steps) % size - own) * scale))
    return lax.ppermute(values, "fsdp", pairs)


def arrange(pieces, count, group, by_z):
    deep, across, cores = digits(count)
    width = pieces[0].shape[1]
    tile = fit(width, 512)
    outer, inner = (deep, across) if by_z else (across, deep)

    def body(*refs):
        out_ref = refs[-1]
        me = lax.axis_index("fsdp")
        my_z, my_x, my_c = me // (across * cores), (me // cores) % across, me % cores
        for core in range(cores):
            for first in range(outer):
                source = refs[core * outer + first]
                for second in range(inner):
                    z, x = (first, second) if by_z else (second, first)
                    place = (
                        ((my_z - z + deep) % deep) * across + (my_x - x + across) % across
                    ) * cores + (my_c - core + cores) % cores
                    out_ref[pl.ds(pl.multiple_of(place * group, group), group), :] = source[
                        second * group : (second + 1) * group, :
                    ]

    return pl.pallas_call(
        body,
        grid=(width // tile,),
        in_specs=[pl.BlockSpec((piece.shape[0], tile), lambda j: (0, j)) for piece in pieces],
        out_specs=pl.BlockSpec((count * group, tile), lambda j: (0, j)),
        out_shape=jax.ShapeDtypeStruct((count * group, width), LOW),
        compiler_params=params(),
        cost_estimate=cost(0, 4 * count * group * width),
        name="arrange",
    )(*pieces)


def gather_z(shard, count):
    deep = digits(count)[0]
    return [shard] + [shift_fsdp(shard, 0, k, count) for k in range(1, deep)]


def gather_x(line, count):
    across = digits(count)[1]
    line = jnp.concatenate(line, axis=0)
    return [line] + [shift_fsdp(line, 1, k, count) for k in range(1, across)]


def gather_core(plane, count):
    cores = digits(count)[2]
    return plane + [shift_fsdp(piece, 2, k, count) for k in range(1, cores) for piece in plane]


def scatter_core(pair, count):
    kept, sent = pair
    return kept, shift_fsdp(sent, 2, 1, count)


def scatter_x(pair, count):
    kept, came = pair
    across = digits(count)[1]
    rows = kept.shape[0] // across

    def both(x):
        part = slice(x * rows, (x + 1) * rows)
        return kept[part].astype(FULL) + came[part].astype(FULL)

    return kept[:rows], came[:rows], [
        shift_fsdp(both(k).astype(LOW), 1, k, count) for k in range(1, across)
    ]


def scatter_z(state, count):
    kept, came, parts = state
    deep = digits(count)[0]
    group = kept.shape[0] // deep

    def both(z):
        rows = slice(z * group, (z + 1) * group)
        return sum(
            (part[rows].astype(FULL) for part in [came] + parts), start=kept[rows].astype(FULL)
        )

    return both(0), [shift_fsdp(both(k).astype(LOW), 0, k, count) for k in range(1, deep)]


def scatter_end(state):
    own, parts = state
    return sum((part.astype(FULL) for part in parts), start=own)


def gather_rows(shard):
    return lax.all_gather(shard, "fsdp", axis=0, tiled=True)


def scatter_rows(whole):
    return lax.psum_scatter(whole, "fsdp", scatter_dimension=0, tiled=True)


def together(*values):
    return lax.optimization_barrier(values)


def modulation_shares(grads, tp_count, fsdp_count, part):
    count = grads.shape[0]
    place = lax.axis_index("tp")
    total = sum(
        shift_tp(
            lax.dynamic_slice_in_dim(grads, (place + k) % tp_count * part, part, axis=1), k, tp_count
        )
        for k in range(tp_count)
    )
    every = lax.all_to_all(
        jnp.broadcast_to(total.reshape(1, count * part), (fsdp_count, count * part)),
        "fsdp",
        split_axis=0,
        concat_axis=0,
        tiled=True,
    )
    return every


def local(
    fsdp_count,
    tp_count,
    latents_in,
    condition,
    out_grad,
    condition_weight,
    condition_first,
    condition_second,
    heads_weight,
    heads_first,
    heads_second,
    merge_weight,
    merge_first,
    merge_second,
    up_weight,
    up_first,
    up_second,
    down_weight,
    down_first,
    down_second,
):
    own, _, depth = latents_in.shape
    shard_rows = condition_weight.shape[0]
    part = condition_weight.shape[2]
    width = heads_weight.shape[2]
    units = up_weight.shape[1]
    ring = range(tp_count)
    others = range(1, tp_count)

    def blocks_of_tokens(values):
        return [shift_tp(values, -k, tp_count) for k in ring]

    pairs = width // PAIR
    spans = [(0, pairs // 2), (pairs // 2, pairs)] if pairs > 1 else [(0, pairs)]
    spans = [(start * PAIR, end * PAIR) for start, end in spans]

    heads_low = jnp.moveaxis(heads_weight.astype(LOW), 0, 1)
    heads_shard = jnp.concatenate(
        [heads_low[:, :, start:end].reshape(shard_rows, -1) for start, end in spans], axis=1
    )
    activated = jax.nn.silu(condition).astype(LOW)
    activated, heads_shard = together(activated, heads_shard)
    heads_whole = gather_rows(heads_shard)
    activated_rows = lax.all_to_all(
        activated.reshape(fsdp_count, shard_rows), "fsdp", split_axis=0, concat_axis=0, tiled=True
    )
    latents, _ = together(latents_in.reshape(own, depth), heads_shard)
    (cotangent,) = together(out_grad.reshape(own, depth))

    unit_one, _ = standardize(latents)
    unit_blocks = blocks_of_tokens(unit_one.astype(LOW))
    shares = jnp.dot(
        activated_rows,
        condition_weight.astype(LOW).reshape(shard_rows, 6 * part),
        preferred_element_type=FULL,
    )
    shares = lax.all_to_all(shares, "fsdp", split_axis=0, concat_axis=0, tiled=True)
    feed_shard = jnp.concatenate([up_weight.astype(LOW), down_weight.astype(LOW).T], axis=1)
    shares, unit_blocks, cotangent = together(shares, unit_blocks, cotangent)
    modulation_part = jnp.sum(shares, axis=0).reshape(6, part)
    modulation = lax.all_gather(modulation_part, "tp", axis=1, tiled=True)
    modulation, merge_shard = together(modulation, merge_weight.astype(LOW).T)
    merge_shard = jnp.concatenate([shift_tp(merge_shard, k, tp_count) for k in ring], axis=1)
    merge_line = gather_z(merge_shard, fsdp_count)
    shift_one, scale_one, gate_one, shift_two, scale_two, gate_two = (
        modulation[k : k + 1] for k in range(6)
    )

    branch_grad = (gate_two * cotangent).astype(LOW)
    branch_grad_blocks = blocks_of_tokens(branch_grad)

    normed_one = jnp.concatenate(
        [
            ((unit_one if k == 0 else unit_blocks[k].astype(FULL)) * (1.0 + scale_one) + shift_one).astype(LOW)
            for k in ring
        ],
        axis=0,
    )
    heads_whole, feed_shard, normed_one, merge_line = together(
        heads_whole, feed_shard, normed_one, merge_line
    )
    feed_whole = gather_rows(feed_shard)
    triple = product(normed_one, heads_whole, LOW)
    triple, merge_line = together(triple, merge_line)
    merge_plane = gather_x(merge_line, fsdp_count)
    attended = []
    mixes = []
    for index, (start, end) in enumerate(spans):
        mixed, level = attend_forward(triple, 3 * start, end - start)
        if index == 0:
            mixed, merge_plane, branch_grad_blocks = together(mixed, merge_plane, branch_grad_blocks)
            merge_whole = arrange(gather_core(merge_plane, fsdp_count), fsdp_count, shard_rows, False)
        mixes.append((mixed, level))
        attended.append([shift_tp(mixed[k * own : (k + 1) * own], k, tp_count) for k in ring])
    attended_own = jnp.concatenate([part[k] for k in ring for part in attended], axis=1)
    attn_branch, after_attn, normed_two = merge_and_normalize(
        attended_own, latents, merge_whole, gate_one, shift_two, scale_two
    )
    normed_two_blocks = blocks_of_tokens(normed_two)

    fed = [None] + [feed_both(normed_two_blocks[k], branch_grad_blocks[k], feed_whole, LOW) for k in others]
    back_parts = [shift_tp(fed[k][1], k, tp_count) for k in others]
    normed_two, fed = together(normed_two, fed)
    fed[0] = feed_both(normed_two, branch_grad, feed_whole, FULL)
    fed, branch_parts = together(fed, [fed[k][0] for k in others])
    branch_parts = [shift_tp(values, k, tp_count) for k, values in zip(others, branch_parts)]
    (feed_grad,) = token_sum(
        [
            (normed_two_blocks, [fed[k][3] for k in ring]),
            (branch_grad_blocks, [fed[k][2] for k in ring]),
        ],
        fsdp_count,
        ordered=False,
    )
    back_parts, feed_grad = together(back_parts, feed_grad)
    feed_sum = scatter_rows(feed_grad)
    cuts = [(k * width + start, k * width + end) for k in ring for start, end in spans]
    after_grad, attn_grad, pieces, second_sums = second_back(
        fed[0][1], back_parts, after_attn, attn_branch, cotangent, merge_whole, gate_one, scale_two, cuts
    )
    attended_grads = []
    for index in range(len(spans)):
        mine = pieces[index :: len(spans)]
        if index:
            attended_grads, mine = together(attended_grads, mine)
        attended_grads.append(
            jnp.concatenate([shift_tp(mine[k], -k, tp_count) for k in ring], axis=0)
        )
    triple_grads = [
        attend_backward(triple, 0, *mixes[0], attended_grads[0], spans[0][1])
    ]
    triple_grads, branch_parts, attended_grads = together(triple_grads, branch_parts, attended_grads)
    pair = token_sum([([attn_grad], [attended_own]), ([normed_one], triple_grads)], fsdp_count)
    state = scatter_core(pair, fsdp_count)
    block_out, last_sums = last_forward(fed[0][0], branch_parts, after_attn, cotangent, gate_two)
    attended_grads, state, block_out = together(attended_grads, state, block_out)
    state = scatter_x(state, fsdp_count)
    for index in range(1, len(spans)):
        start, end = spans[index]
        triple_grads.append(
            attend_backward(triple, 3 * start, *mixes[index], attended_grads[index], end - start)
        )
    parts = [product_back(triple_grads, heads_whole, LOW, own, k) for k in others]
    one_parts = [shift_tp(values, k, tp_count) for k, values in zip(others, parts)]
    triple_grads, parts = together(triple_grads, parts)
    last = None
    if len(spans) > 1:
        last = token_sum([([normed_one], triple_grads[1:])], fsdp_count)
    triple_grads, last, state = together(triple_grads, last, state)
    state = scatter_z(state, fsdp_count)
    if last:
        last = scatter_core(last, fsdp_count)
    normed_one_grad = product_back(triple_grads, heads_whole, FULL, own, 0)
    one_parts, normed_one_grad, last = together(one_parts, normed_one_grad, last)
    if last:
        last = scatter_x(last, fsdp_count)
    latents_grad, first_sums = first_back(normed_one_grad, one_parts, latents, after_grad, scale_one)
    first_sums, last, feed_sum = together(first_sums, last, feed_sum)
    if last:
        last = scatter_z(last, fsdp_count)
    up_new = adam_step(up_weight, up_first, up_second, feed_sum[:, :units].astype(FULL), 0.02)
    down_new = adam_step(down_weight, down_first, down_second, feed_sum[:, units:].T.astype(FULL), 0.01)
    modulation_all = modulation_shares(
        jnp.concatenate([first_sums[:2], second_sums[:3], last_sums[:1]], axis=0),
        tp_count,
        fsdp_count,
        part,
    )
    modulation_all, state, last = together(modulation_all, state, last)
    first_sum = scatter_end(state)
    merge_sum_all, heads_sums = first_sum[:, : tp_count * width], [first_sum[:, tp_count * width :]]
    if last:
        heads_sums.append(scatter_end(last))
    heads_sums = [total.reshape(shard_rows, 3, -1) for total in heads_sums]
    condition_sum = lax.dot_general(
        activated_rows.astype(FULL),
        modulation_all,
        TN,
        precision=lax.Precision.HIGHEST,
        preferred_element_type=FULL,
    ).reshape(shard_rows, 6, part)
    merge_sum = merge_sum_all[:, :width]
    for k in others:
        merge_sum = merge_sum + shift_tp(
            merge_sum_all[:, k * width : (k + 1) * width], -k, tp_count
        )
    heads_sum = jnp.moveaxis(jnp.concatenate(heads_sums, axis=2), 1, 0)
    cond_new = adam_step(condition_weight, condition_first, condition_second, condition_sum, 0.02)
    heads_new = adam_step(heads_weight, heads_first, heads_second, heads_sum, 0.02)
    merge_new = adam_step(merge_weight, merge_first, merge_second, merge_sum.T, 0.15)
    return (
        block_out.reshape(own, 1, depth),
        latents_grad.reshape(own, 1, depth),
        *cond_new,
        *heads_new,
        *merge_new,
        *up_new,
        *down_new,
    )


def solution(mesh):
    stream = P("tp", "fsdp", None)
    cond = P("fsdp", None, "tp")
    heads = P(None, "fsdp", "tp")
    wide = P("tp", "fsdp")
    tall = P("fsdp", "tp")
    in_specs = (stream, P("fsdp", None), stream) + (cond,) * 3 + (heads,) * 3 + (wide,) * 3 + (tall,) * 3 + (wide,) * 3
    out_specs = (stream, stream) + (cond,) * 3 + (heads,) * 3 + (wide,) * 3 + (tall,) * 3 + (wide,) * 3
    return jax.shard_map(
        functools.partial(local, mesh.shape["fsdp"], mesh.shape["tp"]),
        mesh=mesh,
        in_specs=in_specs,
        out_specs=out_specs,
        check_vma=False,
    )
```

```python
import functools

import jax
import jax.numpy as jnp
from jax import lax
from jax.experimental import pallas as pl
from jax.experimental.pallas import tpu as pltpu
from jax.sharding import PartitionSpec as P

HEAD = 64
PAIR = 2 * HEAD
STEP = 5
LOW = jnp.bfloat16
FULL = jnp.float32
NT = (((1,), (1,)), ((), ()))
TN = (((0,), (0,)), ((), ()))


def params(limit=56):
    return pltpu.CompilerParams(vmem_limit_bytes=limit * 1024 * 1024)


def cost(flops, moved, raised=0):
    return pl.CostEstimate(
        flops=int(flops) // 4, bytes_accessed=int(moved) // 4, transcendentals=int(raised) // 4
    )


def resident(shape):
    return pl.BlockSpec(shape, lambda *step: (0,) * len(shape))


def fit(width, most):
    return next(tile for tile in (most, 512, 256, PAIR) if tile <= most and width % tile == 0)


def product(left, right, out_type):
    rows, depth = left.shape
    width = right.shape[1]
    tile = fit(width, 512)

    def body(left_ref, right_ref, out_ref):
        out_ref[...] = jnp.dot(
            left_ref[...], right_ref[...], preferred_element_type=FULL
        ).astype(out_type)

    return pl.pallas_call(
        body,
        grid=(width // tile,),
        in_specs=[
            resident((rows, depth)),
            pl.BlockSpec((depth, tile), lambda j: (0, j)),
        ],
        out_specs=pl.BlockSpec((rows, tile), lambda j: (0, j)),
        out_shape=jax.ShapeDtypeStruct((rows, width), out_type),
        compiler_params=params(),
        cost_estimate=cost(2 * rows * depth * width, 2 * (rows * depth + depth * width) + 4 * rows * width),
        name="product",
    )(left, right)


def product_back(lefts, right, out_type, rows, part):
    width, depth = right.shape
    tile = min(256, width)

    def body(*refs):
        total = None
        start = 0
        for left_ref in refs[:-2]:
            extent = left_ref.shape[1]
            term = lax.dot_general(
                left_ref[...], refs[-2][:, start : start + extent], NT, preferred_element_type=FULL
            )
            total = term if total is None else total + term
            start += extent
        refs[-1][...] = total.astype(out_type)

    return pl.pallas_call(
        body,
        grid=(width // tile,),
        in_specs=[pl.BlockSpec((rows, left.shape[1]), lambda j: (part, 0)) for left in lefts]
        + [pl.BlockSpec((tile, depth), lambda j: (j, 0))],
        out_specs=pl.BlockSpec((rows, tile), lambda j: (0, j)),
        out_shape=jax.ShapeDtypeStruct((rows, width), out_type),
        compiler_params=params(),
        cost_estimate=cost(2 * rows * depth * width, 2 * (rows * depth + width * depth) + 4 * rows * width),
        name="product_back",
    )(*lefts, right)


def token_sum(jobs, count, ordered=True):
    depth = jobs[0][0][0].shape[1]
    widths = [rights[0].shape[1] for _, rights in jobs]
    width = sum(widths)
    tokens = max(sum(left.shape[0] for left in lefts) for lefts, _ in jobs)
    tile = min(fit(extent, 512) for extent in widths)
    deep, across, cores = digits(count)
    group = depth // count
    pieces = len(jobs[0][0])
    starts = [sum(widths[:index]) // tile for index in range(len(jobs) + 1)]

    def flip(left_refs, turned):
        me = lax.axis_index("fsdp")
        my_z, my_x, my_c = me // (across * cores), (me // cores) % across, me % cores
        start = 0
        for left_ref in left_refs:
            flipped = left_ref[...].T
            extent = left_ref.shape[0]
            if not ordered:
                turned[:, start : start + extent] = flipped
            for source in range(count if ordered else 0):
                z, x, c = source // (across * cores), (source // cores) % across, source % cores
                place = (
                    ((c - my_c + cores) % cores) * across + (x - my_x + across) % across
                ) * deep + (z - my_z + deep) % deep
                turned[pl.ds(pl.multiple_of(place * group, group), group), start : start + extent] = (
                    flipped[source * group : (source + 1) * group]
                )
            start += extent

    def body(*refs):
        out_refs, turned = refs[2 * pieces * len(jobs) : -1], refs[-1]
        step = pl.program_id(0)
        for index in range(len(jobs)):
            mine = refs[2 * pieces * index : 2 * pieces * (index + 1)]

            @pl.when(step == starts[index])
            def _():
                flip(mine[:pieces], turned)

            @pl.when((step >= starts[index]) & (step < starts[index + 1]))
            def _():
                total = None
                start = 0
                for right_ref in mine[pieces:]:
                    extent = right_ref.shape[0]
                    term = jnp.dot(
                        turned[:, start : start + extent], right_ref[...], preferred_element_type=FULL
                    )
                    total = term if total is None else total + term
                    start += extent
                total = total.astype(LOW)
                start = 0
                for out_ref in out_refs:
                    out_ref[...] = total[start : start + out_ref.shape[0]]
                    start += out_ref.shape[0]

    def place_of(index):
        last = widths[index] // tile - 1
        return lambda j: (0, jnp.clip(j - starts[index], 0, last))

    half = depth // cores
    heights = (half, depth - half) if ordered else (depth,)
    in_specs = []
    operands = []
    for index, (lefts, rights) in enumerate(jobs):
        in_specs += [resident(left.shape) for left in lefts]
        in_specs += [pl.BlockSpec((right.shape[0], tile), place_of(index)) for right in rights]
        operands += [*lefts, *rights]
    return pl.pallas_call(
        body,
        grid=(width // tile,),
        in_specs=in_specs,
        out_specs=[pl.BlockSpec((height, tile), lambda j: (0, j)) for height in heights],
        out_shape=[jax.ShapeDtypeStruct((height, width), LOW) for height in heights],
        scratch_shapes=[pltpu.VMEM((depth, tokens), LOW)],
        compiler_params=params(),
        cost_estimate=cost(
            2 * depth * tokens * width, 2 * (len(jobs) * depth * tokens + tokens * width + depth * width)
        ),
        name="token_sum",
    )(*operands)


def head_lanes():
    lane = lax.broadcasted_iota(jnp.int32, (1, PAIR), 1)
    first = (lane < HEAD).astype(FULL)
    return lane, ((first, HEAD), (1.0 - first, 0))


def in_lanes(lane, free, column):
    total = 0.0
    for index in range(3):
        piece = column.astype(LOW).astype(FULL)
        total = total + jnp.where(lane == free + index, piece, 0.0)
        column = column - piece
    return total


def ones_in_lanes(lane, free, values):
    return jnp.where((lane >= free) & (lane < free + 3), 1.0, values.astype(FULL)).astype(LOW)


def attend_forward(triple, start, width):
    tokens = triple.shape[0]
    pairs = width // PAIR
    first = start // PAIR
    block = min(512, tokens)
    scaling = HEAD ** (-0.5)

    def body(query_ref, keys_ref, values_ref, out_ref, level_ref):
        lane, heads = head_lanes()
        keys = keys_ref[...]
        values = values_ref[...].astype(FULL)
        query = query_ref[...].astype(FULL)
        total = level = 0.0
        for mask, free in heads:
            scores = lax.dot_general(
                (query * (mask * scaling)).astype(LOW), keys, NT, preferred_element_type=FULL
            )
            peak = jnp.max(scores, axis=-1, keepdims=True)
            raised = jnp.exp(scores - peak).astype(LOW)
            counted = jnp.where(lane == free, 1.0, values * mask).astype(LOW)
            mixed = jnp.dot(raised, counted, preferred_element_type=FULL)
            sums = mixed[:, free : free + 1]
            total = total + mixed * mask / sums
            level = level + mask * (peak + jnp.log(sums))
        out_ref[...] = total.astype(LOW)
        level_ref[...] = level

    return pl.pallas_call(
        body,
        grid=(pairs, tokens // block),
        in_specs=[
            pl.BlockSpec((block, PAIR), lambda h, i: (i, first + h)),
            pl.BlockSpec((tokens, PAIR), lambda h, i: (0, first + pairs + h)),
            pl.BlockSpec((tokens, PAIR), lambda h, i: (0, first + 2 * pairs + h)),
        ],
        out_specs=[pl.BlockSpec((block, PAIR), lambda h, i: (i, h))] * 2,
        out_shape=[
            jax.ShapeDtypeStruct((tokens, width), LOW),
            jax.ShapeDtypeStruct((tokens, width), FULL),
        ],
        compiler_params=params(),
        cost_estimate=cost(16 * tokens * tokens * width, 12 * tokens * width, tokens * tokens * width // HEAD),
        name="attend_forward",
    )(triple, triple, triple)


def probabilities(triple, start, level, width):
    tokens = triple.shape[0]
    pairs = width // PAIR
    first = start // PAIR
    block = min(512, tokens)
    scaling = HEAD ** (-0.5)

    def body(query_ref, keys_ref, level_ref, out_ref):
        lane, heads = head_lanes()
        keys = keys_ref[...]
        query = query_ref[...].astype(FULL)
        for index, (mask, free) in enumerate(heads):
            own = HEAD * index
            scores = lax.dot_general(
                ones_in_lanes(lane, free, keys),
                (
                    query * (mask * scaling) - in_lanes(lane, free, level_ref[:, own : own + 1])
                ).astype(LOW),
                NT,
                preferred_element_type=FULL,
            )
            out_ref[0, index] = jnp.exp(scores).astype(LOW)

    return pl.pallas_call(
        body,
        grid=(pairs, tokens // block),
        in_specs=[
            pl.BlockSpec((block, PAIR), lambda h, i: (i, first + h)),
            pl.BlockSpec((tokens, PAIR), lambda h, i: (0, first + pairs + h)),
            pl.BlockSpec((block, PAIR), lambda h, i: (i, h)),
        ],
        out_specs=pl.BlockSpec((1, 2, tokens, block), lambda h, i: (h, 0, 0, i)),
        out_shape=jax.ShapeDtypeStruct((pairs, 2, tokens, tokens), LOW),
        compiler_params=params(),
        cost_estimate=cost(4 * tokens * tokens * width, 4 * pairs * tokens * tokens, tokens * tokens * width // HEAD),
        name="probabilities",
    )(triple, triple, level)


def attend_backward(triple, start, attended, probs, grads, width):
    tokens = triple.shape[0]
    pairs = width // PAIR
    first = start // PAIR
    block = min(512, tokens)
    steps = tokens // block
    scaling = HEAD ** (-0.5)

    def body(query_ref, keys_ref, values_ref, out_low_ref, probs_ref, grad_ref, out_ref, key_sum, value_sum):
        pair = pl.program_id(0)
        step = pl.program_id(1)
        lane, heads = head_lanes()
        keys = keys_ref[...]
        values = values_ref[...]
        query = query_ref[...].astype(FULL)
        grad = grad_ref[...].astype(FULL)
        inner = grad * out_low_ref[...].astype(FULL)
        query_grad = key_grad = value_grad = None
        for index, (mask, free) in enumerate(heads):
            query_part = (query * (mask * scaling)).astype(LOW)
            grad_part = grad * mask
            probs = probs_ref[0, index]
            prob_grad = lax.dot_general(
                ones_in_lanes(lane, free, values),
                (
                    grad_part - in_lanes(lane, free, jnp.sum(inner * mask, axis=-1, keepdims=True))
                ).astype(LOW),
                NT,
                preferred_element_type=FULL,
            )
            score_grad = (probs.astype(FULL) * prob_grad).astype(LOW)
            value_part = jnp.dot(probs, grad_part.astype(LOW), preferred_element_type=FULL)
            key_part = jnp.dot(score_grad, query_part, preferred_element_type=FULL)
            asked_part = lax.dot_general(
                score_grad, keys * (mask * scaling).astype(LOW), TN, preferred_element_type=FULL
            )
            if query_grad is None:
                query_grad, key_grad, value_grad = asked_part, key_part, value_part
            else:
                query_grad, key_grad, value_grad = (
                    query_grad + asked_part,
                    key_grad + key_part,
                    value_grad + value_part,
                )

        @pl.when(step == 0)
        def _():
            key_sum[...] = key_grad
            value_sum[...] = value_grad

        @pl.when(step > 0)
        def _():
            key_sum[...] += key_grad
            value_sum[...] += value_grad

        rows = pl.ds(pl.multiple_of(step * block, block), block)
        out_ref[rows, pl.ds(pl.multiple_of(pair * PAIR, PAIR), PAIR)] = query_grad.astype(LOW)

        @pl.when(step == steps - 1)
        def _():
            out_ref[:, pl.ds(pl.multiple_of(width + pair * PAIR, PAIR), PAIR)] = key_sum[...].astype(LOW)
            out_ref[:, pl.ds(pl.multiple_of(2 * width + pair * PAIR, PAIR), PAIR)] = value_sum[
                ...
            ].astype(LOW)

    rows_of_pair = pl.BlockSpec((block, PAIR), lambda h, i: (i, h))
    return pl.pallas_call(
        body,
        grid=(pairs, steps),
        in_specs=[
            pl.BlockSpec((block, PAIR), lambda h, i: (i, first + h)),
            pl.BlockSpec((tokens, PAIR), lambda h, i: (0, first + pairs + h)),
            pl.BlockSpec((tokens, PAIR), lambda h, i: (0, first + 2 * pairs + h)),
            rows_of_pair,
            pl.BlockSpec((1, 2, tokens, block), lambda h, i: (h, 0, 0, i)),
            rows_of_pair,
        ],
        out_specs=resident((tokens, 3 * width)),
        out_shape=jax.ShapeDtypeStruct((tokens, 3 * width), LOW),
        scratch_shapes=[pltpu.VMEM((tokens, PAIR), FULL), pltpu.VMEM((tokens, PAIR), FULL)],
        compiler_params=params(),
        cost_estimate=cost(32 * tokens * tokens * width, 20 * tokens * width + 4 * pairs * tokens * tokens),
        name="attend_backward",
    )(triple, triple, triple, attended, probs, grads)


def feed_both(normed, branch_grad, weights, out_type):
    tokens, depth = normed.shape
    units = weights.shape[1] // 2
    tile = min(512, units)
    steps = units // tile

    def body(normed_ref, grad_ref, up_ref, down_ref, out_ref, back_ref, hidden_ref, pre_ref, out_sum, back_sum):
        step = pl.program_id(0)
        up = up_ref[...]
        down = down_ref[...]
        pre = jnp.dot(normed_ref[...], up, preferred_element_type=FULL)
        hidden_grad = jnp.dot(grad_ref[...], down, preferred_element_type=FULL)
        square = pre * pre
        bent = jnp.tanh(0.7978845608028654 * (pre + 0.044715 * (square * pre)))
        half = 0.5 * (1.0 + bent)
        hidden = (pre * half).astype(LOW)
        slope = half + 0.5 * pre * (1.0 - bent * bent) * (
            0.7978845608028654 * (1.0 + 0.134145 * square)
        )
        pre_grad = (hidden_grad * slope).astype(LOW)
        hidden_ref[...] = hidden
        pre_ref[...] = pre_grad
        out_part = lax.dot_general(hidden, down, NT, preferred_element_type=FULL)
        back_part = lax.dot_general(pre_grad, up, NT, preferred_element_type=FULL)

        @pl.when(step == 0)
        def _():
            out_sum[...] = out_part
            back_sum[...] = back_part

        @pl.when(step > 0)
        def _():
            out_sum[...] += out_part
            back_sum[...] += back_part

        @pl.when(step == steps - 1)
        def _():
            out_ref[...] = out_sum[...].astype(out_type)
            back_ref[...] = back_sum[...].astype(out_type)

    return pl.pallas_call(
        body,
        grid=(steps,),
        in_specs=[
            resident((tokens, depth)),
            resident((tokens, depth)),
            pl.BlockSpec((depth, tile), lambda j: (0, j)),
            pl.BlockSpec((depth, tile), lambda j: (0, steps + j)),
        ],
        out_specs=[
            resident((tokens, depth)),
            resident((tokens, depth)),
            pl.BlockSpec((tokens, tile), lambda j: (0, j)),
            pl.BlockSpec((tokens, tile), lambda j: (0, j)),
        ],
        out_shape=[
            jax.ShapeDtypeStruct((tokens, depth), out_type),
            jax.ShapeDtypeStruct((tokens, depth), out_type),
            jax.ShapeDtypeStruct((tokens, units), LOW),
            jax.ShapeDtypeStruct((tokens, units), LOW),
        ],
        scratch_shapes=[pltpu.VMEM((tokens, depth), FULL), pltpu.VMEM((tokens, depth), FULL)],
        compiler_params=params(),
        cost_estimate=cost(8 * tokens * depth * units, 4 * depth * units + 12 * tokens * depth + 4 * tokens * units, tokens * units),
        name="feed_both",
    )(normed, branch_grad, weights, weights)


def standardize(values):
    middle = jnp.mean(values, axis=-1, keepdims=True)
    centred = values - middle
    spread = jnp.mean(centred * centred, axis=-1, keepdims=True)
    rate = lax.rsqrt(spread + 1e-06)
    return centred * rate, rate


def standardize_back(grad, values, scale_term):
    unit, rate = standardize(values)
    pulled = grad * (1.0 + scale_term)
    resid = rate * (
        pulled
        - jnp.mean(pulled, axis=-1, keepdims=True)
        - unit * jnp.mean(pulled * unit, axis=-1, keepdims=True)
    )
    return resid, jnp.sum(grad, axis=0, keepdims=True), jnp.sum(grad * unit, axis=0, keepdims=True)


def store_sums(sums_ref, rows):
    @pl.when(pl.program_id(0) == 0)
    def _():
        sums_ref[...] = jnp.zeros_like(sums_ref)

    for index, row in enumerate(rows):
        sums_ref[index : index + 1, :] += row


def store_lines(out_ref, values):
    for index in range(out_ref.shape[1]):
        out_ref[:, index, :] = values[:, index * PAIR : (index + 1) * PAIR]


def by_tokens(body, arrays, wholes, outs, sums, flops, name):
    tokens = arrays[0].shape[0]
    block = min(256, tokens)

    def cut(shape):
        return pl.BlockSpec((block,) + shape[1:], lambda j: (j,) + (0,) * (len(shape) - 1))

    out_specs = [cut(shape) for shape, _ in outs]
    out_shape = [jax.ShapeDtypeStruct(shape, kind) for shape, kind in outs]
    if sums:
        out_specs.append(resident((8, sums)))
        out_shape.append(jax.ShapeDtypeStruct((8, sums), FULL))
    moved = sum(value.size * value.dtype.itemsize for value in list(arrays) + list(wholes) + out_shape)
    return pl.pallas_call(
        body,
        grid=(tokens // block,),
        in_specs=[cut(value.shape) for value in arrays] + [resident(value.shape) for value in wholes],
        out_specs=out_specs,
        out_shape=out_shape,
        compiler_params=params(),
        cost_estimate=cost(flops, moved),
        name=name,
    )(*arrays, *wholes)


def merge_and_normalize(attended, latents, merge, gate, shift, scale):
    tokens, depth = latents.shape

    def body(attended_ref, latents_ref, merge_ref, gate_ref, shift_ref, scale_ref, branch_ref, after_ref, normed_ref):
        branch = lax.dot_general(attended_ref[...], merge_ref[...], NT, preferred_element_type=FULL)
        after = latents_ref[...] + gate_ref[...] * branch
        branch_ref[...] = branch
        after_ref[...] = after
        normed_ref[...] = (
            standardize(after)[0] * (1.0 + scale_ref[...]) + shift_ref[...]
        ).astype(LOW)

    shape = (tokens, depth)
    return by_tokens(
        body,
        [attended, latents],
        [merge, gate, shift, scale],
        [(shape, FULL), (shape, FULL), (shape, LOW)],
        0,
        2 * tokens * depth * merge.shape[1],
        "merge_and_normalize",
    )


def second_back(grad, parts, after, branch, cotangent, merge, gate, scale, spans):
    tokens, depth = after.shape
    count = len(parts)

    def body(*refs):
        total = refs[0][...]
        for part_ref in refs[1 : 1 + count]:
            total = total + part_ref[...].astype(FULL)
        after_ref, branch_ref, cotangent_ref, merge_ref, gate_ref, scale_ref = refs[1 + count : 7 + count]
        grad_ref, low_ref = refs[7 + count : 9 + count]
        piece_refs, sums_ref = refs[9 + count : -1], refs[-1]
        resid, shift_grad, scale_grad = standardize_back(total, after_ref[...], scale_ref[...])
        after_grad = cotangent_ref[...] + resid
        low = (gate_ref[...] * after_grad).astype(LOW)
        grad_ref[...] = after_grad
        low_ref[...] = low
        back = jnp.dot(low, merge_ref[...], preferred_element_type=FULL).astype(LOW)
        for piece_ref, (start, end) in zip(piece_refs, spans):
            piece_ref[...] = back[:, start:end]
        store_sums(
            sums_ref,
            [jnp.sum(after_grad * branch_ref[...], axis=0, keepdims=True), shift_grad, scale_grad],
        )

    outs = [((tokens, depth), FULL), ((tokens, depth), LOW)]
    outs += [((tokens, end - start), LOW) for start, end in spans]
    results = by_tokens(
        body,
        [grad, *parts, after, branch, cotangent],
        [merge, gate, scale],
        outs,
        depth,
        2 * tokens * depth * merge.shape[1],
        "second_back",
    )
    return results[0], results[1], results[2:-1], results[-1]


def first_back(grad, parts, latents, after_grad, scale):
    tokens, depth = latents.shape
    count = len(parts)

    def body(*refs):
        total = refs[0][...]
        for part_ref in refs[1 : 1 + count]:
            total = total + part_ref[...].astype(FULL)
        latents_ref, after_ref, scale_ref, out_ref, sums_ref = refs[1 + count :]
        resid, shift_grad, scale_grad = standardize_back(total, latents_ref[...], scale_ref[...])
        store_lines(out_ref, after_ref[...] + resid)
        store_sums(sums_ref, [shift_grad, scale_grad])

    return by_tokens(
        body,
        [grad, *parts, latents, after_grad],
        [scale],
        [((tokens, depth // PAIR, PAIR), FULL)],
        depth,
        20 * tokens * depth,
        "first_back",
    )


def last_forward(branch, parts, after, cotangent, gate):
    tokens, depth = after.shape
    count = len(parts)

    def body(*refs):
        total = refs[0][...]
        for part_ref in refs[1 : 1 + count]:
            total = total + part_ref[...].astype(FULL)
        after_ref, cotangent_ref, gate_ref, out_ref, sums_ref = refs[1 + count :]
        store_lines(out_ref, after_ref[...] + gate_ref[...] * total)
        store_sums(sums_ref, [jnp.sum(cotangent_ref[...] * total, axis=0, keepdims=True)])

    return by_tokens(
        body,
        [branch, *parts, after, cotangent],
        [gate],
        [((tokens, depth // PAIR, PAIR), FULL)],
        depth,
        6 * tokens * depth,
        "last_forward",
    )


def adam_step(weight, first, second, grad_sum, rate):
    first_new = 0.9 * first + 0.1 * grad_sum
    second_new = 0.999 * second + 0.001 * grad_sum * grad_sum
    first_hat = first_new / (1.0 - 0.9**STEP)
    second_hat = second_new / (1.0 - 0.999**STEP)
    weight_new = weight - rate * (first_hat / (jnp.sqrt(second_hat) + 1e-08) + 0.01 * weight)
    return (weight_new, first_new, second_new)


def shift_tp(values, steps, count):
    steps = steps % count
    if steps == 0:
        return values
    return lax.ppermute(values, "tp", [(i, (i + steps) % count) for i in range(count)])


def digits(count):
    if count % 8 == 0:
        return 4, count // 8, 2
    return count // 2, 1, 2


def shift_fsdp(values, digit, steps, count):
    sizes = digits(count)
    scale = (sizes[1] * sizes[2], sizes[2], 1)[digit]
    size = sizes[digit]
    pairs = []
    for source in range(count):
        own = (source // scale) % size
        pairs.append((source, source + ((own + steps) % size - own) * scale))
    return lax.ppermute(values, "fsdp", pairs)


def arrange(pieces, count, group, by_z):
    deep, across, cores = digits(count)
    width = pieces[0].shape[1]
    tile = fit(width, 512)
    outer, inner = (deep, across) if by_z else (across, deep)

    def body(*refs):
        out_ref = refs[-1]
        me = lax.axis_index("fsdp")
        my_z, my_x, my_c = me // (across * cores), (me // cores) % across, me % cores
        for core in range(cores):
            for first in range(outer):
                source = refs[core * outer + first]
                for second in range(inner):
                    z, x = (first, second) if by_z else (second, first)
                    place = (
                        ((my_z - z + deep) % deep) * across + (my_x - x + across) % across
                    ) * cores + (my_c - core + cores) % cores
                    out_ref[pl.ds(pl.multiple_of(place * group, group), group), :] = source[
                        second * group : (second + 1) * group, :
                    ]

    return pl.pallas_call(
        body,
        grid=(width // tile,),
        in_specs=[pl.BlockSpec((piece.shape[0], tile), lambda j: (0, j)) for piece in pieces],
        out_specs=pl.BlockSpec((count * group, tile), lambda j: (0, j)),
        out_shape=jax.ShapeDtypeStruct((count * group, width), LOW),
        compiler_params=params(),
        cost_estimate=cost(0, 4 * count * group * width),
        name="arrange",
    )(*pieces)


def gather_z(shard, count):
    deep = digits(count)[0]
    return [shard] + [shift_fsdp(shard, 0, k, count) for k in range(1, deep)]


def gather_x(line, count):
    across = digits(count)[1]
    line = jnp.concatenate(line, axis=0)
    return [line] + [shift_fsdp(line, 1, k, count) for k in range(1, across)]


def gather_core(plane, count):
    cores = digits(count)[2]
    return plane + [shift_fsdp(piece, 2, k, count) for k in range(1, cores) for piece in plane]


def scatter_core(pair, count):
    kept, sent = pair
    return kept, shift_fsdp(sent, 2, 1, count)


def scatter_x(pair, count):
    kept, came = pair
    across = digits(count)[1]
    rows = kept.shape[0] // across

    def both(x):
        part = slice(x * rows, (x + 1) * rows)
        return kept[part].astype(FULL) + came[part].astype(FULL)

    return kept[:rows], came[:rows], [
        shift_fsdp(both(k).astype(LOW), 1, k, count) for k in range(1, across)
    ]


def scatter_z(state, count):
    kept, came, parts = state
    deep = digits(count)[0]
    group = kept.shape[0] // deep

    def both(z):
        rows = slice(z * group, (z + 1) * group)
        return sum(
            (part[rows].astype(FULL) for part in [came] + parts), start=kept[rows].astype(FULL)
        )

    return both(0), [shift_fsdp(both(k).astype(LOW), 0, k, count) for k in range(1, deep)]


def scatter_end(state):
    own, parts = state
    return sum((part.astype(FULL) for part in parts), start=own)


def gather_rows(shard):
    return lax.all_gather(shard, "fsdp", axis=0, tiled=True)


def scatter_rows(whole):
    return lax.psum_scatter(whole, "fsdp", scatter_dimension=0, tiled=True)


def together(*values):
    return lax.optimization_barrier(values)


def modulation_shares(grads, tp_count, fsdp_count, part):
    count = grads.shape[0]
    place = lax.axis_index("tp")
    total = sum(
        shift_tp(
            lax.dynamic_slice_in_dim(grads, (place + k) % tp_count * part, part, axis=1), k, tp_count
        )
        for k in range(tp_count)
    )
    every = lax.all_to_all(
        jnp.broadcast_to(total.reshape(1, count * part), (fsdp_count, count * part)),
        "fsdp",
        split_axis=0,
        concat_axis=0,
        tiled=True,
    )
    return every


def local(
    fsdp_count,
    tp_count,
    latents_in,
    condition,
    out_grad,
    condition_weight,
    condition_first,
    condition_second,
    heads_weight,
    heads_first,
    heads_second,
    merge_weight,
    merge_first,
    merge_second,
    up_weight,
    up_first,
    up_second,
    down_weight,
    down_first,
    down_second,
):
    own, _, depth = latents_in.shape
    shard_rows = condition_weight.shape[0]
    part = condition_weight.shape[2]
    width = heads_weight.shape[2]
    units = up_weight.shape[1]
    ring = range(tp_count)
    others = range(1, tp_count)

    def blocks_of_tokens(values):
        return [shift_tp(values, -k, tp_count) for k in ring]

    pairs = width // PAIR
    spans = [(0, pairs // 2), (pairs // 2, pairs)] if pairs > 1 else [(0, pairs)]
    spans = [(start * PAIR, end * PAIR) for start, end in spans]

    heads_low = jnp.moveaxis(heads_weight.astype(LOW), 0, 1)
    heads_shard = jnp.concatenate(
        [heads_low[:, :, start:end].reshape(shard_rows, -1) for start, end in spans], axis=1
    )
    activated = jax.nn.silu(condition).astype(LOW)
    activated, heads_shard = together(activated, heads_shard)
    heads_whole = gather_rows(heads_shard)
    activated_rows = lax.all_to_all(
        activated.reshape(fsdp_count, shard_rows), "fsdp", split_axis=0, concat_axis=0, tiled=True
    )
    latents, _ = together(latents_in.reshape(own, depth), heads_shard)
    (cotangent,) = together(out_grad.reshape(own, depth))

    unit_one, _ = standardize(latents)
    unit_blocks = blocks_of_tokens(unit_one.astype(LOW))
    shares = jnp.dot(
        activated_rows,
        condition_weight.astype(LOW).reshape(shard_rows, 6 * part),
        preferred_element_type=FULL,
    )
    shares = lax.all_to_all(shares, "fsdp", split_axis=0, concat_axis=0, tiled=True)
    feed_shard = jnp.concatenate([up_weight.astype(LOW), down_weight.astype(LOW).T], axis=1)
    shares, unit_blocks, cotangent = together(shares, unit_blocks, cotangent)
    modulation_part = jnp.sum(shares, axis=0).reshape(6, part)
    modulation = lax.all_gather(modulation_part, "tp", axis=1, tiled=True)
    modulation, merge_shard = together(modulation, merge_weight.astype(LOW).T)
    merge_shard = jnp.concatenate([shift_tp(merge_shard, k, tp_count) for k in ring], axis=1)
    merge_line = gather_z(merge_shard, fsdp_count)
    shift_one, scale_one, gate_one, shift_two, scale_two, gate_two = (
        modulation[k : k + 1] for k in range(6)
    )

    branch_grad = (gate_two * cotangent).astype(LOW)
    branch_grad_blocks = blocks_of_tokens(branch_grad)

    normed_one = jnp.concatenate(
        [
            ((unit_one if k == 0 else unit_blocks[k].astype(FULL)) * (1.0 + scale_one) + shift_one).astype(LOW)
            for k in ring
        ],
        axis=0,
    )
    heads_whole, feed_shard, normed_one, merge_line = together(
        heads_whole, feed_shard, normed_one, merge_line
    )
    feed_whole = gather_rows(feed_shard)
    triple = product(normed_one, heads_whole, LOW)
    triple, merge_line = together(triple, merge_line)
    merge_plane = gather_x(merge_line, fsdp_count)
    attended = []
    mixes = []
    for index, (start, end) in enumerate(spans):
        mixed, level = attend_forward(triple, 3 * start, end - start)
        if index == 0:
            mixed, merge_plane, branch_grad_blocks = together(mixed, merge_plane, branch_grad_blocks)
            merge_whole = arrange(gather_core(merge_plane, fsdp_count), fsdp_count, shard_rows, False)
        mixes.append((mixed, level))
        attended.append([shift_tp(mixed[k * own : (k + 1) * own], k, tp_count) for k in ring])
    attended_own = jnp.concatenate([part[k] for k in ring for part in attended], axis=1)
    attn_branch, after_attn, normed_two = merge_and_normalize(
        attended_own, latents, merge_whole, gate_one, shift_two, scale_two
    )
    normed_two_blocks = blocks_of_tokens(normed_two)

    mixes = [
        (mixed, probabilities(triple, 3 * start, level, end - start))
        for (mixed, level), (start, end) in zip(mixes, spans)
    ]
    normed_two_blocks, mixes = together(normed_two_blocks, mixes)
    fed = [None] + [feed_both(normed_two_blocks[k], branch_grad_blocks[k], feed_whole, LOW) for k in others]
    back_parts = [shift_tp(fed[k][1], k, tp_count) for k in others]
    normed_two, fed = together(normed_two, fed)
    fed[0] = feed_both(normed_two, branch_grad, feed_whole, FULL)
    fed, branch_parts = together(fed, [fed[k][0] for k in others])
    branch_parts = [shift_tp(values, k, tp_count) for k, values in zip(others, branch_parts)]
    (feed_grad,) = token_sum(
        [
            (normed_two_blocks, [fed[k][3] for k in ring]),
            (branch_grad_blocks, [fed[k][2] for k in ring]),
        ],
        fsdp_count,
        ordered=False,
    )
    back_parts, feed_grad = together(back_parts, feed_grad)
    feed_sum = scatter_rows(feed_grad)
    cuts = [(k * width + start, k * width + end) for k in ring for start, end in spans]
    after_grad, attn_grad, pieces, second_sums = second_back(
        fed[0][1], back_parts, after_attn, attn_branch, cotangent, merge_whole, gate_one, scale_two, cuts
    )
    attended_grads = []
    for index in range(len(spans)):
        mine = pieces[index :: len(spans)]
        if index:
            attended_grads, mine = together(attended_grads, mine)
        attended_grads.append(
            jnp.concatenate([shift_tp(mine[k], -k, tp_count) for k in ring], axis=0)
        )
    triple_grads = [
        attend_backward(triple, 0, *mixes[0], attended_grads[0], spans[0][1])
    ]
    triple_grads, branch_parts = together(triple_grads, branch_parts)
    pair = token_sum([([attn_grad], [attended_own]), ([normed_one], triple_grads)], fsdp_count)
    state = scatter_core(pair, fsdp_count)
    block_out, last_sums = last_forward(fed[0][0], branch_parts, after_attn, cotangent, gate_two)
    attended_grads, state, block_out = together(attended_grads, state, block_out)
    state = scatter_x(state, fsdp_count)
    for index in range(1, len(spans)):
        start, end = spans[index]
        triple_grads.append(
            attend_backward(triple, 3 * start, *mixes[index], attended_grads[index], end - start)
        )
    parts = [product_back(triple_grads, heads_whole, LOW, own, k) for k in others]
    one_parts = [shift_tp(values, k, tp_count) for k, values in zip(others, parts)]
    triple_grads, parts = together(triple_grads, parts)
    last = None
    if len(spans) > 1:
        last = token_sum([([normed_one], triple_grads[1:])], fsdp_count)
    triple_grads, last, state = together(triple_grads, last, state)
    state = scatter_z(state, fsdp_count)
    if last:
        last = scatter_core(last, fsdp_count)
    normed_one_grad = product_back(triple_grads, heads_whole, FULL, own, 0)
    one_parts, normed_one_grad, last = together(one_parts, normed_one_grad, last)
    if last:
        last = scatter_x(last, fsdp_count)
    latents_grad, first_sums = first_back(normed_one_grad, one_parts, latents, after_grad, scale_one)
    first_sums, last, feed_sum = together(first_sums, last, feed_sum)
    if last:
        last = scatter_z(last, fsdp_count)
    up_new = adam_step(up_weight, up_first, up_second, feed_sum[:, :units].astype(FULL), 0.02)
    down_new = adam_step(down_weight, down_first, down_second, feed_sum[:, units:].T.astype(FULL), 0.01)
    modulation_all = modulation_shares(
        jnp.concatenate([first_sums[:2], second_sums[:3], last_sums[:1]], axis=0),
        tp_count,
        fsdp_count,
        part,
    )
    modulation_all, state, last = together(modulation_all, state, last)
    first_sum = scatter_end(state)
    merge_sum_all, heads_sums = first_sum[:, : tp_count * width], [first_sum[:, tp_count * width :]]
    if last:
        heads_sums.append(scatter_end(last))
    heads_sums = [total.reshape(shard_rows, 3, -1) for total in heads_sums]
    condition_sum = lax.dot_general(
        activated_rows.astype(FULL),
        modulation_all,
        TN,
        precision=lax.Precision.HIGHEST,
        preferred_element_type=FULL,
    ).reshape(shard_rows, 6, part)
    merge_sum = merge_sum_all[:, :width]
    for k in others:
        merge_sum = merge_sum + shift_tp(
            merge_sum_all[:, k * width : (k + 1) * width], -k, tp_count
        )
    heads_sum = jnp.moveaxis(jnp.concatenate(heads_sums, axis=2), 1, 0)
    cond_new = adam_step(condition_weight, condition_first, condition_second, condition_sum, 0.02)
    heads_new = adam_step(heads_weight, heads_first, heads_second, heads_sum, 0.02)
    merge_new = adam_step(merge_weight, merge_first, merge_second, merge_sum.T, 0.15)
    return (
        block_out.reshape(own, 1, depth),
        latents_grad.reshape(own, 1, depth),
        *cond_new,
        *heads_new,
        *merge_new,
        *up_new,
        *down_new,
    )


def solution(mesh):
    stream = P("tp", "fsdp", None)
    cond = P("fsdp", None, "tp")
    heads = P(None, "fsdp", "tp")
    wide = P("tp", "fsdp")
    tall = P("fsdp", "tp")
    in_specs = (stream, P("fsdp", None), stream) + (cond,) * 3 + (heads,) * 3 + (wide,) * 3 + (tall,) * 3 + (wide,) * 3
    out_specs = (stream, stream) + (cond,) * 3 + (heads,) * 3 + (wide,) * 3 + (tall,) * 3 + (wide,) * 3
    return jax.shard_map(
        functools.partial(local, mesh.shape["fsdp"], mesh.shape["tp"]),
        mesh=mesh,
        in_specs=in_specs,
        out_specs=out_specs,
        check_vma=False,
    )
```

```python
import functools

import jax
import jax.numpy as jnp
from jax import lax
from jax.experimental import pallas as pl
from jax.experimental.pallas import tpu as pltpu
from jax.sharding import PartitionSpec as P

HEAD = 64
PAIR = 2 * HEAD
STEP = 5
LOW = jnp.bfloat16
FULL = jnp.float32
NT = (((1,), (1,)), ((), ()))
TN = (((0,), (0,)), ((), ()))


def params(limit=56):
    return pltpu.CompilerParams(vmem_limit_bytes=limit * 1024 * 1024)


def cost(flops, moved, raised=0):
    return pl.CostEstimate(flops=int(flops), bytes_accessed=int(moved), transcendentals=int(raised))


def resident(shape):
    return pl.BlockSpec(shape, lambda *step: (0,) * len(shape))


def fit(width, most):
    return next(tile for tile in (most, 512, 256, PAIR) if tile <= most and width % tile == 0)


def product(left, right, out_type):
    rows, depth = left.shape
    width = right.shape[1]
    tile = fit(width, 512)

    def body(left_ref, right_ref, out_ref):
        out_ref[...] = jnp.dot(
            left_ref[...], right_ref[...], preferred_element_type=FULL
        ).astype(out_type)

    return pl.pallas_call(
        body,
        grid=(width // tile,),
        in_specs=[
            resident((rows, depth)),
            pl.BlockSpec((depth, tile), lambda j: (0, j)),
        ],
        out_specs=pl.BlockSpec((rows, tile), lambda j: (0, j)),
        out_shape=jax.ShapeDtypeStruct((rows, width), out_type),
        compiler_params=params(),
        cost_estimate=cost(2 * rows * depth * width, 2 * (rows * depth + depth * width) + 4 * rows * width),
        name="product",
    )(left, right)


def product_back(lefts, right, out_type, rows, part):
    width, depth = right.shape
    tile = min(256, width)

    def body(*refs):
        total = None
        start = 0
        for left_ref in refs[:-2]:
            extent = left_ref.shape[1]
            term = lax.dot_general(
                left_ref[...], refs[-2][:, start : start + extent], NT, preferred_element_type=FULL
            )
            total = term if total is None else total + term
            start += extent
        refs[-1][...] = total.astype(out_type)

    return pl.pallas_call(
        body,
        grid=(width // tile,),
        in_specs=[pl.BlockSpec((rows, left.shape[1]), lambda j: (part, 0)) for left in lefts]
        + [pl.BlockSpec((tile, depth), lambda j: (j, 0))],
        out_specs=pl.BlockSpec((rows, tile), lambda j: (0, j)),
        out_shape=jax.ShapeDtypeStruct((rows, width), out_type),
        compiler_params=params(),
        cost_estimate=cost(2 * rows * depth * width, 2 * (rows * depth + width * depth) + 4 * rows * width),
        name="product_back",
    )(*lefts, right)


def token_sum(jobs, count, ordered=True):
    depth = jobs[0][0][0].shape[1]
    widths = [rights[0].shape[1] for _, rights in jobs]
    width = sum(widths)
    tokens = max(sum(left.shape[0] for left in lefts) for lefts, _ in jobs)
    tile = min(fit(extent, 512) for extent in widths)
    deep, across, cores = digits(count)
    group = depth // count
    pieces = len(jobs[0][0])
    starts = [sum(widths[:index]) // tile for index in range(len(jobs) + 1)]

    def flip(left_refs, turned):
        me = lax.axis_index("fsdp")
        my_z, my_x, my_c = me // (across * cores), (me // cores) % across, me % cores
        start = 0
        for left_ref in left_refs:
            flipped = left_ref[...].T
            extent = left_ref.shape[0]
            if not ordered:
                turned[:, start : start + extent] = flipped
            for source in range(count if ordered else 0):
                z, x, c = source // (across * cores), (source // cores) % across, source % cores
                place = (
                    ((c - my_c + cores) % cores) * across + (x - my_x + across) % across
                ) * deep + (z - my_z + deep) % deep
                turned[pl.ds(pl.multiple_of(place * group, group), group), start : start + extent] = (
                    flipped[source * group : (source + 1) * group]
                )
            start += extent

    def body(*refs):
        out_refs, turned = refs[2 * pieces * len(jobs) : -1], refs[-1]
        step = pl.program_id(0)
        for index in range(len(jobs)):
            mine = refs[2 * pieces * index : 2 * pieces * (index + 1)]

            @pl.when(step == starts[index])
            def _():
                flip(mine[:pieces], turned)

            @pl.when((step >= starts[index]) & (step < starts[index + 1]))
            def _():
                total = None
                start = 0
                for right_ref in mine[pieces:]:
                    extent = right_ref.shape[0]
                    term = jnp.dot(
                        turned[:, start : start + extent], right_ref[...], preferred_element_type=FULL
                    )
                    total = term if total is None else total + term
                    start += extent
                total = total.astype(LOW)
                start = 0
                for out_ref in out_refs:
                    out_ref[...] = total[start : start + out_ref.shape[0]]
                    start += out_ref.shape[0]

    def place_of(index):
        last = widths[index] // tile - 1
        return lambda j: (0, jnp.clip(j - starts[index], 0, last))

    half = depth // cores
    heights = (half, depth - half) if ordered else (depth,)
    in_specs = []
    operands = []
    for index, (lefts, rights) in enumerate(jobs):
        in_specs += [resident(left.shape) for left in lefts]
        in_specs += [pl.BlockSpec((right.shape[0], tile), place_of(index)) for right in rights]
        operands += [*lefts, *rights]
    return pl.pallas_call(
        body,
        grid=(width // tile,),
        in_specs=in_specs,
        out_specs=[pl.BlockSpec((height, tile), lambda j: (0, j)) for height in heights],
        out_shape=[jax.ShapeDtypeStruct((height, width), LOW) for height in heights],
        scratch_shapes=[pltpu.VMEM((depth, tokens), LOW)],
        compiler_params=params(),
        cost_estimate=cost(
            2 * depth * tokens * width, 2 * (len(jobs) * depth * tokens + tokens * width + depth * width)
        ),
        name="token_sum",
    )(*operands)


def head_lanes():
    lane = lax.broadcasted_iota(jnp.int32, (1, PAIR), 1)
    first = (lane < HEAD).astype(FULL)
    return lane, ((first, HEAD), (1.0 - first, 0))


def in_lanes(lane, free, column):
    total = 0.0
    for index in range(3):
        piece = column.astype(LOW).astype(FULL)
        total = total + jnp.where(lane == free + index, piece, 0.0)
        column = column - piece
    return total


def ones_in_lanes(lane, free, values):
    return jnp.where((lane >= free) & (lane < free + 3), 1.0, values.astype(FULL)).astype(LOW)


def attend_forward(triple, start, width):
    tokens = triple.shape[0]
    pairs = width // PAIR
    first = start // PAIR
    block = min(512, tokens)
    scaling = HEAD ** (-0.5)

    def body(query_ref, keys_ref, values_ref, out_ref, level_ref):
        lane, heads = head_lanes()
        keys = keys_ref[...]
        values = values_ref[...].astype(FULL)
        query = query_ref[...].astype(FULL)
        total = level = 0.0
        for mask, free in heads:
            scores = lax.dot_general(
                (query * (mask * scaling)).astype(LOW), keys, NT, preferred_element_type=FULL
            )
            peak = jnp.max(scores, axis=-1, keepdims=True)
            raised = jnp.exp(scores - peak).astype(LOW)
            counted = jnp.where(lane == free, 1.0, values * mask).astype(LOW)
            mixed = jnp.dot(raised, counted, preferred_element_type=FULL)
            sums = mixed[:, free : free + 1]
            total = total + mixed * mask / sums
            level = level + mask * (peak + jnp.log(sums))
        out_ref[...] = total.astype(LOW)
        level_ref[...] = level

    return pl.pallas_call(
        body,
        grid=(pairs, tokens // block),
        in_specs=[
            pl.BlockSpec((block, PAIR), lambda h, i: (i, first + h)),
            pl.BlockSpec((tokens, PAIR), lambda h, i: (0, first + pairs + h)),
            pl.BlockSpec((tokens, PAIR), lambda h, i: (0, first + 2 * pairs + h)),
        ],
        out_specs=[pl.BlockSpec((block, PAIR), lambda h, i: (i, h))] * 2,
        out_shape=[
            jax.ShapeDtypeStruct((tokens, width), LOW),
            jax.ShapeDtypeStruct((tokens, width), FULL),
        ],
        compiler_params=params(),
        cost_estimate=cost(16 * tokens * tokens * width, 12 * tokens * width, tokens * tokens * width // HEAD),
        name="attend_forward",
    )(triple, triple, triple)


def probabilities(triple, start, level, width):
    tokens = triple.shape[0]
    pairs = width // PAIR
    first = start // PAIR
    block = min(512, tokens)
    scaling = HEAD ** (-0.5)

    def body(query_ref, keys_ref, level_ref, out_ref):
        lane, heads = head_lanes()
        keys = keys_ref[...]
        query = query_ref[...].astype(FULL)
        for index, (mask, free) in enumerate(heads):
            own = HEAD * index
            scores = lax.dot_general(
                ones_in_lanes(lane, free, keys),
                (
                    query * (mask * scaling) - in_lanes(lane, free, level_ref[:, own : own + 1])
                ).astype(LOW),
                NT,
                preferred_element_type=FULL,
            )
            out_ref[0, index] = jnp.exp(scores).astype(LOW)

    return pl.pallas_call(
        body,
        grid=(pairs, tokens // block),
        in_specs=[
            pl.BlockSpec((block, PAIR), lambda h, i: (i, first + h)),
            pl.BlockSpec((tokens, PAIR), lambda h, i: (0, first + pairs + h)),
            pl.BlockSpec((block, PAIR), lambda h, i: (i, h)),
        ],
        out_specs=pl.BlockSpec((1, 2, tokens, block), lambda h, i: (h, 0, 0, i)),
        out_shape=jax.ShapeDtypeStruct((pairs, 2, tokens, tokens), LOW),
        compiler_params=params(),
        cost_estimate=cost(4 * tokens * tokens * width, 4 * pairs * tokens * tokens, tokens * tokens * width // HEAD),
        name="probabilities",
    )(triple, triple, level)


def attend_backward(triple, start, attended, probs, grads, width):
    tokens = triple.shape[0]
    pairs = width // PAIR
    first = start // PAIR
    block = min(512, tokens)
    steps = tokens // block
    scaling = HEAD ** (-0.5)

    def body(query_ref, keys_ref, values_ref, out_low_ref, probs_ref, grad_ref, out_ref, key_sum, value_sum):
        pair = pl.program_id(0)
        step = pl.program_id(1)
        lane, heads = head_lanes()
        keys = keys_ref[...]
        values = values_ref[...]
        query = query_ref[...].astype(FULL)
        grad = grad_ref[...].astype(FULL)
        inner = grad * out_low_ref[...].astype(FULL)
        query_grad = key_grad = value_grad = None
        for index, (mask, free) in enumerate(heads):
            query_part = (query * (mask * scaling)).astype(LOW)
            grad_part = grad * mask
            probs = probs_ref[0, index]
            prob_grad = lax.dot_general(
                ones_in_lanes(lane, free, values),
                (
                    grad_part - in_lanes(lane, free, jnp.sum(inner * mask, axis=-1, keepdims=True))
                ).astype(LOW),
                NT,
                preferred_element_type=FULL,
            )
            score_grad = (probs.astype(FULL) * prob_grad).astype(LOW)
            value_part = jnp.dot(probs, grad_part.astype(LOW), preferred_element_type=FULL)
            key_part = jnp.dot(score_grad, query_part, preferred_element_type=FULL)
            asked_part = lax.dot_general(
                score_grad, keys * (mask * scaling).astype(LOW), TN, preferred_element_type=FULL
            )
            if query_grad is None:
                query_grad, key_grad, value_grad = asked_part, key_part, value_part
            else:
                query_grad, key_grad, value_grad = (
                    query_grad + asked_part,
                    key_grad + key_part,
                    value_grad + value_part,
                )

        @pl.when(step == 0)
        def _():
            key_sum[...] = key_grad
            value_sum[...] = value_grad

        @pl.when(step > 0)
        def _():
            key_sum[...] += key_grad
            value_sum[...] += value_grad

        rows = pl.ds(pl.multiple_of(step * block, block), block)
        out_ref[rows, pl.ds(pl.multiple_of(pair * PAIR, PAIR), PAIR)] = query_grad.astype(LOW)

        @pl.when(step == steps - 1)
        def _():
            out_ref[:, pl.ds(pl.multiple_of(width + pair * PAIR, PAIR), PAIR)] = key_sum[...].astype(LOW)
            out_ref[:, pl.ds(pl.multiple_of(2 * width + pair * PAIR, PAIR), PAIR)] = value_sum[
                ...
            ].astype(LOW)

    rows_of_pair = pl.BlockSpec((block, PAIR), lambda h, i: (i, h))
    return pl.pallas_call(
        body,
        grid=(pairs, steps),
        in_specs=[
            pl.BlockSpec((block, PAIR), lambda h, i: (i, first + h)),
            pl.BlockSpec((tokens, PAIR), lambda h, i: (0, first + pairs + h)),
            pl.BlockSpec((tokens, PAIR), lambda h, i: (0, first + 2 * pairs + h)),
            rows_of_pair,
            pl.BlockSpec((1, 2, tokens, block), lambda h, i: (h, 0, 0, i)),
            rows_of_pair,
        ],
        out_specs=resident((tokens, 3 * width)),
        out_shape=jax.ShapeDtypeStruct((tokens, 3 * width), LOW),
        scratch_shapes=[pltpu.VMEM((tokens, PAIR), FULL), pltpu.VMEM((tokens, PAIR), FULL)],
        compiler_params=params(),
        cost_estimate=cost(32 * tokens * tokens * width, 20 * tokens * width + 4 * pairs * tokens * tokens),
        name="attend_backward",
    )(triple, triple, triple, attended, probs, grads)


def feed_both(normed, branch_grad, weights, out_type):
    tokens, depth = normed.shape
    units = weights.shape[1] // 2
    tile = min(512, units)
    steps = units // tile

    def body(normed_ref, grad_ref, up_ref, down_ref, out_ref, back_ref, hidden_ref, pre_ref, out_sum, back_sum):
        step = pl.program_id(0)
        up = up_ref[...]
        down = down_ref[...]
        pre = jnp.dot(normed_ref[...], up, preferred_element_type=FULL)
        hidden_grad = jnp.dot(grad_ref[...], down, preferred_element_type=FULL)
        square = pre * pre
        bent = jnp.tanh(0.7978845608028654 * (pre + 0.044715 * (square * pre)))
        half = 0.5 * (1.0 + bent)
        hidden = (pre * half).astype(LOW)
        slope = half + 0.5 * pre * (1.0 - bent * bent) * (
            0.7978845608028654 * (1.0 + 0.134145 * square)
        )
        pre_grad = (hidden_grad * slope).astype(LOW)
        hidden_ref[...] = hidden
        pre_ref[...] = pre_grad
        out_part = lax.dot_general(hidden, down, NT, preferred_element_type=FULL)
        back_part = lax.dot_general(pre_grad, up, NT, preferred_element_type=FULL)

        @pl.when(step == 0)
        def _():
            out_sum[...] = out_part
            back_sum[...] = back_part

        @pl.when(step > 0)
        def _():
            out_sum[...] += out_part
            back_sum[...] += back_part

        @pl.when(step == steps - 1)
        def _():
            out_ref[...] = out_sum[...].astype(out_type)
            back_ref[...] = back_sum[...].astype(out_type)

    return pl.pallas_call(
        body,
        grid=(steps,),
        in_specs=[
            resident((tokens, depth)),
            resident((tokens, depth)),
            pl.BlockSpec((depth, tile), lambda j: (0, j)),
            pl.BlockSpec((depth, tile), lambda j: (0, steps + j)),
        ],
        out_specs=[
            resident((tokens, depth)),
            resident((tokens, depth)),
            pl.BlockSpec((tokens, tile), lambda j: (0, j)),
            pl.BlockSpec((tokens, tile), lambda j: (0, j)),
        ],
        out_shape=[
            jax.ShapeDtypeStruct((tokens, depth), out_type),
            jax.ShapeDtypeStruct((tokens, depth), out_type),
            jax.ShapeDtypeStruct((tokens, units), LOW),
            jax.ShapeDtypeStruct((tokens, units), LOW),
        ],
        scratch_shapes=[pltpu.VMEM((tokens, depth), FULL), pltpu.VMEM((tokens, depth), FULL)],
        compiler_params=params(),
        cost_estimate=cost(8 * tokens * depth * units, 4 * depth * units + 12 * tokens * depth + 4 * tokens * units, tokens * units),
        name="feed_both",
    )(normed, branch_grad, weights, weights)


def standardize(values):
    middle = jnp.mean(values, axis=-1, keepdims=True)
    centred = values - middle
    spread = jnp.mean(centred * centred, axis=-1, keepdims=True)
    rate = lax.rsqrt(spread + 1e-06)
    return centred * rate, rate


def standardize_back(grad, values, scale_term):
    unit, rate = standardize(values)
    pulled = grad * (1.0 + scale_term)
    resid = rate * (
        pulled
        - jnp.mean(pulled, axis=-1, keepdims=True)
        - unit * jnp.mean(pulled * unit, axis=-1, keepdims=True)
    )
    return resid, jnp.sum(grad, axis=0, keepdims=True), jnp.sum(grad * unit, axis=0, keepdims=True)


def store_sums(sums_ref, rows):
    @pl.when(pl.program_id(0) == 0)
    def _():
        sums_ref[...] = jnp.zeros_like(sums_ref)

    for index, row in enumerate(rows):
        sums_ref[index : index + 1, :] += row


def store_lines(out_ref, values):
    for index in range(out_ref.shape[1]):
        out_ref[:, index, :] = values[:, index * PAIR : (index + 1) * PAIR]


def by_tokens(body, arrays, wholes, outs, sums, flops, name):
    tokens = arrays[0].shape[0]
    block = min(256, tokens)

    def cut(shape):
        return pl.BlockSpec((block,) + shape[1:], lambda j: (j,) + (0,) * (len(shape) - 1))

    out_specs = [cut(shape) for shape, _ in outs]
    out_shape = [jax.ShapeDtypeStruct(shape, kind) for shape, kind in outs]
    if sums:
        out_specs.append(resident((8, sums)))
        out_shape.append(jax.ShapeDtypeStruct((8, sums), FULL))
    moved = sum(value.size * value.dtype.itemsize for value in list(arrays) + list(wholes) + out_shape)
    return pl.pallas_call(
        body,
        grid=(tokens // block,),
        in_specs=[cut(value.shape) for value in arrays] + [resident(value.shape) for value in wholes],
        out_specs=out_specs,
        out_shape=out_shape,
        compiler_params=params(),
        cost_estimate=cost(flops, moved),
        name=name,
    )(*arrays, *wholes)


def merge_and_normalize(attended, latents, merge, gate, shift, scale):
    tokens, depth = latents.shape

    def body(attended_ref, latents_ref, merge_ref, gate_ref, shift_ref, scale_ref, branch_ref, after_ref, normed_ref):
        branch = lax.dot_general(attended_ref[...], merge_ref[...], NT, preferred_element_type=FULL)
        after = latents_ref[...] + gate_ref[...] * branch
        branch_ref[...] = branch
        after_ref[...] = after
        normed_ref[...] = (
            standardize(after)[0] * (1.0 + scale_ref[...]) + shift_ref[...]
        ).astype(LOW)

    shape = (tokens, depth)
    return by_tokens(
        body,
        [attended, latents],
        [merge, gate, shift, scale],
        [(shape, FULL), (shape, FULL), (shape, LOW)],
        0,
        2 * tokens * depth * merge.shape[1],
        "merge_and_normalize",
    )


def second_back(grad, parts, after, branch, cotangent, merge, gate, scale, spans):
    tokens, depth = after.shape
    count = len(parts)

    def body(*refs):
        total = refs[0][...]
        for part_ref in refs[1 : 1 + count]:
            total = total + part_ref[...].astype(FULL)
        after_ref, branch_ref, cotangent_ref, merge_ref, gate_ref, scale_ref = refs[1 + count : 7 + count]
        grad_ref, low_ref = refs[7 + count : 9 + count]
        piece_refs, sums_ref = refs[9 + count : -1], refs[-1]
        resid, shift_grad, scale_grad = standardize_back(total, after_ref[...], scale_ref[...])
        after_grad = cotangent_ref[...] + resid
        low = (gate_ref[...] * after_grad).astype(LOW)
        grad_ref[...] = after_grad
        low_ref[...] = low
        back = jnp.dot(low, merge_ref[...], preferred_element_type=FULL).astype(LOW)
        for piece_ref, (start, end) in zip(piece_refs, spans):
            piece_ref[...] = back[:, start:end]
        store_sums(
            sums_ref,
            [jnp.sum(after_grad * branch_ref[...], axis=0, keepdims=True), shift_grad, scale_grad],
        )

    outs = [((tokens, depth), FULL), ((tokens, depth), LOW)]
    outs += [((tokens, end - start), LOW) for start, end in spans]
    results = by_tokens(
        body,
        [grad, *parts, after, branch, cotangent],
        [merge, gate, scale],
        outs,
        depth,
        2 * tokens * depth * merge.shape[1],
        "second_back",
    )
    return results[0], results[1], results[2:-1], results[-1]


def first_back(grad, parts, latents, after_grad, scale):
    tokens, depth = latents.shape
    count = len(parts)

    def body(*refs):
        total = refs[0][...]
        for part_ref in refs[1 : 1 + count]:
            total = total + part_ref[...].astype(FULL)
        latents_ref, after_ref, scale_ref, out_ref, sums_ref = refs[1 + count :]
        resid, shift_grad, scale_grad = standardize_back(total, latents_ref[...], scale_ref[...])
        store_lines(out_ref, after_ref[...] + resid)
        store_sums(sums_ref, [shift_grad, scale_grad])

    return by_tokens(
        body,
        [grad, *parts, latents, after_grad],
        [scale],
        [((tokens, depth // PAIR, PAIR), FULL)],
        depth,
        20 * tokens * depth,
        "first_back",
    )


def last_forward(branch, parts, after, cotangent, gate):
    tokens, depth = after.shape
    count = len(parts)

    def body(*refs):
        total = refs[0][...]
        for part_ref in refs[1 : 1 + count]:
            total = total + part_ref[...].astype(FULL)
        after_ref, cotangent_ref, gate_ref, out_ref, sums_ref = refs[1 + count :]
        store_lines(out_ref, after_ref[...] + gate_ref[...] * total)
        store_sums(sums_ref, [jnp.sum(cotangent_ref[...] * total, axis=0, keepdims=True)])

    return by_tokens(
        body,
        [branch, *parts, after, cotangent],
        [gate],
        [((tokens, depth // PAIR, PAIR), FULL)],
        depth,
        6 * tokens * depth,
        "last_forward",
    )


def adam_step(weight, first, second, grad_sum, rate):
    first_new = 0.9 * first + 0.1 * grad_sum
    second_new = 0.999 * second + 0.001 * grad_sum * grad_sum
    first_hat = first_new / (1.0 - 0.9**STEP)
    second_hat = second_new / (1.0 - 0.999**STEP)
    weight_new = weight - rate * (first_hat / (jnp.sqrt(second_hat) + 1e-08) + 0.01 * weight)
    return (weight_new, first_new, second_new)


def shift_tp(values, steps, count):
    steps = steps % count
    if steps == 0:
        return values
    return lax.ppermute(values, "tp", [(i, (i + steps) % count) for i in range(count)])


def digits(count):
    if count % 8 == 0:
        return 4, count // 8, 2
    return count // 2, 1, 2


def shift_fsdp(values, digit, steps, count):
    sizes = digits(count)
    scale = (sizes[1] * sizes[2], sizes[2], 1)[digit]
    size = sizes[digit]
    pairs = []
    for source in range(count):
        own = (source // scale) % size
        pairs.append((source, source + ((own + steps) % size - own) * scale))
    return lax.ppermute(values, "fsdp", pairs)


def arrange(pieces, count, group, by_z):
    deep, across, cores = digits(count)
    width = pieces[0].shape[1]
    tile = fit(width, 512)
    outer, inner = (deep, across) if by_z else (across, deep)

    def body(*refs):
        out_ref = refs[-1]
        me = lax.axis_index("fsdp")
        my_z, my_x, my_c = me // (across * cores), (me // cores) % across, me % cores
        for core in range(cores):
            for first in range(outer):
                source = refs[core * outer + first]
                for second in range(inner):
                    z, x = (first, second) if by_z else (second, first)
                    place = (
                        ((my_z - z + deep) % deep) * across + (my_x - x + across) % across
                    ) * cores + (my_c - core + cores) % cores
                    out_ref[pl.ds(pl.multiple_of(place * group, group), group), :] = source[
                        second * group : (second + 1) * group, :
                    ]

    return pl.pallas_call(
        body,
        grid=(width // tile,),
        in_specs=[pl.BlockSpec((piece.shape[0], tile), lambda j: (0, j)) for piece in pieces],
        out_specs=pl.BlockSpec((count * group, tile), lambda j: (0, j)),
        out_shape=jax.ShapeDtypeStruct((count * group, width), LOW),
        compiler_params=params(),
        cost_estimate=cost(0, 4 * count * group * width),
        name="arrange",
    )(*pieces)


def gather_z(shard, count):
    deep = digits(count)[0]
    return [shard] + [shift_fsdp(shard, 0, k, count) for k in range(1, deep)]


def gather_x(line, count):
    across = digits(count)[1]
    line = jnp.concatenate(line, axis=0)
    return [line] + [shift_fsdp(line, 1, k, count) for k in range(1, across)]


def gather_core(plane, count):
    cores = digits(count)[2]
    return plane + [shift_fsdp(piece, 2, k, count) for k in range(1, cores) for piece in plane]


def scatter_core(pair, count):
    kept, sent = pair
    return kept, shift_fsdp(sent, 2, 1, count)


def scatter_x(pair, count):
    kept, came = pair
    across = digits(count)[1]
    rows = kept.shape[0] // across

    def both(x):
        part = slice(x * rows, (x + 1) * rows)
        return kept[part].astype(FULL) + came[part].astype(FULL)

    return kept[:rows], came[:rows], [
        shift_fsdp(both(k).astype(LOW), 1, k, count) for k in range(1, across)
    ]


def scatter_z(state, count):
    kept, came, parts = state
    deep = digits(count)[0]
    group = kept.shape[0] // deep

    def both(z):
        rows = slice(z * group, (z + 1) * group)
        return sum(
            (part[rows].astype(FULL) for part in [came] + parts), start=kept[rows].astype(FULL)
        )

    return both(0), [shift_fsdp(both(k).astype(LOW), 0, k, count) for k in range(1, deep)]


def scatter_end(state):
    own, parts = state
    return sum((part.astype(FULL) for part in parts), start=own)


def gather_rows(shard):
    return lax.all_gather(shard, "fsdp", axis=0, tiled=True)


def scatter_rows(whole):
    return lax.psum_scatter(whole, "fsdp", scatter_dimension=0, tiled=True)


def together(*values):
    return lax.optimization_barrier(values)


def modulation_shares(grads, tp_count, fsdp_count, part):
    count = grads.shape[0]
    place = lax.axis_index("tp")
    total = sum(
        shift_tp(
            lax.dynamic_slice_in_dim(grads, (place + k) % tp_count * part, part, axis=1), k, tp_count
        )
        for k in range(tp_count)
    )
    every = lax.all_to_all(
        jnp.broadcast_to(total.reshape(1, count * part), (fsdp_count, count * part)),
        "fsdp",
        split_axis=0,
        concat_axis=0,
        tiled=True,
    )
    return every


def local(
    fsdp_count,
    tp_count,
    latents_in,
    condition,
    out_grad,
    condition_weight,
    condition_first,
    condition_second,
    heads_weight,
    heads_first,
    heads_second,
    merge_weight,
    merge_first,
    merge_second,
    up_weight,
    up_first,
    up_second,
    down_weight,
    down_first,
    down_second,
):
    own, _, depth = latents_in.shape
    shard_rows = condition_weight.shape[0]
    part = condition_weight.shape[2]
    width = heads_weight.shape[2]
    units = up_weight.shape[1]
    ring = range(tp_count)
    others = range(1, tp_count)

    def blocks_of_tokens(values):
        return [shift_tp(values, -k, tp_count) for k in ring]

    pairs = width // PAIR
    spans = [(0, pairs // 2), (pairs // 2, pairs)] if pairs > 1 else [(0, pairs)]
    spans = [(start * PAIR, end * PAIR) for start, end in spans]

    heads_low = jnp.moveaxis(heads_weight.astype(LOW), 0, 1)
    heads_shard = jnp.concatenate(
        [heads_low[:, :, start:end].reshape(shard_rows, -1) for start, end in spans], axis=1
    )
    activated = jax.nn.silu(condition).astype(LOW)
    activated, heads_shard = together(activated, heads_shard)
    heads_whole = gather_rows(heads_shard)
    activated_rows = lax.all_to_all(
        activated.reshape(fsdp_count, shard_rows), "fsdp", split_axis=0, concat_axis=0, tiled=True
    )
    latents, _ = together(latents_in.reshape(own, depth), heads_shard)
    (cotangent,) = together(out_grad.reshape(own, depth))

    unit_one, _ = standardize(latents)
    unit_blocks = blocks_of_tokens(unit_one.astype(LOW))
    shares = jnp.dot(
        activated_rows,
        condition_weight.astype(LOW).reshape(shard_rows, 6 * part),
        preferred_element_type=FULL,
    )
    shares = lax.all_to_all(shares, "fsdp", split_axis=0, concat_axis=0, tiled=True)
    feed_shard = jnp.concatenate([up_weight.astype(LOW), down_weight.astype(LOW).T], axis=1)
    shares, unit_blocks, cotangent = together(shares, unit_blocks, cotangent)
    modulation_part = jnp.sum(shares, axis=0).reshape(6, part)
    modulation = lax.all_gather(modulation_part, "tp", axis=1, tiled=True)
    modulation, merge_shard = together(modulation, merge_weight.astype(LOW).T)
    merge_shard = jnp.concatenate([shift_tp(merge_shard, k, tp_count) for k in ring], axis=1)
    merge_line = gather_z(merge_shard, fsdp_count)
    shift_one, scale_one, gate_one, shift_two, scale_two, gate_two = (
        modulation[k : k + 1] for k in range(6)
    )

    branch_grad = (gate_two * cotangent).astype(LOW)
    branch_grad_blocks = blocks_of_tokens(branch_grad)

    normed_one = jnp.concatenate(
        [
            ((unit_one if k == 0 else unit_blocks[k].astype(FULL)) * (1.0 + scale_one) + shift_one).astype(LOW)
            for k in ring
        ],
        axis=0,
    )
    heads_whole, feed_shard, normed_one, merge_line = together(
        heads_whole, feed_shard, normed_one, merge_line
    )
    feed_whole = gather_rows(feed_shard)
    triple = product(normed_one, heads_whole, LOW)
    triple, merge_line = together(triple, merge_line)
    merge_plane = gather_x(merge_line, fsdp_count)
    attended = []
    mixes = []
    for index, (start, end) in enumerate(spans):
        mixed, level = attend_forward(triple, 3 * start, end - start)
        if index == 0:
            mixed, merge_plane, branch_grad_blocks = together(mixed, merge_plane, branch_grad_blocks)
            merge_whole = arrange(gather_core(merge_plane, fsdp_count), fsdp_count, shard_rows, False)
        mixes.append((mixed, level))
        attended.append([shift_tp(mixed[k * own : (k + 1) * own], k, tp_count) for k in ring])
    attended_own = jnp.concatenate([part[k] for k in ring for part in attended], axis=1)
    attn_branch, after_attn, normed_two = merge_and_normalize(
        attended_own, latents, merge_whole, gate_one, shift_two, scale_two
    )
    normed_two_blocks = blocks_of_tokens(normed_two)

    mixes = [
        (mixed, probabilities(triple, 3 * start, level, end - start))
        for (mixed, level), (start, end) in zip(mixes, spans)
    ]
    normed_two_blocks, mixes = together(normed_two_blocks, mixes)
    fed = [None] + [feed_both(normed_two_blocks[k], branch_grad_blocks[k], feed_whole, LOW) for k in others]
    back_parts = [shift_tp(fed[k][1], k, tp_count) for k in others]
    normed_two, fed = together(normed_two, fed)
    fed[0] = feed_both(normed_two, branch_grad, feed_whole, FULL)
    fed, branch_parts = together(fed, [fed[k][0] for k in others])
    branch_parts = [shift_tp(values, k, tp_count) for k, values in zip(others, branch_parts)]
    (feed_grad,) = token_sum(
        [
            (normed_two_blocks, [fed[k][3] for k in ring]),
            (branch_grad_blocks, [fed[k][2] for k in ring]),
        ],
        fsdp_count,
        ordered=False,
    )
    back_parts, feed_grad = together(back_parts, feed_grad)
    feed_sum = scatter_rows(feed_grad)
    cuts = [(k * width + start, k * width + end) for k in ring for start, end in spans]
    after_grad, attn_grad, pieces, second_sums = second_back(
        fed[0][1], back_parts, after_attn, attn_branch, cotangent, merge_whole, gate_one, scale_two, cuts
    )
    pieces, branch_parts = together(pieces, branch_parts)
    attended_grads = []
    for index in range(len(spans)):
        mine = pieces[index :: len(spans)]
        if index:
            attended_grads, mine = together(attended_grads, mine)
        attended_grads.append(
            jnp.concatenate([shift_tp(mine[k], -k, tp_count) for k in ring], axis=0)
        )
    triple_grads = [
        attend_backward(triple, 0, *mixes[0], attended_grads[0], spans[0][1])
    ]
    triple_grads, attended_grads = together(triple_grads, attended_grads)
    pair = token_sum([([attn_grad], [attended_own]), ([normed_one], triple_grads)], fsdp_count)
    state = scatter_core(pair, fsdp_count)
    block_out, last_sums = last_forward(fed[0][0], branch_parts, after_attn, cotangent, gate_two)
    attended_grads, state, block_out = together(attended_grads, state, block_out)
    state = scatter_x(state, fsdp_count)
    for index in range(1, len(spans)):
        start, end = spans[index]
        triple_grads.append(
            attend_backward(triple, 3 * start, *mixes[index], attended_grads[index], end - start)
        )
    parts = [product_back(triple_grads, heads_whole, LOW, own, k) for k in others]
    one_parts = [shift_tp(values, k, tp_count) for k, values in zip(others, parts)]
    triple_grads, parts = together(triple_grads, parts)
    last = None
    if len(spans) > 1:
        last = token_sum([([normed_one], triple_grads[1:])], fsdp_count)
    triple_grads, last, state = together(triple_grads, last, state)
    state = scatter_z(state, fsdp_count)
    if last:
        last = scatter_core(last, fsdp_count)
    normed_one_grad = product_back(triple_grads, heads_whole, FULL, own, 0)
    one_parts, normed_one_grad, last = together(one_parts, normed_one_grad, last)
    if last:
        last = scatter_x(last, fsdp_count)
    latents_grad, first_sums = first_back(normed_one_grad, one_parts, latents, after_grad, scale_one)
    first_sums, last, feed_sum = together(first_sums, last, feed_sum)
    if last:
        last = scatter_z(last, fsdp_count)
    up_new = adam_step(up_weight, up_first, up_second, feed_sum[:, :units].astype(FULL), 0.02)
    down_new = adam_step(down_weight, down_first, down_second, feed_sum[:, units:].T.astype(FULL), 0.01)
    modulation_all = modulation_shares(
        jnp.concatenate([first_sums[:2], second_sums[:3], last_sums[:1]], axis=0),
        tp_count,
        fsdp_count,
        part,
    )
    modulation_all, state, last = together(modulation_all, state, last)
    first_sum = scatter_end(state)
    merge_sum_all, heads_sums = first_sum[:, : tp_count * width], [first_sum[:, tp_count * width :]]
    if last:
        heads_sums.append(scatter_end(last))
    heads_sums = [total.reshape(shard_rows, 3, -1) for total in heads_sums]
    condition_sum = lax.dot_general(
        activated_rows.astype(FULL),
        modulation_all,
        TN,
        precision=lax.Precision.HIGHEST,
        preferred_element_type=FULL,
    ).reshape(shard_rows, 6, part)
    merge_sum = merge_sum_all[:, :width]
    for k in others:
        merge_sum = merge_sum + shift_tp(
            merge_sum_all[:, k * width : (k + 1) * width], -k, tp_count
        )
    heads_sum = jnp.moveaxis(jnp.concatenate(heads_sums, axis=2), 1, 0)
    cond_new = adam_step(condition_weight, condition_first, condition_second, condition_sum, 0.02)
    heads_new = adam_step(heads_weight, heads_first, heads_second, heads_sum, 0.02)
    merge_new = adam_step(merge_weight, merge_first, merge_second, merge_sum.T, 0.15)
    return (
        block_out.reshape(own, 1, depth),
        latents_grad.reshape(own, 1, depth),
        *cond_new,
        *heads_new,
        *merge_new,
        *up_new,
        *down_new,
    )


def solution(mesh):
    stream = P("tp", "fsdp", None)
    cond = P("fsdp", None, "tp")
    heads = P(None, "fsdp", "tp")
    wide = P("tp", "fsdp")
    tall = P("fsdp", "tp")
    in_specs = (stream, P("fsdp", None), stream) + (cond,) * 3 + (heads,) * 3 + (wide,) * 3 + (tall,) * 3 + (wide,) * 3
    out_specs = (stream, stream) + (cond,) * 3 + (heads,) * 3 + (wide,) * 3 + (tall,) * 3 + (wide,) * 3
    return jax.shard_map(
        functools.partial(local, mesh.shape["fsdp"], mesh.shape["tp"]),
        mesh=mesh,
        in_specs=in_specs,
        out_specs=out_specs,
        check_vma=False,
    )
```

```python
import functools

import jax
import jax.numpy as jnp
from jax import lax
from jax.experimental import pallas as pl
from jax.experimental.pallas import tpu as pltpu
from jax.sharding import PartitionSpec as P

HEAD = 64
PAIR = 2 * HEAD
STEP = 5
LOW = jnp.bfloat16
FULL = jnp.float32
NT = (((1,), (1,)), ((), ()))
TN = (((0,), (0,)), ((), ()))


def params(limit=56):
    return pltpu.CompilerParams(vmem_limit_bytes=limit * 1024 * 1024)


def cost(flops, moved, raised=0):
    return pl.CostEstimate(flops=int(flops), bytes_accessed=int(moved), transcendentals=int(raised))


def resident(shape):
    return pl.BlockSpec(shape, lambda *step: (0,) * len(shape))


def fit(width, most):
    return next(tile for tile in (most, 512, 256, PAIR) if tile <= most and width % tile == 0)


def product(left, right, out_type):
    rows, depth = left.shape
    width = right.shape[1]
    tile = fit(width, 512)

    def body(left_ref, right_ref, out_ref):
        out_ref[...] = jnp.dot(
            left_ref[...], right_ref[...], preferred_element_type=FULL
        ).astype(out_type)

    return pl.pallas_call(
        body,
        grid=(width // tile,),
        in_specs=[
            resident((rows, depth)),
            pl.BlockSpec((depth, tile), lambda j: (0, j)),
        ],
        out_specs=pl.BlockSpec((rows, tile), lambda j: (0, j)),
        out_shape=jax.ShapeDtypeStruct((rows, width), out_type),
        compiler_params=params(),
        cost_estimate=cost(2 * rows * depth * width, 2 * (rows * depth + depth * width) + 4 * rows * width),
        name="product",
    )(left, right)


def product_back(lefts, right, out_type, rows, part):
    width, depth = right.shape
    tile = min(256, width)

    def body(*refs):
        total = None
        start = 0
        for left_ref in refs[:-2]:
            extent = left_ref.shape[1]
            term = lax.dot_general(
                left_ref[...], refs[-2][:, start : start + extent], NT, preferred_element_type=FULL
            )
            total = term if total is None else total + term
            start += extent
        refs[-1][...] = total.astype(out_type)

    return pl.pallas_call(
        body,
        grid=(width // tile,),
        in_specs=[pl.BlockSpec((rows, left.shape[1]), lambda j: (part, 0)) for left in lefts]
        + [pl.BlockSpec((tile, depth), lambda j: (j, 0))],
        out_specs=pl.BlockSpec((rows, tile), lambda j: (0, j)),
        out_shape=jax.ShapeDtypeStruct((rows, width), out_type),
        compiler_params=params(),
        cost_estimate=cost(2 * rows * depth * width, 2 * (rows * depth + width * depth) + 4 * rows * width),
        name="product_back",
    )(*lefts, right)


def token_sum(jobs, count, ordered=True):
    depth = jobs[0][0][0].shape[1]
    widths = [rights[0].shape[1] for _, rights in jobs]
    width = sum(widths)
    tokens = max(sum(left.shape[0] for left in lefts) for lefts, _ in jobs)
    tile = min(fit(extent, 512) for extent in widths)
    deep, across, cores = digits(count)
    group = depth // count
    pieces = len(jobs[0][0])
    starts = [sum(widths[:index]) // tile for index in range(len(jobs) + 1)]

    def flip(left_refs, turned):
        me = lax.axis_index("fsdp")
        my_z, my_x, my_c = me // (across * cores), (me // cores) % across, me % cores
        start = 0
        for left_ref in left_refs:
            flipped = left_ref[...].T
            extent = left_ref.shape[0]
            if not ordered:
                turned[:, start : start + extent] = flipped
            for source in range(count if ordered else 0):
                z, x, c = source // (across * cores), (source // cores) % across, source % cores
                place = (
                    ((c - my_c + cores) % cores) * across + (x - my_x + across) % across
                ) * deep + (z - my_z + deep) % deep
                turned[pl.ds(pl.multiple_of(place * group, group), group), start : start + extent] = (
                    flipped[source * group : (source + 1) * group]
                )
            start += extent

    def body(*refs):
        out_refs, turned = refs[2 * pieces * len(jobs) : -1], refs[-1]
        step = pl.program_id(0)
        for index in range(len(jobs)):
            mine = refs[2 * pieces * index : 2 * pieces * (index + 1)]

            @pl.when(step == starts[index])
            def _():
                flip(mine[:pieces], turned)

            @pl.when((step >= starts[index]) & (step < starts[index + 1]))
            def _():
                total = None
                start = 0
                for right_ref in mine[pieces:]:
                    extent = right_ref.shape[0]
                    term = jnp.dot(
                        turned[:, start : start + extent], right_ref[...], preferred_element_type=FULL
                    )
                    total = term if total is None else total + term
                    start += extent
                total = total.astype(LOW)
                start = 0
                for out_ref in out_refs:
                    out_ref[...] = total[start : start + out_ref.shape[0]]
                    start += out_ref.shape[0]

    def place_of(index):
        last = widths[index] // tile - 1
        return lambda j: (0, jnp.clip(j - starts[index], 0, last))

    half = depth // cores
    heights = (half, depth - half) if ordered else (depth,)
    in_specs = []
    operands = []
    for index, (lefts, rights) in enumerate(jobs):
        in_specs += [resident(left.shape) for left in lefts]
        in_specs += [pl.BlockSpec((right.shape[0], tile), place_of(index)) for right in rights]
        operands += [*lefts, *rights]
    return pl.pallas_call(
        body,
        grid=(width // tile,),
        in_specs=in_specs,
        out_specs=[pl.BlockSpec((height, tile), lambda j: (0, j)) for height in heights],
        out_shape=[jax.ShapeDtypeStruct((height, width), LOW) for height in heights],
        scratch_shapes=[pltpu.VMEM((depth, tokens), LOW)],
        compiler_params=params(),
        cost_estimate=cost(
            2 * depth * tokens * width, 2 * (len(jobs) * depth * tokens + tokens * width + depth * width)
        ),
        name="token_sum",
    )(*operands)


def head_lanes():
    lane = lax.broadcasted_iota(jnp.int32, (1, PAIR), 1)
    first = (lane < HEAD).astype(FULL)
    return lane, ((first, HEAD), (1.0 - first, 0))


def in_lanes(lane, free, column):
    total = 0.0
    for index in range(3):
        piece = column.astype(LOW).astype(FULL)
        total = total + jnp.where(lane == free + index, piece, 0.0)
        column = column - piece
    return total


def ones_in_lanes(lane, free, values):
    return jnp.where((lane >= free) & (lane < free + 3), 1.0, values.astype(FULL)).astype(LOW)


def attend_forward(triple, start, width):
    tokens = triple.shape[0]
    pairs = width // PAIR
    first = start // PAIR
    block = min(512, tokens)
    scaling = HEAD ** (-0.5)

    def body(query_ref, keys_ref, values_ref, out_ref, level_ref):
        lane, heads = head_lanes()
        keys = keys_ref[...]
        values = values_ref[...].astype(FULL)
        query = query_ref[...].astype(FULL)
        total = level = 0.0
        for mask, free in heads:
            scores = lax.dot_general(
                (query * (mask * scaling)).astype(LOW), keys, NT, preferred_element_type=FULL
            )
            peak = jnp.max(scores, axis=-1, keepdims=True)
            raised = jnp.exp(scores - peak).astype(LOW)
            counted = jnp.where(lane == free, 1.0, values * mask).astype(LOW)
            mixed = jnp.dot(raised, counted, preferred_element_type=FULL)
            sums = mixed[:, free : free + 1]
            total = total + mixed * mask / sums
            level = level + mask * (peak + jnp.log(sums))
        out_ref[...] = total.astype(LOW)
        level_ref[...] = level

    return pl.pallas_call(
        body,
        grid=(pairs, tokens // block),
        in_specs=[
            pl.BlockSpec((block, PAIR), lambda h, i: (i, first + h)),
            pl.BlockSpec((tokens, PAIR), lambda h, i: (0, first + pairs + h)),
            pl.BlockSpec((tokens, PAIR), lambda h, i: (0, first + 2 * pairs + h)),
        ],
        out_specs=[pl.BlockSpec((block, PAIR), lambda h, i: (i, h))] * 2,
        out_shape=[
            jax.ShapeDtypeStruct((tokens, width), LOW),
            jax.ShapeDtypeStruct((tokens, width), FULL),
        ],
        compiler_params=params(),
        cost_estimate=cost(16 * tokens * tokens * width, 12 * tokens * width, tokens * tokens * width // HEAD),
        name="attend_forward",
    )(triple, triple, triple)


def probabilities(triple, start, level, width):
    tokens = triple.shape[0]
    pairs = width // PAIR
    first = start // PAIR
    block = min(512, tokens)
    scaling = HEAD ** (-0.5)

    def body(query_ref, keys_ref, level_ref, out_ref):
        lane, heads = head_lanes()
        keys = keys_ref[...]
        query = query_ref[...].astype(FULL)
        for index, (mask, free) in enumerate(heads):
            own = HEAD * index
            scores = lax.dot_general(
                ones_in_lanes(lane, free, keys),
                (
                    query * (mask * scaling) - in_lanes(lane, free, level_ref[:, own : own + 1])
                ).astype(LOW),
                NT,
                preferred_element_type=FULL,
            )
            out_ref[0, index] = jnp.exp(scores).astype(LOW)

    return pl.pallas_call(
        body,
        grid=(pairs, tokens // block),
        in_specs=[
            pl.BlockSpec((block, PAIR), lambda h, i: (i, first + h)),
            pl.BlockSpec((tokens, PAIR), lambda h, i: (0, first + pairs + h)),
            pl.BlockSpec((block, PAIR), lambda h, i: (i, h)),
        ],
        out_specs=pl.BlockSpec((1, 2, tokens, block), lambda h, i: (h, 0, 0, i)),
        out_shape=jax.ShapeDtypeStruct((pairs, 2, tokens, tokens), LOW),
        compiler_params=params(),
        cost_estimate=cost(4 * tokens * tokens * width, 4 * pairs * tokens * tokens, tokens * tokens * width // HEAD),
        name="probabilities",
    )(triple, triple, level)


def attend_backward(triple, start, attended, probs, grads, width):
    tokens = triple.shape[0]
    pairs = width // PAIR
    first = start // PAIR
    block = min(512, tokens)
    steps = tokens // block
    scaling = HEAD ** (-0.5)

    def body(query_ref, keys_ref, values_ref, out_low_ref, probs_ref, grad_ref, out_ref, key_sum, value_sum):
        pair = pl.program_id(0)
        step = pl.program_id(1)
        lane, heads = head_lanes()
        keys = keys_ref[...]
        values = values_ref[...]
        query = query_ref[...].astype(FULL)
        grad = grad_ref[...].astype(FULL)
        inner = grad * out_low_ref[...].astype(FULL)
        query_grad = key_grad = value_grad = None
        for index, (mask, free) in enumerate(heads):
            query_part = (query * (mask * scaling)).astype(LOW)
            grad_part = grad * mask
            probs = probs_ref[0, index]
            prob_grad = lax.dot_general(
                ones_in_lanes(lane, free, values),
                (
                    grad_part - in_lanes(lane, free, jnp.sum(inner * mask, axis=-1, keepdims=True))
                ).astype(LOW),
                NT,
                preferred_element_type=FULL,
            )
            score_grad = (probs.astype(FULL) * prob_grad).astype(LOW)
            value_part = jnp.dot(probs, grad_part.astype(LOW), preferred_element_type=FULL)
            key_part = jnp.dot(score_grad, query_part, preferred_element_type=FULL)
            asked_part = lax.dot_general(
                score_grad, keys * (mask * scaling).astype(LOW), TN, preferred_element_type=FULL
            )
            if query_grad is None:
                query_grad, key_grad, value_grad = asked_part, key_part, value_part
            else:
                query_grad, key_grad, value_grad = (
                    query_grad + asked_part,
                    key_grad + key_part,
                    value_grad + value_part,
                )

        @pl.when(step == 0)
        def _():
            key_sum[...] = key_grad
            value_sum[...] = value_grad

        @pl.when(step > 0)
        def _():
            key_sum[...] += key_grad
            value_sum[...] += value_grad

        rows = pl.ds(pl.multiple_of(step * block, block), block)
        out_ref[rows, pl.ds(pl.multiple_of(pair * PAIR, PAIR), PAIR)] = query_grad.astype(LOW)

        @pl.when(step == steps - 1)
        def _():
            out_ref[:, pl.ds(pl.multiple_of(width + pair * PAIR, PAIR), PAIR)] = key_sum[...].astype(LOW)
            out_ref[:, pl.ds(pl.multiple_of(2 * width + pair * PAIR, PAIR), PAIR)] = value_sum[
                ...
            ].astype(LOW)

    rows_of_pair = pl.BlockSpec((block, PAIR), lambda h, i: (i, h))
    return pl.pallas_call(
        body,
        grid=(pairs, steps),
        in_specs=[
            pl.BlockSpec((block, PAIR), lambda h, i: (i, first + h)),
            pl.BlockSpec((tokens, PAIR), lambda h, i: (0, first + pairs + h)),
            pl.BlockSpec((tokens, PAIR), lambda h, i: (0, first + 2 * pairs + h)),
            rows_of_pair,
            pl.BlockSpec((1, 2, tokens, block), lambda h, i: (h, 0, 0, i)),
            rows_of_pair,
        ],
        out_specs=resident((tokens, 3 * width)),
        out_shape=jax.ShapeDtypeStruct((tokens, 3 * width), LOW),
        scratch_shapes=[pltpu.VMEM((tokens, PAIR), FULL), pltpu.VMEM((tokens, PAIR), FULL)],
        compiler_params=params(),
        cost_estimate=cost(32 * tokens * tokens * width, 20 * tokens * width + 4 * pairs * tokens * tokens),
        name="attend_backward",
    )(triple, triple, triple, attended, probs, grads)


def feed_both(normed, branch_grad, weights, out_type):
    tokens, depth = normed.shape
    units = weights.shape[1] // 2
    tile = min(512, units)
    steps = units // tile

    def body(normed_ref, grad_ref, up_ref, down_ref, out_ref, back_ref, hidden_ref, pre_ref, out_sum, back_sum):
        step = pl.program_id(0)
        up = up_ref[...]
        down = down_ref[...]
        pre = jnp.dot(normed_ref[...], up, preferred_element_type=FULL)
        hidden_grad = jnp.dot(grad_ref[...], down, preferred_element_type=FULL)
        square = pre * pre
        bent = jnp.tanh(0.7978845608028654 * (pre + 0.044715 * (square * pre)))
        half = 0.5 * (1.0 + bent)
        hidden = (pre * half).astype(LOW)
        slope = half + 0.5 * pre * (1.0 - bent * bent) * (
            0.7978845608028654 * (1.0 + 0.134145 * square)
        )
        pre_grad = (hidden_grad * slope).astype(LOW)
        hidden_ref[...] = hidden
        pre_ref[...] = pre_grad
        out_part = lax.dot_general(hidden, down, NT, preferred_element_type=FULL)
        back_part = lax.dot_general(pre_grad, up, NT, preferred_element_type=FULL)

        @pl.when(step == 0)
        def _():
            out_sum[...] = out_part
            back_sum[...] = back_part

        @pl.when(step > 0)
        def _():
            out_sum[...] += out_part
            back_sum[...] += back_part

        @pl.when(step == steps - 1)
        def _():
            out_ref[...] = out_sum[...].astype(out_type)
            back_ref[...] = back_sum[...].astype(out_type)

    return pl.pallas_call(
        body,
        grid=(steps,),
        in_specs=[
            resident((tokens, depth)),
            resident((tokens, depth)),
            pl.BlockSpec((depth, tile), lambda j: (0, j)),
            pl.BlockSpec((depth, tile), lambda j: (0, steps + j)),
        ],
        out_specs=[
            resident((tokens, depth)),
            resident((tokens, depth)),
            pl.BlockSpec((tokens, tile), lambda j: (0, j)),
            pl.BlockSpec((tokens, tile), lambda j: (0, j)),
        ],
        out_shape=[
            jax.ShapeDtypeStruct((tokens, depth), out_type),
            jax.ShapeDtypeStruct((tokens, depth), out_type),
            jax.ShapeDtypeStruct((tokens, units), LOW),
            jax.ShapeDtypeStruct((tokens, units), LOW),
        ],
        scratch_shapes=[pltpu.VMEM((tokens, depth), FULL), pltpu.VMEM((tokens, depth), FULL)],
        compiler_params=params(),
        cost_estimate=cost(8 * tokens * depth * units, 4 * depth * units + 12 * tokens * depth + 4 * tokens * units, tokens * units),
        name="feed_both",
    )(normed, branch_grad, weights, weights)


def standardize(values):
    middle = jnp.mean(values, axis=-1, keepdims=True)
    centred = values - middle
    spread = jnp.mean(centred * centred, axis=-1, keepdims=True)
    rate = lax.rsqrt(spread + 1e-06)
    return centred * rate, rate


def standardize_back(grad, values, scale_term):
    unit, rate = standardize(values)
    pulled = grad * (1.0 + scale_term)
    resid = rate * (
        pulled
        - jnp.mean(pulled, axis=-1, keepdims=True)
        - unit * jnp.mean(pulled * unit, axis=-1, keepdims=True)
    )
    return resid, jnp.sum(grad, axis=0, keepdims=True), jnp.sum(grad * unit, axis=0, keepdims=True)


def store_sums(sums_ref, rows):
    @pl.when(pl.program_id(0) == 0)
    def _():
        sums_ref[...] = jnp.zeros_like(sums_ref)

    for index, row in enumerate(rows):
        sums_ref[index : index + 1, :] += row


def store_lines(out_ref, values):
    for index in range(out_ref.shape[1]):
        out_ref[:, index, :] = values[:, index * PAIR : (index + 1) * PAIR]


def by_tokens(body, arrays, wholes, outs, sums, flops, name):
    tokens = arrays[0].shape[0]
    block = min(256, tokens)

    def cut(shape):
        return pl.BlockSpec((block,) + shape[1:], lambda j: (j,) + (0,) * (len(shape) - 1))

    out_specs = [cut(shape) for shape, _ in outs]
    out_shape = [jax.ShapeDtypeStruct(shape, kind) for shape, kind in outs]
    if sums:
        out_specs.append(resident((8, sums)))
        out_shape.append(jax.ShapeDtypeStruct((8, sums), FULL))
    moved = sum(value.size * value.dtype.itemsize for value in list(arrays) + list(wholes) + out_shape)
    return pl.pallas_call(
        body,
        grid=(tokens // block,),
        in_specs=[cut(value.shape) for value in arrays] + [resident(value.shape) for value in wholes],
        out_specs=out_specs,
        out_shape=out_shape,
        compiler_params=params(),
        cost_estimate=cost(flops, moved),
        name=name,
    )(*arrays, *wholes)


def merge_and_normalize(attended, latents, merge, gate, shift, scale):
    tokens, depth = latents.shape

    def body(attended_ref, latents_ref, merge_ref, gate_ref, shift_ref, scale_ref, branch_ref, after_ref, normed_ref):
        branch = lax.dot_general(attended_ref[...], merge_ref[...], NT, preferred_element_type=FULL)
        after = latents_ref[...] + gate_ref[...] * branch
        branch_ref[...] = branch
        after_ref[...] = after
        normed_ref[...] = (
            standardize(after)[0] * (1.0 + scale_ref[...]) + shift_ref[...]
        ).astype(LOW)

    shape = (tokens, depth)
    return by_tokens(
        body,
        [attended, latents],
        [merge, gate, shift, scale],
        [(shape, FULL), (shape, FULL), (shape, LOW)],
        0,
        2 * tokens * depth * merge.shape[1],
        "merge_and_normalize",
    )


def second_back(grad, parts, after, branch, cotangent, merge, gate, scale, spans):
    tokens, depth = after.shape
    count = len(parts)

    def body(*refs):
        total = refs[0][...]
        for part_ref in refs[1 : 1 + count]:
            total = total + part_ref[...].astype(FULL)
        after_ref, branch_ref, cotangent_ref, merge_ref, gate_ref, scale_ref = refs[1 + count : 7 + count]
        grad_ref, low_ref = refs[7 + count : 9 + count]
        piece_refs, sums_ref = refs[9 + count : -1], refs[-1]
        resid, shift_grad, scale_grad = standardize_back(total, after_ref[...], scale_ref[...])
        after_grad = cotangent_ref[...] + resid
        low = (gate_ref[...] * after_grad).astype(LOW)
        grad_ref[...] = after_grad
        low_ref[...] = low
        back = jnp.dot(low, merge_ref[...], preferred_element_type=FULL).astype(LOW)
        for piece_ref, (start, end) in zip(piece_refs, spans):
            piece_ref[...] = back[:, start:end]
        store_sums(
            sums_ref,
            [jnp.sum(after_grad * branch_ref[...], axis=0, keepdims=True), shift_grad, scale_grad],
        )

    outs = [((tokens, depth), FULL), ((tokens, depth), LOW)]
    outs += [((tokens, end - start), LOW) for start, end in spans]
    results = by_tokens(
        body,
        [grad, *parts, after, branch, cotangent],
        [merge, gate, scale],
        outs,
        depth,
        2 * tokens * depth * merge.shape[1],
        "second_back",
    )
    return results[0], results[1], results[2:-1], results[-1]


def first_back(grad, parts, latents, after_grad, scale):
    tokens, depth = latents.shape
    count = len(parts)

    def body(*refs):
        total = refs[0][...]
        for part_ref in refs[1 : 1 + count]:
            total = total + part_ref[...].astype(FULL)
        latents_ref, after_ref, scale_ref, out_ref, sums_ref = refs[1 + count :]
        resid, shift_grad, scale_grad = standardize_back(total, latents_ref[...], scale_ref[...])
        store_lines(out_ref, after_ref[...] + resid)
        store_sums(sums_ref, [shift_grad, scale_grad])

    return by_tokens(
        body,
        [grad, *parts, latents, after_grad],
        [scale],
        [((tokens, depth // PAIR, PAIR), FULL)],
        depth,
        20 * tokens * depth,
        "first_back",
    )


def last_forward(branch, parts, after, cotangent, gate):
    tokens, depth = after.shape
    count = len(parts)

    def body(*refs):
        total = refs[0][...]
        for part_ref in refs[1 : 1 + count]:
            total = total + part_ref[...].astype(FULL)
        after_ref, cotangent_ref, gate_ref, out_ref, sums_ref = refs[1 + count :]
        store_lines(out_ref, after_ref[...] + gate_ref[...] * total)
        store_sums(sums_ref, [jnp.sum(cotangent_ref[...] * total, axis=0, keepdims=True)])

    return by_tokens(
        body,
        [branch, *parts, after, cotangent],
        [gate],
        [((tokens, depth // PAIR, PAIR), FULL)],
        depth,
        6 * tokens * depth,
        "last_forward",
    )


def adam_step(weight, first, second, grad_sum, rate):
    first_new = 0.9 * first + 0.1 * grad_sum
    second_new = 0.999 * second + 0.001 * grad_sum * grad_sum
    first_hat = first_new / (1.0 - 0.9**STEP)
    second_hat = second_new / (1.0 - 0.999**STEP)
    weight_new = weight - rate * (first_hat / (jnp.sqrt(second_hat) + 1e-08) + 0.01 * weight)
    return (weight_new, first_new, second_new)


def shift_tp(values, steps, count):
    steps = steps % count
    if steps == 0:
        return values
    return lax.ppermute(values, "tp", [(i, (i + steps) % count) for i in range(count)])


def digits(count):
    if count % 8 == 0:
        return 4, count // 8, 2
    return count // 2, 1, 2


def shift_fsdp(values, digit, steps, count):
    sizes = digits(count)
    scale = (sizes[1] * sizes[2], sizes[2], 1)[digit]
    size = sizes[digit]
    pairs = []
    for source in range(count):
        own = (source // scale) % size
        pairs.append((source, source + ((own + steps) % size - own) * scale))
    return lax.ppermute(values, "fsdp", pairs)


def arrange(pieces, count, group, by_z):
    deep, across, cores = digits(count)
    width = pieces[0].shape[1]
    tile = fit(width, 512)
    outer, inner = (deep, across) if by_z else (across, deep)

    def body(*refs):
        out_ref = refs[-1]
        me = lax.axis_index("fsdp")
        my_z, my_x, my_c = me // (across * cores), (me // cores) % across, me % cores
        for core in range(cores):
            for first in range(outer):
                source = refs[core * outer + first]
                for second in range(inner):
                    z, x = (first, second) if by_z else (second, first)
                    place = (
                        ((my_z - z + deep) % deep) * across + (my_x - x + across) % across
                    ) * cores + (my_c - core + cores) % cores
                    out_ref[pl.ds(pl.multiple_of(place * group, group), group), :] = source[
                        second * group : (second + 1) * group, :
                    ]

    return pl.pallas_call(
        body,
        grid=(width // tile,),
        in_specs=[pl.BlockSpec((piece.shape[0], tile), lambda j: (0, j)) for piece in pieces],
        out_specs=pl.BlockSpec((count * group, tile), lambda j: (0, j)),
        out_shape=jax.ShapeDtypeStruct((count * group, width), LOW),
        compiler_params=params(),
        cost_estimate=cost(0, 4 * count * group * width),
        name="arrange",
    )(*pieces)


def gather_z(shard, count):
    deep = digits(count)[0]
    return [shard] + [shift_fsdp(shard, 0, k, count) for k in range(1, deep)]


def gather_x(line, count):
    across = digits(count)[1]
    line = jnp.concatenate(line, axis=0)
    return [line] + [shift_fsdp(line, 1, k, count) for k in range(1, across)]


def gather_core(plane, count):
    cores = digits(count)[2]
    return plane + [shift_fsdp(piece, 2, k, count) for k in range(1, cores) for piece in plane]


def scatter_core(pair, count):
    kept, sent = pair
    return kept, shift_fsdp(sent, 2, 1, count)


def scatter_x(pair, count):
    kept, came = pair
    across = digits(count)[1]
    rows = kept.shape[0] // across

    def both(x):
        part = slice(x * rows, (x + 1) * rows)
        return kept[part].astype(FULL) + came[part].astype(FULL)

    return kept[:rows], came[:rows], [
        shift_fsdp(both(k).astype(LOW), 1, k, count) for k in range(1, across)
    ]


def scatter_z(state, count):
    kept, came, parts = state
    deep = digits(count)[0]
    group = kept.shape[0] // deep

    def both(z):
        rows = slice(z * group, (z + 1) * group)
        return sum(
            (part[rows].astype(FULL) for part in [came] + parts), start=kept[rows].astype(FULL)
        )

    return both(0), [shift_fsdp(both(k).astype(LOW), 0, k, count) for k in range(1, deep)]


def scatter_end(state):
    own, parts = state
    return sum((part.astype(FULL) for part in parts), start=own)


def gather_rows(shard):
    return lax.all_gather(shard, "fsdp", axis=0, tiled=True)


def scatter_rows(whole):
    return lax.psum_scatter(whole, "fsdp", scatter_dimension=0, tiled=True)


def together(*values):
    return lax.optimization_barrier(values)


def modulation_shares(grads, tp_count, fsdp_count, part):
    count = grads.shape[0]
    place = lax.axis_index("tp")
    total = sum(
        shift_tp(
            lax.dynamic_slice_in_dim(grads, (place + k) % tp_count * part, part, axis=1), k, tp_count
        )
        for k in range(tp_count)
    )
    every = lax.all_to_all(
        jnp.broadcast_to(total.reshape(1, count * part), (fsdp_count, count * part)),
        "fsdp",
        split_axis=0,
        concat_axis=0,
        tiled=True,
    )
    return every


def local(
    fsdp_count,
    tp_count,
    latents_in,
    condition,
    out_grad,
    condition_weight,
    condition_first,
    condition_second,
    heads_weight,
    heads_first,
    heads_second,
    merge_weight,
    merge_first,
    merge_second,
    up_weight,
    up_first,
    up_second,
    down_weight,
    down_first,
    down_second,
):
    own, _, depth = latents_in.shape
    shard_rows = condition_weight.shape[0]
    part = condition_weight.shape[2]
    width = heads_weight.shape[2]
    units = up_weight.shape[1]
    ring = range(tp_count)
    others = range(1, tp_count)

    def blocks_of_tokens(values):
        return [shift_tp(values, -k, tp_count) for k in ring]

    pairs = width // PAIR
    spans = [(0, pairs // 2), (pairs // 2, pairs)] if pairs > 1 else [(0, pairs)]
    spans = [(start * PAIR, end * PAIR) for start, end in spans]

    heads_low = jnp.moveaxis(heads_weight.astype(LOW), 0, 1)
    heads_shard = jnp.concatenate(
        [heads_low[:, :, start:end].reshape(shard_rows, -1) for start, end in spans], axis=1
    )
    activated = jax.nn.silu(condition).astype(LOW)
    activated, heads_shard = together(activated, heads_shard)
    heads_whole = gather_rows(heads_shard)
    activated_rows = lax.all_to_all(
        activated.reshape(fsdp_count, shard_rows), "fsdp", split_axis=0, concat_axis=0, tiled=True
    )
    latents, _ = together(latents_in.reshape(own, depth), heads_shard)
    (cotangent,) = together(out_grad.reshape(own, depth))

    unit_one, _ = standardize(latents)
    unit_blocks = blocks_of_tokens(unit_one.astype(LOW))
    shares = jnp.dot(
        activated_rows,
        condition_weight.astype(LOW).reshape(shard_rows, 6 * part),
        preferred_element_type=FULL,
    )
    shares = lax.all_to_all(shares, "fsdp", split_axis=0, concat_axis=0, tiled=True)
    feed_shard = jnp.concatenate([up_weight.astype(LOW), down_weight.astype(LOW).T], axis=1)
    shares, unit_blocks, cotangent = together(shares, unit_blocks, cotangent)
    modulation_part = jnp.sum(shares, axis=0).reshape(6, part)
    modulation = lax.all_gather(modulation_part, "tp", axis=1, tiled=True)
    modulation, merge_shard = together(modulation, merge_weight.astype(LOW).T)
    merge_shard = jnp.concatenate([shift_tp(merge_shard, k, tp_count) for k in ring], axis=1)
    merge_line = gather_z(merge_shard, fsdp_count)
    shift_one, scale_one, gate_one, shift_two, scale_two, gate_two = (
        modulation[k : k + 1] for k in range(6)
    )

    branch_grad = (gate_two * cotangent).astype(LOW)
    branch_grad_blocks = blocks_of_tokens(branch_grad)

    normed_one = jnp.concatenate(
        [
            ((unit_one if k == 0 else unit_blocks[k].astype(FULL)) * (1.0 + scale_one) + shift_one).astype(LOW)
            for k in ring
        ],
        axis=0,
    )
    heads_whole, feed_shard, normed_one, merge_line = together(
        heads_whole, feed_shard, normed_one, merge_line
    )
    feed_whole = gather_rows(feed_shard)
    triple = product(normed_one, heads_whole, LOW)
    triple, merge_line = together(triple, merge_line)
    merge_plane = gather_x(merge_line, fsdp_count)
    attended = []
    mixes = []
    for index, (start, end) in enumerate(spans):
        mixed, level = attend_forward(triple, 3 * start, end - start)
        if index == 0:
            mixed, merge_plane, branch_grad_blocks = together(mixed, merge_plane, branch_grad_blocks)
            merge_whole = arrange(gather_core(merge_plane, fsdp_count), fsdp_count, shard_rows, False)
        mixes.append((mixed, level))
        attended.append([shift_tp(mixed[k * own : (k + 1) * own], k, tp_count) for k in ring])
    attended_own = jnp.concatenate([part[k] for k in ring for part in attended], axis=1)
    attn_branch, after_attn, normed_two = merge_and_normalize(
        attended_own, latents, merge_whole, gate_one, shift_two, scale_two
    )
    normed_two_blocks = blocks_of_tokens(normed_two)

    mixes = [
        (mixed, probabilities(triple, 3 * start, level, end - start))
        for (mixed, level), (start, end) in zip(mixes, spans)
    ]
    normed_two_blocks, mixes = together(normed_two_blocks, mixes)
    fed = [None] + [feed_both(normed_two_blocks[k], branch_grad_blocks[k], feed_whole, LOW) for k in others]
    back_parts = [shift_tp(fed[k][1], k, tp_count) for k in others]
    normed_two, fed = together(normed_two, fed)
    fed[0] = feed_both(normed_two, branch_grad, feed_whole, FULL)
    fed, branch_parts = together(fed, [fed[k][0] for k in others])
    branch_parts = [shift_tp(values, k, tp_count) for k, values in zip(others, branch_parts)]
    (feed_grad,) = token_sum(
        [
            (normed_two_blocks, [fed[k][3] for k in ring]),
            (branch_grad_blocks, [fed[k][2] for k in ring]),
        ],
        fsdp_count,
        ordered=False,
    )
    back_parts, feed_grad = together(back_parts, feed_grad)
    feed_sum = scatter_rows(feed_grad)
    cuts = [(k * width + start, k * width + end) for k in ring for start, end in spans]
    after_grad, attn_grad, pieces, second_sums = second_back(
        fed[0][1], back_parts, after_attn, attn_branch, cotangent, merge_whole, gate_one, scale_two, cuts
    )
    attended_grads = []
    for index in range(len(spans)):
        mine = pieces[index :: len(spans)]
        if index:
            attended_grads, mine = together(attended_grads, mine)
        attended_grads.append(
            jnp.concatenate([shift_tp(mine[k], -k, tp_count) for k in ring], axis=0)
        )
    triple_grads = [
        attend_backward(triple, 0, *mixes[0], attended_grads[0], spans[0][1])
    ]
    triple_grads, branch_parts, attended_grads = together(triple_grads, branch_parts, attended_grads)
    pair = token_sum([([attn_grad], [attended_own]), ([normed_one], triple_grads)], fsdp_count)
    state = scatter_core(pair, fsdp_count)
    block_out, last_sums = last_forward(fed[0][0], branch_parts, after_attn, cotangent, gate_two)
    attended_grads, state, block_out = together(attended_grads, state, block_out)
    state = scatter_x(state, fsdp_count)
    for index in range(1, len(spans)):
        start, end = spans[index]
        triple_grads.append(
            attend_backward(triple, 3 * start, *mixes[index], attended_grads[index], end - start)
        )
    parts = [product_back(triple_grads, heads_whole, LOW, own, k) for k in others]
    one_parts = [shift_tp(values, k, tp_count) for k, values in zip(others, parts)]
    triple_grads, parts = together(triple_grads, parts)
    last = None
    if len(spans) > 1:
        last = token_sum([([normed_one], triple_grads[1:])], fsdp_count)
    triple_grads, last, state = together(triple_grads, last, state)
    state = scatter_z(state, fsdp_count)
    if last:
        last = scatter_core(last, fsdp_count)
    normed_one_grad = product_back(triple_grads, heads_whole, FULL, own, 0)
    one_parts, normed_one_grad, last = together(one_parts, normed_one_grad, last)
    if last:
        last = scatter_x(last, fsdp_count)
    latents_grad, first_sums = first_back(normed_one_grad, one_parts, latents, after_grad, scale_one)
    first_sums, last, feed_sum = together(first_sums, last, feed_sum)
    if last:
        last = scatter_z(last, fsdp_count)
    up_new = adam_step(up_weight, up_first, up_second, feed_sum[:, :units].astype(FULL), 0.02)
    down_new = adam_step(down_weight, down_first, down_second, feed_sum[:, units:].T.astype(FULL), 0.01)
    modulation_all = modulation_shares(
        jnp.concatenate([first_sums[:2], second_sums[:3], last_sums[:1]], axis=0),
        tp_count,
        fsdp_count,
        part,
    )
    modulation_all, state, last = together(modulation_all, state, last)
    first_sum = scatter_end(state)
    merge_sum_all, heads_sums = first_sum[:, : tp_count * width], [first_sum[:, tp_count * width :]]
    if last:
        heads_sums.append(scatter_end(last))
    heads_sums = [total.reshape(shard_rows, 3, -1) for total in heads_sums]
    condition_sum = lax.dot_general(
        activated_rows.astype(FULL),
        modulation_all,
        TN,
        precision=lax.Precision.HIGHEST,
        preferred_element_type=FULL,
    ).reshape(shard_rows, 6, part)
    merge_sum = merge_sum_all[:, :width]
    for k in others:
        merge_sum = merge_sum + shift_tp(
            merge_sum_all[:, k * width : (k + 1) * width], -k, tp_count
        )
    heads_sum = jnp.moveaxis(jnp.concatenate(heads_sums, axis=2), 1, 0)
    cond_new = adam_step(condition_weight, condition_first, condition_second, condition_sum, 0.02)
    heads_new = adam_step(heads_weight, heads_first, heads_second, heads_sum, 0.02)
    merge_new = adam_step(merge_weight, merge_first, merge_second, merge_sum.T, 0.15)
    return (
        block_out.reshape(own, 1, depth),
        latents_grad.reshape(own, 1, depth),
        *cond_new,
        *heads_new,
        *merge_new,
        *up_new,
        *down_new,
    )


def solution(mesh):
    stream = P("tp", "fsdp", None)
    cond = P("fsdp", None, "tp")
    heads = P(None, "fsdp", "tp")
    wide = P("tp", "fsdp")
    tall = P("fsdp", "tp")
    in_specs = (stream, P("fsdp", None), stream) + (cond,) * 3 + (heads,) * 3 + (wide,) * 3 + (tall,) * 3 + (wide,) * 3
    out_specs = (stream, stream) + (cond,) * 3 + (heads,) * 3 + (wide,) * 3 + (tall,) * 3 + (wide,) * 3
    return jax.shard_map(
        functools.partial(local, mesh.shape["fsdp"], mesh.shape["tp"]),
        mesh=mesh,
        in_specs=in_specs,
        out_specs=out_specs,
        check_vma=False,
    )
```
